32 devices in a mesh: expert: 16 (over z, y, x), tensor: 2 (over core).
Axes of the slice: x: 2, y: 2, z: 4, core: 2. Of those that a mesh axis runs over, the one named last changes fastest.
Arguments:
- tokens: bfloat16 [4096, 2048], P('expert', 'tensor'), may hold values from -6 to 6
- upstream: bfloat16 [4096, 2048], P('expert', 'tensor'), may hold values from -6 to 6
- expert_ids: int32 [4096, 1], P('expert'), may hold values from 0 to 15; in each aligned block of 256 rows (0 to 255, 256 to 511, ...) at most 32 rows name the same one
- w_gate: bfloat16 [16, 1408, 2048], P('expert', 'tensor'), may hold values from -0.125 to 0.125
- w_up: bfloat16 [16, 1408, 2048], P('expert', 'tensor'), may hold values from -0.125 to 0.125
- w_down: bfloat16 [16, 1408, 2048], P('expert', 'tensor'), may hold values from -0.15625 to 0.15625
Outputs:
- grad_tokens: bfloat16 [4096, 2048], P('expert', 'tensor')
- grad_gate: bfloat16 [16, 1408, 2048], P('expert', 'tensor')
- grad_up: bfloat16 [16, 1408, 2048], P('expert', 'tensor')
- grad_down: bfloat16 [16, 1408, 2048], P('expert', 'tensor')
The draws below stay inside these ranges and needn't reach their ends.
Inputs may be any that keep to these rules, and one draw needn't show every extreme that they name: `expert_ids`: among the 256 tokens of one index of expert, at most 32 name the same expert, and in some such block one expert is named exactly 32 times; every expert is named somewhere.
All inputs are finite; a program needn't handle non-finite values.
Results may differ from the reference program's by a relative error of at most 0.014.
Values may be sent and summed in bfloat16 or wider, within the bound.
No kernel may reach another device: no remote copies, remote signals or barrier semaphores. Data moves between devices by JAX's collectives and lax.ppermute only.
A program may use at most 64 MiB of HBM per device.

```python
import math
import jax
import jax.numpy as jnp
import numpy as np
from jax import lax

D = 2048
FF = 1408
TOK_DEV = 256
EXPERTS = 16
CAP = 32
TOKENS = 4096


def level_of(rng, shape, shards, smallest, top_value):
    factor_of, own = 1.0, jax.random.fold_in(rng, 6)
    for dim, shards_of in shards:
        draws = jnp.exp(jax.random.uniform(jax.random.fold_in(own, dim), (shards_of,), jnp.float32, smallest / len(shards), top_value / len(shards)))
        factor_of = factor_of * jnp.repeat(draws, shape[dim] // shards_of).reshape([-1 if axis == dim else 1 for axis in range(len(shape))])
    return factor_of


def deal_out(own_key, own, number, rows, count, top, bound, slope):
    sequence = jax.random.permutation(own_key, count)
    crowded, ordinary = portions_of(count, rows * top, bound, slope, True), portions_of(count, rows * top, bound, slope, False)
    places = jnp.arange(count)

    def named(sizes, offset_by):
        used = int((sizes > 0).sum())
        fixed = max(1, used // 4)
        shifted = fixed + (places - fixed + offset_by * (used - fixed)) % max(1, count - fixed)
        return jnp.zeros((count,), jnp.int32).at[sequence[jnp.where(places < fixed, places, shifted)]].set(jnp.asarray(sizes, jnp.int32))

    sizes = jnp.where(number % 4 == 0, named(crowded, number // 4), named(ordinary, number - number // 4 - 1))
    mixed = jax.random.permutation(jax.random.fold_in(own, 3), count)
    giver, receiver = mixed[0:count // 2 * 2:2], mixed[1:count // 2 * 2:2]
    slack = jnp.minimum(sizes[giver] - 1, bound - sizes[receiver]) // 2
    slack = jnp.where((giver == sequence[0]) | (receiver == sequence[0]) | (sizes[receiver] == 0), 0, jnp.maximum(slack, 0))
    shifted = jax.random.randint(jax.random.fold_in(own, 4), (count // 2,), 0, 1 << 20) % (slack + 1)
    sizes = sizes.at[giver].add(-shifted).at[receiver].add(shifted)
    labels = jnp.searchsorted(jnp.cumsum(sizes), jnp.arange(rows * top), side="right").astype(jnp.int32)
    listing = labels.reshape(top, rows).T
    listing = listing[jax.random.permutation(jax.random.fold_in(own, 1), rows)]
    offset_by = jax.random.randint(jax.random.fold_in(own, 2), (rows, 1), 0, top)
    return jnp.take_along_axis(listing, (jnp.arange(top)[None, :] + offset_by) % top, axis=1)


def portions_of(amount, total, reach, slope, full):
    portions = [(1 << 20) // math.isqrt(standing ** slope) + 1 for standing in range(1, amount + 1)]
    largest = reach if full else min(reach, max(-(-total // amount), total * portions[0] // sum(portions)))
    least = 1 if total - largest >= amount - 1 else 0
    holding, surplus = [largest] + [least] * (amount - 1), total - largest - least * (amount - 1)
    while surplus > 0:
        movable = [i for i in range(1, amount) if holding[i] < largest] or [i for i in range(1, amount) if holding[i] < reach]
        whole, budget = sum([portions[i] for i in movable]), surplus
        for i in movable:
            extra = min(reach - holding[i], max(1, budget * portions[i] // whole), surplus)
            holding[i] = holding[i] + extra
            surplus = surplus - extra
    return np.array(holding)


def scatter_about(stream_key, shape, width, most, split=(), kind=jnp.bfloat16):
    entries = width * jax.random.normal(stream_key, shape, jnp.float32)
    if split:
        entries = entries * level_of(stream_key, shape, split, -0.22, 0.18)
    return jnp.clip(entries, -most, most).astype(kind)


def setup_inputs(seed: int = 0) -> dict:
    keys = jax.random.split(jax.random.key(seed), 7)
    tokens = scatter_about(keys[0], (TOKENS, D), 1.0, 6.0, ((0, 16), (1, 2)))
    upstream = scatter_about(keys[1], (TOKENS, D), 1.0, 6.0, ((0, 16), (1, 2)))
    expert_ids_keys = jax.random.split(jax.random.fold_in(keys[2], 1), TOKENS // TOK_DEV)
    expert_ids_turns = jax.random.permutation(jax.random.fold_in(keys[2], 3), TOKENS // TOK_DEV)
    expert_ids = jax.vmap(lambda own, number: deal_out(jax.random.fold_in(keys[2], 2), own, number, TOK_DEV, EXPERTS, 1, CAP, 2))(expert_ids_keys, expert_ids_turns).reshape((TOKENS, 1))
    w_gate = scatter_about(keys[3], (EXPERTS, FF, D), D ** -0.5, 0.125, ((0, 16), (1, 2)))
    w_up = scatter_about(keys[4], (EXPERTS, FF, D), D ** -0.5, 0.125, ((0, 16), (1, 2)))
    w_down = scatter_about(keys[5], (EXPERTS, FF, D), FF ** -0.5, 0.15625, ((0, 16), (1, 2)))
    return dict(tokens=tokens, upstream=upstream, expert_ids=expert_ids, w_gate=w_gate, w_up=w_up, w_down=w_down)


def reference(tokens, upstream, expert_ids, w_gate, w_up, w_down):
    route = expert_ids[:, 0]
    row_count = EXPERTS * CAP
    order_all = jnp.arange(TOKENS, dtype=jnp.int32)

    def one_expert(carry, items):
        expert_now, gate_rows, up_rows, down_rows = items
        sort_key = jnp.where(route == expert_now, 0, 1).astype(jnp.int32) * TOKENS + order_all
        picked = jnp.argsort(sort_key)[:row_count].astype(jnp.int32)
        valid = (route[picked] == expert_now)[:, None]
        x_rows = jnp.where(valid, tokens[picked], jnp.zeros((), jnp.bfloat16)).astype(jnp.bfloat16)
        dy_rows = jnp.where(valid, upstream[picked], jnp.zeros((), jnp.bfloat16)).astype(jnp.bfloat16)
        gate_pre = jnp.dot(x_rows, gate_rows.T, preferred_element_type=jnp.float32)
        up_pre = jnp.dot(x_rows, up_rows.T, preferred_element_type=jnp.float32)
        sig_gate = jax.nn.sigmoid(gate_pre)
        silu_gate = gate_pre * sig_gate
        hidden = (silu_gate * up_pre).astype(jnp.bfloat16)
        d_hidden = jnp.dot(dy_rows, down_rows.T, preferred_element_type=jnp.float32)
        d_up = (d_hidden * silu_gate).astype(jnp.bfloat16)
        d_gate = (d_hidden * up_pre * sig_gate * (1.0 + gate_pre * (1.0 - sig_gate))).astype(jnp.bfloat16)
        grad_down = jnp.dot(hidden.T, dy_rows, preferred_element_type=jnp.float32).astype(jnp.bfloat16)
        grad_gate = jnp.dot(d_gate.T, x_rows, preferred_element_type=jnp.float32).astype(jnp.bfloat16)
        grad_up = jnp.dot(d_up.T, x_rows, preferred_element_type=jnp.float32).astype(jnp.bfloat16)
        d_rows = jnp.dot(d_gate, gate_rows, preferred_element_type=jnp.float32) + jnp.dot(d_up, up_rows, preferred_element_type=jnp.float32)
        d_rows = jnp.where(valid, d_rows.astype(jnp.bfloat16), jnp.zeros((), jnp.bfloat16)).astype(jnp.bfloat16)
        carry = carry.at[picked].add(d_rows)
        return carry, (grad_gate, grad_up, grad_down)

    start = jnp.zeros((TOKENS, D), jnp.bfloat16)
    numbers = jnp.arange(EXPERTS, dtype=jnp.int32)
    grad_tokens, grads = lax.scan(one_expert, start, (numbers, w_gate, w_up, w_down))
    return (grad_tokens, grads[0], grads[1], grads[2])
```

```python
import jax
import jax.numpy as jnp
from jax import lax
from jax.sharding import PartitionSpec as P

F32 = jnp.float32
BF16 = jnp.bfloat16


def gather_features(own):
    if lax.axis_size("tensor") != 2:
        return lax.all_gather(own, "tensor", axis=1, tiled=True)
    other = lax.ppermute(own, "tensor", [(0, 1), (1, 0)])
    first = lax.axis_index("tensor") == 0
    return jnp.concatenate(
        [jnp.where(first, own, other), jnp.where(first, other, own)], axis=1
    )


def scatter_sum(partial):
    parts = lax.axis_size("tensor")
    width = partial.shape[1] // parts
    if parts != 2:
        return lax.psum_scatter(
            partial.astype(BF16), "tensor", scatter_dimension=1, tiled=True
        )
    first = lax.axis_index("tensor") == 0
    lower, upper = partial[:, :width], partial[:, width:]
    sent = jnp.where(first, upper, lower).astype(BF16)
    kept = jnp.where(first, lower, upper)
    got = lax.ppermute(sent, "tensor", [(0, 1), (1, 0)])
    return (kept + got.astype(F32)).astype(BF16)


def on_device(tokens, upstream, expert_ids, w_gate, w_up, w_down):
    experts = lax.axis_size("expert")
    tok_rows, feat_width = tokens.shape
    capacity = max(2, 2 * tok_rows // experts)
    slot_count = experts * capacity
    route = expert_ids[:, 0]
    onehot = (route[:, None] == jnp.arange(experts, dtype=jnp.int32)[None, :]).astype(jnp.int32)
    before = jnp.cumsum(onehot, axis=0) - onehot
    within = jnp.sum(before * onehot, axis=1)
    target = route * capacity + within
    placing = (target[None, :] == jnp.arange(slot_count, dtype=jnp.int32)[:, None]).astype(BF16)
    gate_rows, up_rows, down_rows = w_gate[0], w_up[0], w_down[0]

    def spread(values):
        placed = jnp.dot(placing, values, preferred_element_type=F32).astype(BF16)
        placed = placed.reshape(experts, capacity, feat_width)
        got = lax.all_to_all(placed, "expert", split_axis=0, concat_axis=0, tiled=True)
        return got.reshape(slot_count, feat_width)

    def rows_by_weights(rows, weights):
        return lax.dot_general(
            rows, weights, (((1,), (1,)), ((), ())), preferred_element_type=F32
        )

    def weight_grad(left, right):
        return lax.dot_general(
            left, right, (((0,), (0,)), ((), ())), preferred_element_type=F32
        ).astype(BF16)

    got_x, got_dy = spread(tokens), spread(upstream)
    x_all = gather_features(got_x)
    gate_pre = rows_by_weights(x_all, gate_rows)
    up_pre = rows_by_weights(x_all, up_rows)
    sig_gate = jax.nn.sigmoid(gate_pre)
    silu_gate = gate_pre * sig_gate
    hidden = (silu_gate * up_pre).astype(BF16)
    dy_all = gather_features(got_dy)
    d_hidden = rows_by_weights(dy_all, down_rows)
    d_up = (d_hidden * silu_gate).astype(BF16)
    d_gate = (d_hidden * up_pre * sig_gate * (1.0 + gate_pre * (1.0 - sig_gate))).astype(BF16)
    partial_rows = jnp.dot(d_gate, gate_rows, preferred_element_type=F32) + jnp.dot(
        d_up, up_rows, preferred_element_type=F32
    )
    totals = scatter_sum(partial_rows)
    returned = lax.all_to_all(
        totals.reshape(experts, capacity, feat_width),
        "expert",
        split_axis=0,
        concat_axis=0,
        tiled=True,
    ).reshape(slot_count, feat_width)
    grad_gate = weight_grad(d_gate, x_all)
    grad_up = weight_grad(d_up, x_all)
    grad_down = weight_grad(hidden, dy_all)
    grad_tokens = weight_grad(placing, returned)
    return (grad_tokens, grad_gate[None], grad_up[None], grad_down[None])


def solution(mesh):
    rows = P("expert", "tensor")
    weights = P("expert", "tensor", None)
    return jax.shard_map(
        on_device,
        mesh=mesh,
        in_specs=(rows, rows, P("expert", None), weights, weights, weights),
        out_specs=(rows, weights, weights, weights),
        check_vma=False,
    )
```

```python
import functools

import jax
import jax.numpy as jnp
from jax import lax
from jax.experimental import pallas as pl
from jax.experimental.pallas import tpu as pltpu
from jax.sharding import PartitionSpec as P

F32 = jnp.float32
BF16 = jnp.bfloat16
VMEM = pltpu.VMEM
LIMIT = 48 * 2**20


def whole(count):
    return [pl.BlockSpec(memory_space=VMEM)] * count


def place_kernel(capacity, col_ref, row_ref, x_ref, dy_ref, *slabs):
    me = lax.axis_index("expert")
    rows = x_ref.shape[0]
    col, row = col_ref[...], row_ref[...]
    earlier = lax.broadcasted_iota(jnp.int32, (rows, rows), 0) < lax.broadcasted_iota(
        jnp.int32, (rows, rows), 1
    )
    same = jnp.where((col == row) & earlier, 1.0, 0.0)
    within = jnp.sum(same, axis=0, keepdims=True).astype(jnp.int32)
    target = (row ^ me) * capacity + within
    slots = len(slabs) * capacity
    slot = lax.broadcasted_iota(jnp.int32, (slots, rows), 0)
    placing = jnp.where(slot == target, 1.0, 0.0).astype(BF16)
    x = jnp.dot(placing, x_ref[...], preferred_element_type=F32).astype(BF16)
    dy = jnp.dot(placing, dy_ref[...], preferred_element_type=F32).astype(BF16)
    for k, slab in enumerate(slabs):
        slab[:capacity, :] = x[k * capacity : (k + 1) * capacity]
        slab[capacity:, :] = dy[k * capacity : (k + 1) * capacity]


def combine_kernel(capacity, col_ref, row_ref, *refs):
    *slabs, out_ref = refs
    me = lax.axis_index("expert")
    rows = out_ref.shape[0]
    col, row = col_ref[...], row_ref[...]
    earlier = lax.broadcasted_iota(jnp.int32, (rows, rows), 1) < lax.broadcasted_iota(
        jnp.int32, (rows, rows), 0
    )
    same = jnp.where((col == row) & earlier, 1.0, 0.0)
    within = jnp.sum(same, axis=1, keepdims=True).astype(jnp.int32)
    target = (col ^ me) * capacity + within
    slots = len(slabs) * capacity
    slot = lax.broadcasted_iota(jnp.int32, (rows, slots), 1)
    placing = jnp.where(slot == target, 1.0, 0.0).astype(BF16)
    returned = jnp.concatenate([slab[...] for slab in slabs], axis=0)
    out_ref[...] = jnp.dot(placing, returned, preferred_element_type=F32).astype(BF16)


def gather_features(own):
    if lax.axis_size("tensor") != 2:
        return lax.all_gather(own, "tensor", axis=1, tiled=True)
    other = lax.ppermute(own, "tensor", [(0, 1), (1, 0)])
    first = lax.axis_index("tensor") == 0
    return jnp.concatenate(
        [jnp.where(first, own, other), jnp.where(first, other, own)], axis=1
    )


def scatter_sum(partial):
    parts = lax.axis_size("tensor")
    width = partial.shape[1] // parts
    if parts != 2:
        return lax.psum_scatter(
            partial.astype(BF16), "tensor", scatter_dimension=1, tiled=True
        )
    first = lax.axis_index("tensor") == 0
    lower, upper = partial[:, :width], partial[:, width:]
    sent = jnp.where(first, upper, lower).astype(BF16)
    kept = jnp.where(first, lower, upper)
    got = lax.ppermute(sent, "tensor", [(0, 1), (1, 0)])
    return (kept + got.astype(F32)).astype(BF16)


def on_device(tokens, upstream, expert_ids, w_gate, w_up, w_down):
    experts = lax.axis_size("expert")
    tok_rows, feat_width = tokens.shape
    capacity = max(2, 2 * tok_rows // experts)
    gate_rows, up_rows, down_rows = w_gate[0], w_up[0], w_down[0]
    ids_row = expert_ids.reshape(1, tok_rows)

    def swap(slab, k):
        if k == 0:
            return slab
        return lax.ppermute(slab, "expert", [(e, e ^ k) for e in range(experts)])

    def swap_all(slabs):
        got = {k: swap(slabs[k], k) for k in reversed(range(experts))}
        return [got[k] for k in range(experts)]

    def rows_by_weights(rows, weights):
        return lax.dot_general(
            rows, weights, (((1,), (1,)), ((), ())), preferred_element_type=F32
        )

    def weight_grad(left, right):
        return lax.dot_general(
            left, right, (((0,), (0,)), ((), ())), preferred_element_type=F32
        ).astype(BF16)

    slabs = pl.pallas_call(
        functools.partial(place_kernel, capacity),
        out_shape=[jax.ShapeDtypeStruct((2 * capacity, feat_width), BF16)] * experts,
        in_specs=whole(4),
        out_specs=whole(experts),
        compiler_params=pltpu.CompilerParams(vmem_limit_bytes=LIMIT),
        name="place",
    )(expert_ids, ids_row, tokens, upstream)
    arrived = swap_all(slabs)
    got_x = jnp.concatenate([slab[:capacity] for slab in arrived], axis=0)
    got_dy = jnp.concatenate([slab[capacity:] for slab in arrived], axis=0)
    x_all = gather_features(got_x)
    gate_pre = rows_by_weights(x_all, gate_rows)
    up_pre = rows_by_weights(x_all, up_rows)
    sig_gate = jax.nn.sigmoid(gate_pre)
    silu_gate = gate_pre * sig_gate
    hidden = (silu_gate * up_pre).astype(BF16)
    dy_all = gather_features(got_dy)
    d_hidden = rows_by_weights(dy_all, down_rows)
    d_up = (d_hidden * silu_gate).astype(BF16)
    d_gate = (d_hidden * up_pre * sig_gate * (1.0 + gate_pre * (1.0 - sig_gate))).astype(BF16)
    partial_rows = jnp.dot(d_gate, gate_rows, preferred_element_type=F32) + jnp.dot(
        d_up, up_rows, preferred_element_type=F32
    )
    totals = scatter_sum(partial_rows)
    returned = swap_all([totals[k * capacity : (k + 1) * capacity] for k in range(experts)])
    grad_gate = weight_grad(d_gate, x_all)
    grad_up = weight_grad(d_up, x_all)
    grad_down = weight_grad(hidden, dy_all)
    grad_tokens = pl.pallas_call(
        functools.partial(combine_kernel, capacity),
        out_shape=jax.ShapeDtypeStruct((tok_rows, feat_width), BF16),
        in_specs=whole(2 + experts),
        out_specs=pl.BlockSpec(memory_space=VMEM),
        compiler_params=pltpu.CompilerParams(vmem_limit_bytes=LIMIT),
        name="combine",
    )(expert_ids, ids_row, *returned)
    return (grad_tokens, grad_gate[None], grad_up[None], grad_down[None])


def solution(mesh):
    rows = P("expert", "tensor")
    weights = P("expert", "tensor", None)
    return jax.shard_map(
        on_device,
        mesh=mesh,
        in_specs=(rows, rows, P("expert", None), weights, weights, weights),
        out_specs=(rows, weights, weights, weights),
        check_vma=False,
    )
```

```python
import functools

import jax
import jax.numpy as jnp
from jax import lax
from jax.experimental import pallas as pl
from jax.experimental.pallas import tpu as pltpu
from jax.sharding import PartitionSpec as P

F32 = jnp.float32
BF16 = jnp.bfloat16
LIMIT = 24 * 2**20
PIECES = 4


def rank_among_same(row, axis):
    rows = row.shape[1]
    down = lax.broadcasted_iota(jnp.int32, (rows, rows), 0)
    right = lax.broadcasted_iota(jnp.int32, (rows, rows), 1)
    col = jnp.sum(jnp.where(down == right, row, 0), axis=1, keepdims=True)
    earlier = down > right if axis else down < right
    same = jnp.where((col == row) & earlier, 1, 0)
    return (col if axis else row), jnp.sum(same, axis=axis, keepdims=True)


def place_kernel(capacity, row_ref, x_hbm, dy_hbm, out_ref, x_ref, dy_ref, sems):
    copies = [
        pltpu.make_async_copy(x_hbm, x_ref, sems.at[0]),
        pltpu.make_async_copy(dy_hbm, dy_ref, sems.at[1]),
    ]
    for copy in copies:
        copy.start()
    width = x_ref.shape[1]
    route, within = rank_among_same(row_ref[...], 0)
    slot = lax.broadcasted_iota(jnp.int32, (out_ref.shape[0], x_ref.shape[0]), 0)
    placing = jnp.where(slot == route * capacity + within, 1.0, 0.0).astype(BF16)
    for i, ref in enumerate((x_ref, dy_ref)):
        copies[i].wait()
        out_ref[:, i * width : (i + 1) * width] = jnp.dot(
            placing, ref[...], preferred_element_type=F32
        ).astype(BF16)


def combine_kernel(capacity, row_ref, back_hbm, out_ref, back_ref, sems):
    slots = back_ref.shape[0]
    step = slots // PIECES
    copies = [
        pltpu.make_async_copy(
            back_hbm.at[i * step : (i + 1) * step],
            back_ref.at[i * step : (i + 1) * step],
            sems.at[i],
        )
        for i in range(PIECES)
    ]
    for copy in copies:
        copy.start()
    route, within = rank_among_same(row_ref[...], 1)
    slot = lax.broadcasted_iota(jnp.int32, (out_ref.shape[0], slots), 1)
    placing = jnp.where(slot == route * capacity + within, 1.0, 0.0).astype(BF16)
    total = jnp.zeros(out_ref.shape, F32)
    for i, copy in enumerate(copies):
        copy.wait()
        total += jnp.dot(
            placing[:, i * step : (i + 1) * step],
            back_ref[i * step : (i + 1) * step],
            preferred_element_type=F32,
        )
    out_ref[...] = total.astype(BF16)


def rows_by_weights(rows, weights):
    return lax.dot_general(rows, weights, (((1,), (1,)), ((), ())), preferred_element_type=F32)


def weight_grad(left, right):
    return lax.dot_general(
        left, right, (((0,), (0,)), ((), ())), preferred_element_type=F32
    ).astype(BF16)


def on_device(tokens, upstream, expert_ids, w_gate, w_up, w_down):
    experts, parts = lax.axis_size("expert"), lax.axis_size("tensor")
    tok_rows, width = tokens.shape
    capacity = max(2, 2 * tok_rows // experts)
    slot_count = experts * capacity
    gate_rows, up_rows, down_rows = w_gate[0], w_up[0], w_down[0]
    ids_row = expert_ids.reshape(1, tok_rows)
    vmem = pl.BlockSpec(memory_space=pltpu.VMEM)
    hbm = pl.BlockSpec(memory_space=pl.ANY)
    params = pltpu.CompilerParams(vmem_limit_bytes=LIMIT)

    def to_experts(rows):
        return lax.all_to_all(
            rows.reshape(experts, capacity, rows.shape[1]),
            "expert",
            split_axis=0,
            concat_axis=0,
            tiled=True,
        ).reshape(slot_count, rows.shape[1])

    placed = pl.pallas_call(
        functools.partial(place_kernel, capacity),
        out_shape=jax.ShapeDtypeStruct((slot_count, 2 * width), BF16),
        in_specs=[vmem, hbm, hbm],
        out_specs=vmem,
        scratch_shapes=[
            pltpu.VMEM((tok_rows, width), BF16),
            pltpu.VMEM((tok_rows, width), BF16),
            pltpu.SemaphoreType.DMA((2,)),
        ],
        compiler_params=params,
        name="place",
    )(ids_row, tokens, upstream)
    own = to_experts(placed)
    own_x, own_dy = own[:, :width], own[:, width:]

    if parts == 2:
        other = lax.ppermute(own, "tensor", [(0, 1), (1, 0)])
        other_x, other_dy = other[:, :width], other[:, width:]
        mine = lax.axis_index("tensor")

        def halves(weights):
            return [
                lax.dynamic_slice_in_dim(weights, which * width, width, 1)
                for which in (mine, 1 - mine)
            ]

        gate_own, gate_other = halves(gate_rows)
        up_own, up_other = halves(up_rows)
        down_own, down_other = halves(down_rows)
        gate_pre = rows_by_weights(own_x, gate_own) + rows_by_weights(other_x, gate_other)
        up_pre = rows_by_weights(own_x, up_own) + rows_by_weights(other_x, up_other)
        d_hidden = rows_by_weights(own_dy, down_own) + rows_by_weights(other_dy, down_other)

        def in_order(left, right):
            first = mine == 0
            return jnp.concatenate(
                [jnp.where(first, left, right), jnp.where(first, right, left)], axis=1
            )

        x_all, dy_all = in_order(own_x, other_x), in_order(own_dy, other_dy)
    else:
        x_all = lax.all_gather(own_x, "tensor", axis=1, tiled=True)
        dy_all = lax.all_gather(own_dy, "tensor", axis=1, tiled=True)
        gate_pre = rows_by_weights(x_all, gate_rows)
        up_pre = rows_by_weights(x_all, up_rows)
        d_hidden = rows_by_weights(dy_all, down_rows)

    sig_gate = jax.nn.sigmoid(gate_pre)
    silu_gate = gate_pre * sig_gate
    hidden = (silu_gate * up_pre).astype(BF16)
    d_up = (d_hidden * silu_gate).astype(BF16)
    d_gate = (d_hidden * up_pre * sig_gate * (1.0 + gate_pre * (1.0 - sig_gate))).astype(BF16)

    def input_rows(gate_part, up_part):
        return jnp.dot(d_gate, gate_part, preferred_element_type=F32) + jnp.dot(
            d_up, up_part, preferred_element_type=F32
        )

    if parts == 2:
        sent = input_rows(gate_other, up_other).astype(BF16)
        got = lax.ppermute(sent, "tensor", [(0, 1), (1, 0)])
        totals = (input_rows(gate_own, up_own) + got.astype(F32)).astype(BF16)
    else:
        totals = lax.psum_scatter(
            input_rows(gate_rows, up_rows).astype(BF16),
            "tensor",
            scatter_dimension=1,
            tiled=True,
        )
    returned = to_experts(totals)
    grad_gate = weight_grad(d_gate, x_all)
    grad_up = weight_grad(d_up, x_all)
    grad_down = weight_grad(hidden, dy_all)
    grad_tokens = pl.pallas_call(
        functools.partial(combine_kernel, capacity),
        out_shape=jax.ShapeDtypeStruct((tok_rows, width), BF16),
        in_specs=[vmem, hbm],
        out_specs=vmem,
        scratch_shapes=[
            pltpu.VMEM((slot_count, width), BF16),
            pltpu.SemaphoreType.DMA((PIECES,)),
        ],
        compiler_params=params,
        name="combine",
    )(ids_row, returned)
    return (grad_tokens, grad_gate[None], grad_up[None], grad_down[None])


def solution(mesh):
    rows = P("expert", "tensor")
    weights = P("expert", "tensor", None)
    return jax.shard_map(
        on_device,
        mesh=mesh,
        in_specs=(rows, rows, P("expert", None), weights, weights, weights),
        out_specs=(rows, weights, weights, weights),
        check_vma=False,
    )
```

```python
import functools

import jax
import jax.numpy as jnp
from jax import lax
from jax.experimental import pallas as pl
from jax.experimental.pallas import tpu as pltpu
from jax.sharding import PartitionSpec as P

F32 = jnp.float32
BF16 = jnp.bfloat16
SMALL = 20 * 2**20
LARGE = 56 * 2**20
PIECES = 4
IN_VMEM = pl.BlockSpec(memory_space=pltpu.VMEM)
ANYWHERE = pl.BlockSpec(memory_space=pl.ANY)


def rank_among_same(row, axis):
    rows = row.shape[1]
    down = lax.broadcasted_iota(jnp.int32, (rows, rows), 0)
    right = lax.broadcasted_iota(jnp.int32, (rows, rows), 1)
    col = jnp.sum(jnp.where(down == right, row, 0), axis=1, keepdims=True)
    earlier = down > right if axis else down < right
    same = jnp.where((col == row) & earlier, 1, 0)
    return (col if axis else row), jnp.sum(same, axis=axis, keepdims=True)


def place_kernel(capacity, row_ref, x_hbm, dy_hbm, *refs):
    *slabs, x_ref, dy_ref, sems = refs
    copies = [
        pltpu.make_async_copy(x_hbm, x_ref, sems.at[0]),
        pltpu.make_async_copy(dy_hbm, dy_ref, sems.at[1]),
    ]
    for copy in copies:
        copy.start()
    me = lax.axis_index("expert")
    route, within = rank_among_same(row_ref[...], 0)
    slots = len(slabs) * capacity
    slot = lax.broadcasted_iota(jnp.int32, (slots, x_ref.shape[0]), 0)
    placing = jnp.where(slot == (route ^ me) * capacity + within, 1.0, 0.0).astype(BF16)
    for i, ref in enumerate((x_ref, dy_ref)):
        copies[i].wait()
        placed = jnp.dot(placing, ref[...], preferred_element_type=F32).astype(BF16)
        for k, slab in enumerate(slabs):
            slab[i * capacity : (i + 1) * capacity, :] = placed[k * capacity : (k + 1) * capacity]


def collect_kernel(capacity, *refs):
    *slabs, out_ref = refs
    half = len(slabs) * capacity
    for i, slab in enumerate(slabs):
        out_ref[i * capacity : (i + 1) * capacity, :] = slab[:capacity, :]
        out_ref[half + i * capacity : half + (i + 1) * capacity, :] = slab[capacity:, :]


def side(which, width):
    return pl.ds(pl.multiple_of(which * width, width), width)


def input_rows(d_gate_ref, d_up_ref, gate_ref, up_ref, columns):
    over_hidden = (((0,), (0,)), ((), ()))
    return lax.dot_general(
        d_gate_ref[...], gate_ref[:, columns], over_hidden, preferred_element_type=F32
    ) + lax.dot_general(
        d_up_ref[...], up_ref[:, columns], over_hidden, preferred_element_type=F32
    )


def front_kernel(tile, own_ref, other_ref, gate_ref, up_ref, down_ref, *refs):
    x_ref, dy_ref, hidden_ref, d_gate_ref, d_up_ref, sent_ref = refs[-6:]
    rows, width = x_ref.shape[0], own_ref.shape[1]
    mine = lax.axis_index("tensor")
    for half, whole_ref in enumerate((x_ref, dy_ref)):
        whole_ref[:, side(mine, width)] = own_ref[half * rows : (half + 1) * rows, :]
        whole_ref[:, side(1 - mine, width)] = other_ref[half * rows : (half + 1) * rows, :]
    over_features = (((1,), (1,)), ((), ()))

    @pl.loop(0, hidden_ref.shape[0] // tile)
    def _(step):
        units = pl.ds(pl.multiple_of(step * tile, tile), tile)

        def product(weight_ref, whole_ref):
            return lax.dot_general(
                weight_ref[units, :], whole_ref[...], over_features, preferred_element_type=F32
            )

        gate_pre = product(gate_ref, x_ref)
        up_pre = product(up_ref, x_ref)
        d_hidden = product(down_ref, dy_ref)
        sig = jax.nn.sigmoid(gate_pre)
        silu = gate_pre * sig
        hidden_ref[units, :] = (silu * up_pre).astype(BF16)
        d_up_ref[units, :] = (d_hidden * silu).astype(BF16)
        d_gate_ref[units, :] = (
            d_hidden * up_pre * sig * (1.0 + gate_pre * (1.0 - sig))
        ).astype(BF16)

    sent_ref[...] = input_rows(
        d_gate_ref, d_up_ref, gate_ref, up_ref, side(1 - mine, width)
    ).astype(BF16)


def kept_kernel(d_gate_ref, d_up_ref, gate_ref, up_ref, out_ref):
    columns = side(lax.axis_index("tensor"), out_ref.shape[1])
    out_ref[...] = input_rows(d_gate_ref, d_up_ref, gate_ref, up_ref, columns)


def total_kernel(capacity, groups, *refs):
    *parts, out_ref, done_ref = refs
    me = lax.axis_index("expert")
    done_ref[...] = jnp.zeros_like(done_ref)
    for kept_ref, got_ref, group in zip(parts[::2], parts[1::2], groups):
        for i, k in enumerate(group):
            here = slice(i * capacity, (i + 1) * capacity)
            there = pl.ds(pl.multiple_of((me ^ k) * capacity, capacity), capacity)
            out_ref[there, :] = (kept_ref[here, :] + got_ref[here, :].astype(F32)).astype(BF16)


def grads_kernel(groups, *refs):
    *ins, _, grad_gate_ref, grad_up_ref, grad_down_ref = refs
    by_group = [ins[i :: groups] for i in range(groups)]

    def total(left, right):
        return sum(
            jnp.dot(one[left][...], one[right][...], preferred_element_type=F32)
            for one in by_group
        ).astype(BF16)

    grad_gate_ref[...] = total(0, 3)
    grad_up_ref[...] = total(1, 3)
    grad_down_ref[...] = total(2, 4)


def combine_kernel(capacity, row_ref, back_hbm, out_ref, back_ref, sems):
    slots = back_ref.shape[0]
    step = slots // PIECES
    copies = [
        pltpu.make_async_copy(
            back_hbm.at[i * step : (i + 1) * step],
            back_ref.at[i * step : (i + 1) * step],
            sems.at[i],
        )
        for i in range(PIECES)
    ]
    for copy in copies:
        copy.start()
    route, within = rank_among_same(row_ref[...], 1)
    slot = lax.broadcasted_iota(jnp.int32, (out_ref.shape[0], slots), 1)
    placing = jnp.where(slot == route * capacity + within, 1.0, 0.0).astype(BF16)
    total = jnp.zeros(out_ref.shape, F32)
    for i, copy in enumerate(copies):
        copy.wait()
        total += jnp.dot(
            placing[:, i * step : (i + 1) * step],
            back_ref[i * step : (i + 1) * step],
            preferred_element_type=F32,
        )
    out_ref[...] = total.astype(BF16)


def params(limit):
    return pltpu.CompilerParams(vmem_limit_bytes=limit)


def cost(products, rows, hidden, features):
    return pl.CostEstimate(
        flops=2 * products * rows * hidden * features,
        bytes_accessed=2 * products * (hidden + rows) * features,
        transcendentals=0,
    )


def combine(capacity, ids_row, returned, tok_rows):
    slots, width = returned.shape
    return pl.pallas_call(
        functools.partial(combine_kernel, capacity),
        out_shape=jax.ShapeDtypeStruct((tok_rows, width), BF16),
        in_specs=[IN_VMEM, ANYWHERE],
        out_specs=IN_VMEM,
        scratch_shapes=[pltpu.VMEM((slots, width), BF16), pltpu.SemaphoreType.DMA((PIECES,))],
        compiler_params=params(LARGE),
        name="combine",
    )(ids_row, returned)


def to_experts(rows, experts):
    return lax.all_to_all(
        rows.reshape(experts, rows.shape[0] // experts, rows.shape[1]),
        "expert",
        split_axis=0,
        concat_axis=0,
        tiled=True,
    ).reshape(rows.shape)


def grouped(tokens, upstream, expert_ids, gate_rows, up_rows, down_rows):
    experts = lax.axis_size("expert")
    tok_rows, width = tokens.shape
    units, features = gate_rows.shape
    capacity = max(2, 2 * tok_rows // experts)
    ids_row = expert_ids.reshape(1, tok_rows)
    tile = units // 2 if units % 32 == 0 else units

    far = [k for k in reversed(range(1, experts)) if k >= experts // 2]
    near = [k for k in reversed(range(1, experts)) if k < experts // 2]
    early = experts // 4 - 1
    share = experts // 2 - 1 - early
    turns = [k for pair in zip(far[:early], near[:early]) for k in pair]
    first = [0] + turns + near[early:share]
    second = far[early:] + near[share:]
    late = second[-2:]
    rows = len(first) * capacity

    slabs = list(
        pl.pallas_call(
            functools.partial(place_kernel, capacity),
            out_shape=[jax.ShapeDtypeStruct((2 * capacity, width), BF16)] * experts,
            in_specs=[IN_VMEM, ANYWHERE, ANYWHERE],
            out_specs=[IN_VMEM] * experts,
            scratch_shapes=[
                pltpu.VMEM((tok_rows, width), BF16),
                pltpu.VMEM((tok_rows, width), BF16),
                pltpu.SemaphoreType.DMA((2,)),
            ],
            compiler_params=params(LARGE),
            name="place",
        )(ids_row, tokens, upstream)
    )

    def swap(k):
        return lax.ppermute(slabs[k], "expert", [(e, e ^ k) for e in range(experts)])

    def exchange(values):
        return lax.ppermute(values, "tensor", [(0, 1), (1, 0)])

    def collect(arrived):
        return pl.pallas_call(
            functools.partial(collect_kernel, capacity),
            out_shape=jax.ShapeDtypeStruct((2 * rows, width), BF16),
            in_specs=[IN_VMEM] * len(arrived),
            out_specs=IN_VMEM,
            compiler_params=params(SMALL),
            name="collect",
        )(*arrived)

    def front(own, passed):
        other = exchange(own)
        outs = pl.pallas_call(
            functools.partial(front_kernel, tile),
            out_shape=[jax.ShapeDtypeStruct(one.shape, one.dtype) for one in passed]
            + [jax.ShapeDtypeStruct((rows, features), BF16)] * 2
            + [jax.ShapeDtypeStruct((units, rows), BF16)] * 3
            + [jax.ShapeDtypeStruct((rows, width), BF16)],
            in_specs=[IN_VMEM] * (5 + len(passed)),
            out_specs=[IN_VMEM] * (len(passed) + 6),
            input_output_aliases={5 + i: i for i in range(len(passed))},
            compiler_params=params(SMALL),
            cost_estimate=cost(4, rows, units, features),
            name="front",
        )(own, other, gate_rows, up_rows, down_rows, *passed)
        return outs[: len(passed)], outs[len(passed) :]

    def kept_rows(d_gate, d_up):
        return pl.pallas_call(
            kept_kernel,
            out_shape=jax.ShapeDtypeStruct((rows, width), F32),
            in_specs=[IN_VMEM] * 4,
            out_specs=IN_VMEM,
            compiler_params=params(SMALL),
            cost_estimate=cost(1, rows, units, features),
            name="kept",
        )(d_gate, d_up, gate_rows, up_rows)

    got = {k: swap(k) for k in first + second if k and k not in late}
    got[0] = slabs[0]
    passed, front_a = front(collect([got[k] for k in first]), [slabs[k] for k in late])
    for k, slab in zip(late, passed):
        slabs[k] = slab
        got[k] = swap(k)
    _, front_b = front(collect([got[k] for k in second]), [])
    sums = []
    for _, _, _, d_gate, d_up, sent in (front_a, front_b):
        sums += [kept_rows(d_gate, d_up), exchange(sent)]
    totals, done = pl.pallas_call(
        functools.partial(total_kernel, capacity, (first, second)),
        out_shape=[
            jax.ShapeDtypeStruct((experts * capacity, width), BF16),
            jax.ShapeDtypeStruct((8, 128), F32),
        ],
        in_specs=[IN_VMEM] * 4,
        out_specs=[IN_VMEM] * 2,
        compiler_params=params(SMALL),
        name="total",
    )(*sums)
    returned = to_experts(totals, experts)

    lefts = [front_a[3], front_b[3], front_a[4], front_b[4], front_a[2], front_b[2]]
    rights = [front_a[0], front_b[0], front_a[1], front_b[1]]
    grads = pl.pallas_call(
        functools.partial(grads_kernel, 2),
        grid=(units // tile,),
        out_shape=[jax.ShapeDtypeStruct((units, features), BF16)] * 3,
        in_specs=[pl.BlockSpec((tile, rows), lambda i: (i, 0))] * 6
        + [pl.BlockSpec((rows, features), lambda i: (0, 0))] * 4
        + [pl.BlockSpec((8, 128), lambda i: (0, 0))],
        out_specs=[pl.BlockSpec((tile, features), lambda i: (i, 0))] * 3,
        compiler_params=params(32 * 2**20),
        cost_estimate=cost(6, rows, units, features),
        name="grads",
    )(*lefts, *rights, done)
    return combine(capacity, ids_row, returned, tok_rows), grads


def rows_by_weights(rows, weights):
    return lax.dot_general(rows, weights, (((1,), (1,)), ((), ())), preferred_element_type=F32)


def weight_grad(left, right):
    return lax.dot_general(
        left, right, (((0,), (0,)), ((), ())), preferred_element_type=F32
    ).astype(BF16)


def general(tokens, upstream, expert_ids, gate_rows, up_rows, down_rows):
    experts = lax.axis_size("expert")
    tok_rows, width = tokens.shape
    capacity = max(2, 2 * tok_rows // experts)
    route = expert_ids[:, 0]
    onehot = (route[:, None] == jnp.arange(experts, dtype=jnp.int32)[None, :]).astype(jnp.int32)
    before = jnp.cumsum(onehot, axis=0) - onehot
    target = route * capacity + jnp.sum(before * onehot, axis=1)
    slot = jnp.arange(experts * capacity, dtype=jnp.int32)
    placing = (target[None, :] == slot[:, None]).astype(BF16)
    both = jnp.concatenate([tokens, upstream], axis=1)
    own = to_experts(jnp.dot(placing, both, preferred_element_type=F32).astype(BF16), experts)
    x_all = lax.all_gather(own[:, :width], "tensor", axis=1, tiled=True)
    dy_all = lax.all_gather(own[:, width:], "tensor", axis=1, tiled=True)
    gate_pre = rows_by_weights(x_all, gate_rows)
    up_pre = rows_by_weights(x_all, up_rows)
    d_hidden = rows_by_weights(dy_all, down_rows)
    sig = jax.nn.sigmoid(gate_pre)
    silu = gate_pre * sig
    hidden = (silu * up_pre).astype(BF16)
    d_up = (d_hidden * silu).astype(BF16)
    d_gate = (d_hidden * up_pre * sig * (1.0 + gate_pre * (1.0 - sig))).astype(BF16)
    partial = jnp.dot(d_gate, gate_rows, preferred_element_type=F32) + jnp.dot(
        d_up, up_rows, preferred_element_type=F32
    )
    totals = lax.psum_scatter(partial.astype(BF16), "tensor", scatter_dimension=1, tiled=True)
    returned = to_experts(totals, experts)
    grads = [weight_grad(d_gate, x_all), weight_grad(d_up, x_all), weight_grad(hidden, dy_all)]
    return weight_grad(placing, returned), grads


def on_device(tokens, upstream, expert_ids, w_gate, w_up, w_down):
    experts = lax.axis_size("expert")
    capacity = 2 * tokens.shape[0] // experts
    pairs = lax.axis_size("tensor") == 2 and experts & (experts - 1) == 0 and experts > 4
    run = grouped if pairs and capacity % 16 == 0 else general
    grad_tokens, grads = run(tokens, upstream, expert_ids, w_gate[0], w_up[0], w_down[0])
    return (grad_tokens, *(grad[None] for grad in grads))


def solution(mesh):
    rows = P("expert", "tensor")
    weights = P("expert", "tensor", None)
    return jax.shard_map(
        on_device,
        mesh=mesh,
        in_specs=(rows, rows, P("expert", None), weights, weights, weights),
        out_specs=(rows, weights, weights, weights),
        check_vma=False,
    )
```

```python
import functools

import jax
import jax.numpy as jnp
from jax import lax
from jax.experimental import pallas as pl
from jax.experimental.pallas import tpu as pltpu
from jax.sharding import PartitionSpec as P

F32 = jnp.float32
BF16 = jnp.bfloat16
SMALL = 20 * 2**20
LARGE = 56 * 2**20
PIECES = 4
COLLECT = 16
IN_VMEM = pl.BlockSpec(memory_space=pltpu.VMEM)
ANYWHERE = pl.BlockSpec(memory_space=pl.ANY)


def rank_among_same(row, axis):
    rows = row.shape[1]
    down = lax.broadcasted_iota(jnp.int32, (rows, rows), 0)
    right = lax.broadcasted_iota(jnp.int32, (rows, rows), 1)
    col = jnp.sum(jnp.where(down == right, row, 0), axis=1, keepdims=True)
    earlier = down > right if axis else down < right
    same = jnp.where((col == row) & earlier, 1, 0)
    return (col if axis else row), jnp.sum(same, axis=axis, keepdims=True)


def place_kernel(capacity, row_ref, x_hbm, dy_hbm, *refs):
    *slabs, x_ref, dy_ref, sems = refs
    step = x_ref.shape[0] // PIECES
    copies = [
        [
            pltpu.make_async_copy(
                from_ref.at[i * step : (i + 1) * step],
                to_ref.at[i * step : (i + 1) * step],
                sems.at[which, i],
            )
            for i in range(PIECES)
        ]
        for which, (from_ref, to_ref) in enumerate(((x_hbm, x_ref), (dy_hbm, dy_ref)))
    ]
    for copy in copies[0] + copies[1]:
        copy.start()
    me = lax.axis_index("expert")
    route, within = rank_among_same(row_ref[...], 0)
    slots = len(slabs) * capacity
    slot = lax.broadcasted_iota(jnp.int32, (slots, x_ref.shape[0]), 0)
    placing = jnp.where(slot == (route ^ me) * capacity + within, 1.0, 0.0).astype(BF16)
    for i, ref in enumerate((x_ref, dy_ref)):
        for copy in copies[i]:
            copy.wait()
        placed = jnp.dot(placing, ref[...], preferred_element_type=F32).astype(BF16)
        for k, slab in enumerate(slabs):
            slab[i * capacity : (i + 1) * capacity, :] = placed[k * capacity : (k + 1) * capacity]


def collect_kernel(capacity, *refs):
    *slabs, out_ref = refs
    half = len(slabs) * capacity
    for i, slab in enumerate(slabs):
        out_ref[i * capacity : (i + 1) * capacity, :] = slab[:capacity, :]
        out_ref[half + i * capacity : half + (i + 1) * capacity, :] = slab[capacity:, :]


def side(which, width):
    return pl.ds(pl.multiple_of(which * width, width), width)


def input_rows(d_gate_ref, d_up_ref, gate_ref, up_ref, columns):
    over_hidden = (((0,), (0,)), ((), ()))
    return lax.dot_general(
        d_gate_ref[...], gate_ref[:, columns], over_hidden, preferred_element_type=F32
    ) + lax.dot_general(
        d_up_ref[...], up_ref[:, columns], over_hidden, preferred_element_type=F32
    )


def front_kernel(tile, own_ref, other_ref, gate_ref, up_ref, down_ref, *refs):
    x_ref, dy_ref, hidden_ref, d_gate_ref, d_up_ref, sent_ref = refs
    rows, width = x_ref.shape[0], own_ref.shape[1]
    mine = lax.axis_index("tensor")
    for half, whole_ref in enumerate((x_ref, dy_ref)):
        whole_ref[:, side(mine, width)] = own_ref[half * rows : (half + 1) * rows, :]
        whole_ref[:, side(1 - mine, width)] = other_ref[half * rows : (half + 1) * rows, :]
    over_features = (((1,), (1,)), ((), ()))

    @pl.loop(0, hidden_ref.shape[0] // tile)
    def _(step):
        units = pl.ds(pl.multiple_of(step * tile, tile), tile)

        def product(weight_ref, whole_ref):
            return lax.dot_general(
                weight_ref[units, :], whole_ref[...], over_features, preferred_element_type=F32
            )

        gate_pre = product(gate_ref, x_ref)
        up_pre = product(up_ref, x_ref)
        d_hidden = product(down_ref, dy_ref)
        sig = jax.nn.sigmoid(gate_pre)
        silu = gate_pre * sig
        hidden_ref[units, :] = (silu * up_pre).astype(BF16)
        d_up_ref[units, :] = (d_hidden * silu).astype(BF16)
        d_gate_ref[units, :] = (
            d_hidden * up_pre * sig * (1.0 + gate_pre * (1.0 - sig))
        ).astype(BF16)

    sent_ref[...] = input_rows(
        d_gate_ref, d_up_ref, gate_ref, up_ref, side(1 - mine, width)
    ).astype(BF16)


def kept_kernel(d_gate_ref, d_up_ref, gate_ref, up_ref, out_ref):
    columns = side(lax.axis_index("tensor"), out_ref.shape[1])
    out_ref[...] = input_rows(d_gate_ref, d_up_ref, gate_ref, up_ref, columns)


def total_kernel(capacity, groups, *refs):
    *parts, out_ref, done_ref = refs
    me = lax.axis_index("expert")
    done_ref[...] = jnp.zeros_like(done_ref)
    for kept_ref, got_ref, group in zip(parts[::2], parts[1::2], groups):
        for i, k in enumerate(group):
            here = slice(i * capacity, (i + 1) * capacity)
            there = pl.ds(pl.multiple_of((me ^ k) * capacity, capacity), capacity)
            out_ref[there, :] = (kept_ref[here, :] + got_ref[here, :].astype(F32)).astype(BF16)


def grads_kernel(groups, *refs):
    *ins, _, grad_gate_ref, grad_up_ref, grad_down_ref = refs
    by_group = [ins[i :: groups] for i in range(groups)]

    def total(left, right):
        return sum(
            jnp.dot(one[left][...], one[right][...], preferred_element_type=F32)
            for one in by_group
        ).astype(BF16)

    grad_gate_ref[...] = total(0, 3)
    grad_up_ref[...] = total(1, 3)
    grad_down_ref[...] = total(2, 4)


def combine_kernel(capacity, row_ref, back_hbm, out_ref, back_ref, sems):
    slots = back_ref.shape[0]
    step = slots // PIECES
    copies = [
        pltpu.make_async_copy(
            back_hbm.at[i * step : (i + 1) * step],
            back_ref.at[i * step : (i + 1) * step],
            sems.at[i],
        )
        for i in range(PIECES)
    ]
    for copy in copies:
        copy.start()
    route, within = rank_among_same(row_ref[...], 1)
    slot = lax.broadcasted_iota(jnp.int32, (out_ref.shape[0], slots), 1)
    placing = jnp.where(slot == route * capacity + within, 1.0, 0.0).astype(BF16)
    total = jnp.zeros(out_ref.shape, F32)
    for i, copy in enumerate(copies):
        copy.wait()
        total += jnp.dot(
            placing[:, i * step : (i + 1) * step],
            back_ref[i * step : (i + 1) * step],
            preferred_element_type=F32,
        )
    out_ref[...] = total.astype(BF16)


def params(limit):
    return pltpu.CompilerParams(vmem_limit_bytes=limit)


def cost(products, rows, hidden, features):
    return pl.CostEstimate(
        flops=2 * products * rows * hidden * features,
        bytes_accessed=2 * products * (hidden + rows) * features,
        transcendentals=0,
    )


def combine(capacity, ids_row, returned, tok_rows):
    slots, width = returned.shape
    return pl.pallas_call(
        functools.partial(combine_kernel, capacity),
        out_shape=jax.ShapeDtypeStruct((tok_rows, width), BF16),
        in_specs=[IN_VMEM, ANYWHERE],
        out_specs=IN_VMEM,
        scratch_shapes=[pltpu.VMEM((slots, width), BF16), pltpu.SemaphoreType.DMA((PIECES,))],
        compiler_params=params(LARGE),
        name="combine",
    )(ids_row, returned)


def to_experts(rows, experts):
    return lax.all_to_all(
        rows.reshape(experts, rows.shape[0] // experts, rows.shape[1]),
        "expert",
        split_axis=0,
        concat_axis=0,
        tiled=True,
    ).reshape(rows.shape)


def grouped(tokens, upstream, expert_ids, gate_rows, up_rows, down_rows):
    experts = lax.axis_size("expert")
    tok_rows, width = tokens.shape
    units, features = gate_rows.shape
    capacity = max(2, 2 * tok_rows // experts)
    ids_row = expert_ids.reshape(1, tok_rows)
    tile = units // 2 if units % 32 == 0 else units

    far = [k for k in reversed(range(1, experts)) if k >= experts // 2]
    near = [k for k in reversed(range(1, experts)) if k < experts // 2]
    turns = [k for pair in zip(far, near) for k in pair] + far[len(near) :]
    first, second = [0] + turns[: experts // 2 - 1], turns[experts // 2 - 1 :]
    rows = len(first) * capacity

    slabs = list(
        pl.pallas_call(
            functools.partial(place_kernel, capacity),
            out_shape=[jax.ShapeDtypeStruct((2 * capacity, width), BF16)] * experts,
            in_specs=[IN_VMEM, ANYWHERE, ANYWHERE],
            out_specs=[IN_VMEM] * experts,
            scratch_shapes=[
                pltpu.VMEM((tok_rows, width), BF16),
                pltpu.VMEM((tok_rows, width), BF16),
                pltpu.SemaphoreType.DMA((2, PIECES)),
            ],
            compiler_params=params(LARGE),
            name="place",
        )(ids_row, tokens, upstream)
    )

    def swap(k):
        return lax.ppermute(slabs[k], "expert", [(e, e ^ k) for e in range(experts)])

    def exchange(values):
        return lax.ppermute(values, "tensor", [(0, 1), (1, 0)])

    def collect(arrived):
        return pl.pallas_call(
            functools.partial(collect_kernel, capacity),
            out_shape=jax.ShapeDtypeStruct((2 * rows, width), BF16),
            in_specs=[IN_VMEM] * len(arrived),
            out_specs=IN_VMEM,
            compiler_params=params(SMALL),
            cost_estimate=cost(COLLECT, rows, units, features),
            name="collect",
        )(*arrived)

    def front(own):
        other = exchange(own)
        return pl.pallas_call(
            functools.partial(front_kernel, tile),
            out_shape=[jax.ShapeDtypeStruct((rows, features), BF16)] * 2
            + [jax.ShapeDtypeStruct((units, rows), BF16)] * 3
            + [jax.ShapeDtypeStruct((rows, width), BF16)],
            in_specs=[IN_VMEM] * 5,
            out_specs=[IN_VMEM] * 6,
            compiler_params=params(SMALL),
            cost_estimate=cost(4, rows, units, features),
            name="front",
        )(own, other, gate_rows, up_rows, down_rows)

    def kept_rows(d_gate, d_up):
        return pl.pallas_call(
            kept_kernel,
            out_shape=jax.ShapeDtypeStruct((rows, width), F32),
            in_specs=[IN_VMEM] * 4,
            out_specs=IN_VMEM,
            compiler_params=params(SMALL),
            cost_estimate=cost(1, rows, units, features),
            name="kept",
        )(d_gate, d_up, gate_rows, up_rows)

    got = {k: swap(k) for k in turns}
    got[0] = slabs[0]
    front_a = front(collect([got[k] for k in first]))
    front_b = front(collect([got[k] for k in second]))
    sums = []
    for _, _, _, d_gate, d_up, sent in (front_a, front_b):
        sums += [kept_rows(d_gate, d_up), exchange(sent)]
    totals, done = pl.pallas_call(
        functools.partial(total_kernel, capacity, (first, second)),
        out_shape=[
            jax.ShapeDtypeStruct((experts * capacity, width), BF16),
            jax.ShapeDtypeStruct((8, 128), F32),
        ],
        in_specs=[IN_VMEM] * 4,
        out_specs=[IN_VMEM] * 2,
        compiler_params=params(SMALL),
        name="total",
    )(*sums)
    returned = to_experts(totals, experts)

    lefts = [front_a[3], front_b[3], front_a[4], front_b[4], front_a[2], front_b[2]]
    rights = [front_a[0], front_b[0], front_a[1], front_b[1]]
    grads = pl.pallas_call(
        functools.partial(grads_kernel, 2),
        grid=(units // tile,),
        out_shape=[jax.ShapeDtypeStruct((units, features), BF16)] * 3,
        in_specs=[pl.BlockSpec((tile, rows), lambda i: (i, 0))] * 6
        + [pl.BlockSpec((rows, features), lambda i: (0, 0))] * 4
        + [pl.BlockSpec((8, 128), lambda i: (0, 0))],
        out_specs=[pl.BlockSpec((tile, features), lambda i: (i, 0))] * 3,
        compiler_params=params(32 * 2**20),
        cost_estimate=cost(6, rows, units, features),
        name="grads",
    )(*lefts, *rights, done)
    return combine(capacity, ids_row, returned, tok_rows), grads


def rows_by_weights(rows, weights):
    return lax.dot_general(rows, weights, (((1,), (1,)), ((), ())), preferred_element_type=F32)


def weight_grad(left, right):
    return lax.dot_general(
        left, right, (((0,), (0,)), ((), ())), preferred_element_type=F32
    ).astype(BF16)


def general(tokens, upstream, expert_ids, gate_rows, up_rows, down_rows):
    experts = lax.axis_size("expert")
    tok_rows, width = tokens.shape
    capacity = max(2, 2 * tok_rows // experts)
    route = expert_ids[:, 0]
    onehot = (route[:, None] == jnp.arange(experts, dtype=jnp.int32)[None, :]).astype(jnp.int32)
    before = jnp.cumsum(onehot, axis=0) - onehot
    target = route * capacity + jnp.sum(before * onehot, axis=1)
    slot = jnp.arange(experts * capacity, dtype=jnp.int32)
    placing = (target[None, :] == slot[:, None]).astype(BF16)
    both = jnp.concatenate([tokens, upstream], axis=1)
    own = to_experts(jnp.dot(placing, both, preferred_element_type=F32).astype(BF16), experts)
    x_all = lax.all_gather(own[:, :width], "tensor", axis=1, tiled=True)
    dy_all = lax.all_gather(own[:, width:], "tensor", axis=1, tiled=True)
    gate_pre = rows_by_weights(x_all, gate_rows)
    up_pre = rows_by_weights(x_all, up_rows)
    d_hidden = rows_by_weights(dy_all, down_rows)
    sig = jax.nn.sigmoid(gate_pre)
    silu = gate_pre * sig
    hidden = (silu * up_pre).astype(BF16)
    d_up = (d_hidden * silu).astype(BF16)
    d_gate = (d_hidden * up_pre * sig * (1.0 + gate_pre * (1.0 - sig))).astype(BF16)
    partial = jnp.dot(d_gate, gate_rows, preferred_element_type=F32) + jnp.dot(
        d_up, up_rows, preferred_element_type=F32
    )
    totals = lax.psum_scatter(partial.astype(BF16), "tensor", scatter_dimension=1, tiled=True)
    returned = to_experts(totals, experts)
    grads = [weight_grad(d_gate, x_all), weight_grad(d_up, x_all), weight_grad(hidden, dy_all)]
    return weight_grad(placing, returned), grads


def on_device(tokens, upstream, expert_ids, w_gate, w_up, w_down):
    experts = lax.axis_size("expert")
    capacity = 2 * tokens.shape[0] // experts
    pairs = lax.axis_size("tensor") == 2 and experts & (experts - 1) == 0 and experts > 4
    run = grouped if pairs and capacity % 16 == 0 else general
    grad_tokens, grads = run(tokens, upstream, expert_ids, w_gate[0], w_up[0], w_down[0])
    return (grad_tokens, *(grad[None] for grad in grads))


def solution(mesh):
    rows = P("expert", "tensor")
    weights = P("expert", "tensor", None)
    return jax.shard_map(
        on_device,
        mesh=mesh,
        in_specs=(rows, rows, P("expert", None), weights, weights, weights),
        out_specs=(rows, weights, weights, weights),
        check_vma=False,
    )
```

```python
import functools

import jax
import jax.numpy as jnp
from jax import lax
from jax.experimental import pallas as pl
from jax.experimental.pallas import tpu as pltpu
from jax.sharding import PartitionSpec as P

F32 = jnp.float32
BF16 = jnp.bfloat16
SMALL = 20 * 2**20
LARGE = 56 * 2**20
PIECES = 4
COLLECT = 16
IN_VMEM = pl.BlockSpec(memory_space=pltpu.VMEM)
ANYWHERE = pl.BlockSpec(memory_space=pl.ANY)


def rank_among_same(row, axis):
    rows = row.shape[1]
    down = lax.broadcasted_iota(jnp.int32, (rows, rows), 0)
    right = lax.broadcasted_iota(jnp.int32, (rows, rows), 1)
    col = jnp.sum(jnp.where(down == right, row, 0), axis=1, keepdims=True)
    earlier = down > right if axis else down < right
    same = jnp.where((col == row) & earlier, 1, 0)
    return (col if axis else row), jnp.sum(same, axis=axis, keepdims=True)


def place_kernel(capacity, row_ref, x_hbm, dy_hbm, *refs):
    *slabs, x_ref, dy_ref, sems = refs
    step = x_ref.shape[0] // PIECES
    copies = [
        [
            pltpu.make_async_copy(
                from_ref.at[i * step : (i + 1) * step],
                to_ref.at[i * step : (i + 1) * step],
                sems.at[which, i],
            )
            for i in range(PIECES)
        ]
        for which, (from_ref, to_ref) in enumerate(((x_hbm, x_ref), (dy_hbm, dy_ref)))
    ]
    for copy in copies[0] + copies[1]:
        copy.start()
    me = lax.axis_index("expert")
    route, within = rank_among_same(row_ref[...], 0)
    slots = len(slabs) * capacity
    slot = lax.broadcasted_iota(jnp.int32, (slots, x_ref.shape[0]), 0)
    placing = jnp.where(slot == (route ^ me) * capacity + within, 1.0, 0.0).astype(BF16)
    for i, ref in enumerate((x_ref, dy_ref)):
        for copy in copies[i]:
            copy.wait()
        placed = jnp.dot(placing, ref[...], preferred_element_type=F32).astype(BF16)
        for k, slab in enumerate(slabs):
            slab[i * capacity : (i + 1) * capacity, :] = placed[k * capacity : (k + 1) * capacity]


def collect_kernel(capacity, count, *refs):
    slabs, out_ref = refs[:count], refs[-1]
    half = len(slabs) * capacity
    for i, slab in enumerate(slabs):
        out_ref[i * capacity : (i + 1) * capacity, :] = slab[:capacity, :]
        out_ref[half + i * capacity : half + (i + 1) * capacity, :] = slab[capacity:, :]


def side(which, width):
    return pl.ds(pl.multiple_of(which * width, width), width)


def input_rows(d_gate_ref, d_up_ref, gate_ref, up_ref, columns):
    over_hidden = (((0,), (0,)), ((), ()))
    return lax.dot_general(
        d_gate_ref[...], gate_ref[:, columns], over_hidden, preferred_element_type=F32
    ) + lax.dot_general(
        d_up_ref[...], up_ref[:, columns], over_hidden, preferred_element_type=F32
    )


def front_kernel(
    tile, own_ref, other_ref, gate_ref, up_ref, down_ref, hidden_ref, d_gate_ref, d_up_ref, sent_ref
):
    rows, width = sent_ref.shape
    mine = lax.axis_index("tensor")
    over_features = (((1,), (1,)), ((), ()))

    @pl.loop(0, hidden_ref.shape[0] // tile)
    def _(step):
        units = pl.ds(pl.multiple_of(step * tile, tile), tile)

        def product(weight_ref, start):
            return sum(
                lax.dot_general(
                    weight_ref[units, side(which, width)],
                    half_ref[start : start + rows, :],
                    over_features,
                    preferred_element_type=F32,
                )
                for which, half_ref in ((mine, own_ref), (1 - mine, other_ref))
            )

        gate_pre = product(gate_ref, 0)
        up_pre = product(up_ref, 0)
        d_hidden = product(down_ref, rows)
        sig = jax.nn.sigmoid(gate_pre)
        silu = gate_pre * sig
        hidden_ref[units, :] = (silu * up_pre).astype(BF16)
        d_up_ref[units, :] = (d_hidden * silu).astype(BF16)
        d_gate_ref[units, :] = (
            d_hidden * up_pre * sig * (1.0 + gate_pre * (1.0 - sig))
        ).astype(BF16)

    sent_ref[...] = input_rows(
        d_gate_ref, d_up_ref, gate_ref, up_ref, side(1 - mine, width)
    ).astype(BF16)


def kept_kernel(d_gate_ref, d_up_ref, gate_ref, up_ref, out_ref):
    columns = side(lax.axis_index("tensor"), out_ref.shape[1])
    out_ref[...] = input_rows(d_gate_ref, d_up_ref, gate_ref, up_ref, columns)


def total_kernel(capacity, groups, *refs):
    *parts, out_ref, done_ref = refs
    me = lax.axis_index("expert")
    done_ref[...] = jnp.zeros_like(done_ref)
    for kept_ref, got_ref, group in zip(parts[::2], parts[1::2], groups):
        for i, k in enumerate(group):
            here = slice(i * capacity, (i + 1) * capacity)
            there = pl.ds(pl.multiple_of((me ^ k) * capacity, capacity), capacity)
            out_ref[there, :] = (kept_ref[here, :] + got_ref[here, :].astype(F32)).astype(BF16)


def grads_kernel(sizes, *refs):
    *ins, _, grad_gate_ref, grad_up_ref, grad_down_ref = refs
    mine = lax.axis_index("tensor")
    groups = [(*ins[5 * i : 5 * i + 5], rows) for i, rows in enumerate(sizes)]
    width = groups[0][0].shape[1]

    def total(left, half, second):
        return sum(
            jnp.dot(
                one[left][...],
                one[half][one[5] * second : one[5] * (second + 1), :],
                preferred_element_type=F32,
            )
            for one in groups
        ).astype(BF16)

    for half, which in enumerate((mine, 1 - mine)):
        grad_gate_ref[:, side(which, width)] = total(2, half, 0)
        grad_up_ref[:, side(which, width)] = total(3, half, 0)
        grad_down_ref[:, side(which, width)] = total(4, half, 1)


def combine_kernel(capacity, row_ref, back_hbm, out_ref, back_ref, sems):
    slots = back_ref.shape[0]
    step = slots // PIECES
    copies = [
        pltpu.make_async_copy(
            back_hbm.at[i * step : (i + 1) * step],
            back_ref.at[i * step : (i + 1) * step],
            sems.at[i],
        )
        for i in range(PIECES)
    ]
    for copy in copies:
        copy.start()
    route, within = rank_among_same(row_ref[...], 1)
    slot = lax.broadcasted_iota(jnp.int32, (out_ref.shape[0], slots), 1)
    placing = jnp.where(slot == route * capacity + within, 1.0, 0.0).astype(BF16)
    total = jnp.zeros(out_ref.shape, F32)
    for i, copy in enumerate(copies):
        copy.wait()
        total += jnp.dot(
            placing[:, i * step : (i + 1) * step],
            back_ref[i * step : (i + 1) * step],
            preferred_element_type=F32,
        )
    out_ref[...] = total.astype(BF16)


def params(limit):
    return pltpu.CompilerParams(vmem_limit_bytes=limit)


def cost(products, rows, hidden, features):
    return pl.CostEstimate(
        flops=2 * products * rows * hidden * features,
        bytes_accessed=2 * products * (hidden + rows) * features,
        transcendentals=0,
    )


def combine(capacity, ids_row, returned, tok_rows):
    slots, width = returned.shape
    return pl.pallas_call(
        functools.partial(combine_kernel, capacity),
        out_shape=jax.ShapeDtypeStruct((tok_rows, width), BF16),
        in_specs=[IN_VMEM, ANYWHERE],
        out_specs=IN_VMEM,
        scratch_shapes=[pltpu.VMEM((slots, width), BF16), pltpu.SemaphoreType.DMA((PIECES,))],
        compiler_params=params(LARGE),
        name="combine",
    )(ids_row, returned)


def to_experts(rows, experts):
    return lax.all_to_all(
        rows.reshape(experts, rows.shape[0] // experts, rows.shape[1]),
        "expert",
        split_axis=0,
        concat_axis=0,
        tiled=True,
    ).reshape(rows.shape)


def grouped(tokens, upstream, expert_ids, gate_rows, up_rows, down_rows):
    experts = lax.axis_size("expert")
    tok_rows, width = tokens.shape
    units, features = gate_rows.shape
    capacity = max(2, 2 * tok_rows // experts)
    ids_row = expert_ids.reshape(1, tok_rows)
    tile = units // 2 if units % 32 == 0 else units

    far = [k for k in reversed(range(1, experts)) if k >= experts // 2]
    near = [k for k in reversed(range(1, experts)) if k < experts // 2]
    turns = [k for pair in zip(far, near) for k in pair] + far[len(near) :]
    cut = 3 * experts // 4
    first, second = turns[:cut], turns[cut:] + [0]

    slabs = list(
        pl.pallas_call(
            functools.partial(place_kernel, capacity),
            out_shape=[jax.ShapeDtypeStruct((2 * capacity, width), BF16)] * experts,
            in_specs=[IN_VMEM, ANYWHERE, ANYWHERE],
            out_specs=[IN_VMEM] * experts,
            scratch_shapes=[
                pltpu.VMEM((tok_rows, width), BF16),
                pltpu.VMEM((tok_rows, width), BF16),
                pltpu.SemaphoreType.DMA((2, PIECES)),
            ],
            compiler_params=params(LARGE),
            name="place",
        )(ids_row, tokens, upstream)
    )

    def swap(k):
        return lax.ppermute(slabs[k], "expert", [(e, e ^ k) for e in range(experts)])

    def exchange(values):
        return lax.ppermute(values, "tensor", [(0, 1), (1, 0)])

    def collect(arrived, after):
        return pl.pallas_call(
            functools.partial(collect_kernel, capacity, len(arrived)),
            out_shape=jax.ShapeDtypeStruct((2 * len(arrived) * capacity, width), BF16),
            in_specs=[IN_VMEM] * (len(arrived) + len(after)),
            out_specs=IN_VMEM,
            compiler_params=params(SMALL),
            cost_estimate=cost(COLLECT, len(arrived) * capacity, units, features),
            name="collect",
        )(*arrived, *after)

    def front(own):
        other = exchange(own)
        rows = own.shape[0] // 2
        hidden, d_gate, d_up, sent = pl.pallas_call(
            functools.partial(front_kernel, tile),
            out_shape=[jax.ShapeDtypeStruct((units, rows), BF16)] * 3
            + [jax.ShapeDtypeStruct((rows, width), BF16)],
            in_specs=[IN_VMEM] * 5,
            out_specs=[IN_VMEM] * 4,
            compiler_params=params(SMALL),
            cost_estimate=cost(4, rows, units, features),
            name="front",
        )(own, other, gate_rows, up_rows, down_rows)
        kept = pl.pallas_call(
            kept_kernel,
            out_shape=jax.ShapeDtypeStruct((rows, width), F32),
            in_specs=[IN_VMEM] * 4,
            out_specs=IN_VMEM,
            compiler_params=params(SMALL),
            cost_estimate=cost(1, rows, units, features),
            name="kept",
        )(d_gate, d_up, gate_rows, up_rows)
        return (own, other, d_gate, d_up, hidden), (kept, exchange(sent))

    got = {k: swap(k) for k in turns}
    got[0] = slabs[0]
    for_grads_a, sums_a = front(collect([got[k] for k in first], []))
    for_grads_b, sums_b = front(collect([got[k] for k in second], sums_a[:1]))
    totals, done = pl.pallas_call(
        functools.partial(total_kernel, capacity, (first, second)),
        out_shape=[
            jax.ShapeDtypeStruct((experts * capacity, width), BF16),
            jax.ShapeDtypeStruct((8, 128), F32),
        ],
        in_specs=[IN_VMEM] * 4,
        out_specs=[IN_VMEM] * 2,
        compiler_params=params(SMALL),
        name="total",
    )(*sums_a, *sums_b)
    returned = to_experts(totals, experts)

    def grads_specs(rows):
        return [pl.BlockSpec((2 * rows, width), lambda i: (0, 0))] * 2 + [
            pl.BlockSpec((tile, rows), lambda i: (i, 0))
        ] * 3

    sizes = [len(group) * capacity for group in (first, second)]
    grads = pl.pallas_call(
        functools.partial(grads_kernel, sizes),
        grid=(units // tile,),
        out_shape=[jax.ShapeDtypeStruct((units, features), BF16)] * 3,
        in_specs=grads_specs(sizes[0])
        + grads_specs(sizes[1])
        + [pl.BlockSpec((8, 128), lambda i: (0, 0))],
        out_specs=[pl.BlockSpec((tile, features), lambda i: (i, 0))] * 3,
        compiler_params=params(32 * 2**20),
        cost_estimate=cost(3, sum(sizes), units, features),
        name="grads",
    )(*for_grads_a, *for_grads_b, done)
    return combine(capacity, ids_row, returned, tok_rows), grads


def rows_by_weights(rows, weights):
    return lax.dot_general(rows, weights, (((1,), (1,)), ((), ())), preferred_element_type=F32)


def weight_grad(left, right):
    return lax.dot_general(
        left, right, (((0,), (0,)), ((), ())), preferred_element_type=F32
    ).astype(BF16)


def general(tokens, upstream, expert_ids, gate_rows, up_rows, down_rows):
    experts = lax.axis_size("expert")
    tok_rows, width = tokens.shape
    capacity = max(2, 2 * tok_rows // experts)
    route = expert_ids[:, 0]
    onehot = (route[:, None] == jnp.arange(experts, dtype=jnp.int32)[None, :]).astype(jnp.int32)
    before = jnp.cumsum(onehot, axis=0) - onehot
    target = route * capacity + jnp.sum(before * onehot, axis=1)
    slot = jnp.arange(experts * capacity, dtype=jnp.int32)
    placing = (target[None, :] == slot[:, None]).astype(BF16)
    both = jnp.concatenate([tokens, upstream], axis=1)
    own = to_experts(jnp.dot(placing, both, preferred_element_type=F32).astype(BF16), experts)
    x_all = lax.all_gather(own[:, :width], "tensor", axis=1, tiled=True)
    dy_all = lax.all_gather(own[:, width:], "tensor", axis=1, tiled=True)
    gate_pre = rows_by_weights(x_all, gate_rows)
    up_pre = rows_by_weights(x_all, up_rows)
    d_hidden = rows_by_weights(dy_all, down_rows)
    sig = jax.nn.sigmoid(gate_pre)
    silu = gate_pre * sig
    hidden = (silu * up_pre).astype(BF16)
    d_up = (d_hidden * silu).astype(BF16)
    d_gate = (d_hidden * up_pre * sig * (1.0 + gate_pre * (1.0 - sig))).astype(BF16)
    partial = jnp.dot(d_gate, gate_rows, preferred_element_type=F32) + jnp.dot(
        d_up, up_rows, preferred_element_type=F32
    )
    totals = lax.psum_scatter(partial.astype(BF16), "tensor", scatter_dimension=1, tiled=True)
    returned = to_experts(totals, experts)
    grads = [weight_grad(d_gate, x_all), weight_grad(d_up, x_all), weight_grad(hidden, dy_all)]
    return weight_grad(placing, returned), grads


def on_device(tokens, upstream, expert_ids, w_gate, w_up, w_down):
    experts = lax.axis_size("expert")
    capacity = 2 * tokens.shape[0] // experts
    pairs = lax.axis_size("tensor") == 2 and experts & (experts - 1) == 0 and experts > 4
    run = grouped if pairs and capacity % 16 == 0 else general
    grad_tokens, grads = run(tokens, upstream, expert_ids, w_gate[0], w_up[0], w_down[0])
    return (grad_tokens, *(grad[None] for grad in grads))


def solution(mesh):
    rows = P("expert", "tensor")
    weights = P("expert", "tensor", None)
    return jax.shard_map(
        on_device,
        mesh=mesh,
        in_specs=(rows, rows, P("expert", None), weights, weights, weights),
        out_specs=(rows, weights, weights, weights),
        check_vma=False,
    )
```

```python
import functools

import jax
import jax.numpy as jnp
from jax import lax
from jax.experimental import pallas as pl
from jax.experimental.pallas import tpu as pltpu
from jax.sharding import PartitionSpec as P

F32 = jnp.float32
BF16 = jnp.bfloat16
SMALL = 16 * 2**20
LARGE = 56 * 2**20
PIECES = 4
COLLECT = 16
IN_VMEM = pl.BlockSpec(memory_space=pltpu.VMEM)
IN_HBM = pl.BlockSpec(memory_space=pltpu.HBM)


def rank_among_same(row, axis):
    rows = row.shape[1]
    down = lax.broadcasted_iota(jnp.int32, (rows, rows), 0)
    right = lax.broadcasted_iota(jnp.int32, (rows, rows), 1)
    col = jnp.sum(jnp.where(down == right, row, 0), axis=1, keepdims=True)
    earlier = down > right if axis else down < right
    same = jnp.where((col == row) & earlier, 1, 0)
    return (col if axis else row), jnp.sum(same, axis=axis, keepdims=True)


def place_kernel(capacity, row_hbm, x_hbm, dy_hbm, *refs):
    *slabs, row_ref, x_ref, dy_ref, placed_ref, row_sem, in_sems, out_sems = refs
    row_copy = pltpu.make_async_copy(row_hbm, row_ref, row_sem)
    row_copy.start()
    step = x_ref.shape[0] // PIECES
    copies = [
        [
            pltpu.make_async_copy(
                from_ref.at[i * step : (i + 1) * step],
                to_ref.at[i * step : (i + 1) * step],
                in_sems.at[which, i],
            )
            for i in range(PIECES)
        ]
        for which, (from_ref, to_ref) in enumerate(((x_hbm, x_ref), (dy_hbm, dy_ref)))
    ]
    for copy in copies[0] + copies[1]:
        copy.start()
    me = lax.axis_index("expert")
    row_copy.wait()
    route, within = rank_among_same(row_ref[...], 0)
    slots = len(slabs) * capacity
    slot = lax.broadcasted_iota(jnp.int32, (slots, x_ref.shape[0]), 0)
    placing = jnp.where(slot == (route ^ me) * capacity + within, 1.0, 0.0).astype(BF16)
    out_copies = []
    for i, ref in enumerate((x_ref, dy_ref)):
        for copy in copies[i]:
            copy.wait()
        placed_ref[i] = jnp.dot(placing, ref[...], preferred_element_type=F32).astype(BF16)
        for k, slab in enumerate(slabs):
            out_copies.append(
                pltpu.make_async_copy(
                    placed_ref.at[i, k * capacity : (k + 1) * capacity],
                    slab.at[i * capacity : (i + 1) * capacity],
                    out_sems.at[i, k],
                )
            )
            out_copies[-1].start()
    for copy in out_copies:
        copy.wait()


def collect_kernel(capacity, count, *refs):
    slabs, out_ref = refs[:count], refs[-1]
    half = len(slabs) * capacity
    for i, slab in enumerate(slabs):
        out_ref[i * capacity : (i + 1) * capacity, :] = slab[:capacity, :]
        out_ref[half + i * capacity : half + (i + 1) * capacity, :] = slab[capacity:, :]


def side(which, width):
    return pl.ds(pl.multiple_of(which * width, width), width)


def input_rows(d_gate_ref, d_up_ref, gate_ref, up_ref, columns):
    over_hidden = (((0,), (0,)), ((), ()))
    return lax.dot_general(
        d_gate_ref[...], gate_ref[:, columns], over_hidden, preferred_element_type=F32
    ) + lax.dot_general(
        d_up_ref[...], up_ref[:, columns], over_hidden, preferred_element_type=F32
    )


def front_kernel(
    tile, own_ref, other_ref, gate_ref, up_ref, down_ref, hidden_ref, d_gate_ref, d_up_ref, sent_ref
):
    rows, width = sent_ref.shape
    mine = lax.axis_index("tensor")
    over_features = (((1,), (1,)), ((), ()))

    @pl.loop(0, hidden_ref.shape[0] // tile)
    def _(step):
        units = pl.ds(pl.multiple_of(step * tile, tile), tile)

        def product(weight_ref, start):
            return sum(
                lax.dot_general(
                    weight_ref[units, side(which, width)],
                    half_ref[start : start + rows, :],
                    over_features,
                    preferred_element_type=F32,
                )
                for which, half_ref in ((mine, own_ref), (1 - mine, other_ref))
            )

        gate_pre = product(gate_ref, 0)
        up_pre = product(up_ref, 0)
        d_hidden = product(down_ref, rows)
        sig = jax.nn.sigmoid(gate_pre)
        silu = gate_pre * sig
        hidden_ref[units, :] = (silu * up_pre).astype(BF16)
        d_up_ref[units, :] = (d_hidden * silu).astype(BF16)
        d_gate_ref[units, :] = (
            d_hidden * up_pre * sig * (1.0 + gate_pre * (1.0 - sig))
        ).astype(BF16)

    sent_ref[...] = input_rows(
        d_gate_ref, d_up_ref, gate_ref, up_ref, side(1 - mine, width)
    ).astype(BF16)


def sum_kernel(d_gate_ref, d_up_ref, gate_ref, up_ref, got_ref, out_ref):
    columns = side(lax.axis_index("tensor"), out_ref.shape[1])
    own = input_rows(d_gate_ref, d_up_ref, gate_ref, up_ref, columns)
    out_ref[...] = (own + got_ref[...].astype(F32)).astype(BF16)


def last_sum_kernel(capacity, groups, *refs):
    *earlier_refs, d_gate_ref, d_up_ref, gate_ref, up_ref, got_ref = refs[:-3]
    out_ref, done_ref, sum_ref = refs[-3:]
    done_ref[...] = jnp.zeros_like(done_ref)
    me = lax.axis_index("expert")

    def put(rows_ref, group):
        for i, k in enumerate(group):
            there = pl.ds(pl.multiple_of((me ^ k) * capacity, capacity), capacity)
            out_ref[there, :] = rows_ref[i * capacity : (i + 1) * capacity, :]

    sum_kernel(d_gate_ref, d_up_ref, gate_ref, up_ref, got_ref, sum_ref)
    for rows_ref, group in zip((*earlier_refs, sum_ref), groups):
        put(rows_ref, group)


def grads_kernel(sizes, *refs):
    *ins, _, grad_gate_ref, grad_up_ref, grad_down_ref = refs
    mine = lax.axis_index("tensor")
    groups = [(*ins[5 * i : 5 * i + 5], rows) for i, rows in enumerate(sizes)]
    width = groups[0][0].shape[1]

    def total(left, half, second):
        return sum(
            jnp.dot(
                one[left][...],
                one[half][one[5] * second : one[5] * (second + 1), :],
                preferred_element_type=F32,
            )
            for one in groups
        ).astype(BF16)

    for half, which in enumerate((mine, 1 - mine)):
        grad_gate_ref[:, side(which, width)] = total(2, half, 0)
        grad_up_ref[:, side(which, width)] = total(3, half, 0)
        grad_down_ref[:, side(which, width)] = total(4, half, 1)


def combine_kernel(capacity, row_ref, back_hbm, out_ref, back_ref, sems):
    slots = back_ref.shape[0]
    step = slots // PIECES
    copies = [
        pltpu.make_async_copy(
            back_hbm.at[i * step : (i + 1) * step],
            back_ref.at[i * step : (i + 1) * step],
            sems.at[i],
        )
        for i in range(PIECES)
    ]
    for copy in copies:
        copy.start()
    route, within = rank_among_same(row_ref[...], 1)
    slot = lax.broadcasted_iota(jnp.int32, (out_ref.shape[0], slots), 1)
    placing = jnp.where(slot == route * capacity + within, 1.0, 0.0).astype(BF16)
    total = jnp.zeros(out_ref.shape, F32)
    for i, copy in enumerate(copies):
        copy.wait()
        total += jnp.dot(
            placing[:, i * step : (i + 1) * step],
            back_ref[i * step : (i + 1) * step],
            preferred_element_type=F32,
        )
    out_ref[...] = total.astype(BF16)


def params(limit):
    return pltpu.CompilerParams(vmem_limit_bytes=limit)


def cost(products, rows, hidden, features):
    return pl.CostEstimate(
        flops=2 * products * rows * hidden * features,
        bytes_accessed=2 * products * (hidden + rows) * features,
        transcendentals=0,
    )


def combine(capacity, ids_row, returned, tok_rows):
    slots, width = returned.shape
    return pl.pallas_call(
        functools.partial(combine_kernel, capacity),
        out_shape=jax.ShapeDtypeStruct((tok_rows, width), BF16),
        in_specs=[IN_VMEM, IN_HBM],
        out_specs=IN_VMEM,
        scratch_shapes=[pltpu.VMEM((slots, width), BF16), pltpu.SemaphoreType.DMA((PIECES,))],
        compiler_params=params(SMALL),
        name="combine",
    )(ids_row, returned)


def to_experts(rows, experts):
    return lax.all_to_all(
        rows.reshape(experts, rows.shape[0] // experts, rows.shape[1]),
        "expert",
        split_axis=0,
        concat_axis=0,
        tiled=True,
    ).reshape(rows.shape)


def grouped(tokens, upstream, expert_ids, gate_rows, up_rows, down_rows):
    experts = lax.axis_size("expert")
    tok_rows, width = tokens.shape
    units, features = gate_rows.shape
    capacity = max(2, 2 * tok_rows // experts)
    ids_row = expert_ids.reshape(1, tok_rows)
    tile = units // 2 if units % 32 == 0 else units

    far = [k for k in reversed(range(1, experts)) if k >= experts // 2]
    near = [k for k in reversed(range(1, experts)) if k < experts // 2]
    turns = [k for pair in zip(far, near) for k in pair] + far[len(near) :]
    cut = experts // 2
    first, second = turns[:cut], turns[cut:] + [0]

    slabs = list(
        pl.pallas_call(
            functools.partial(place_kernel, capacity),
            out_shape=[jax.ShapeDtypeStruct((2 * capacity, width), BF16)] * experts,
            in_specs=[IN_HBM] * 3,
            out_specs=[IN_HBM] * experts,
            scratch_shapes=[
                pltpu.VMEM((1, tok_rows), jnp.int32),
                pltpu.VMEM((tok_rows, width), BF16),
                pltpu.VMEM((tok_rows, width), BF16),
                pltpu.VMEM((2, experts * capacity, width), BF16),
                pltpu.SemaphoreType.DMA,
                pltpu.SemaphoreType.DMA((2, PIECES)),
                pltpu.SemaphoreType.DMA((2, experts)),
            ],
            compiler_params=params(LARGE),
            name="place",
        )(ids_row, tokens, upstream)
    )

    def swap(k):
        return lax.ppermute(slabs[k], "expert", [(e, e ^ k) for e in range(experts)])

    def exchange(values):
        return lax.ppermute(values, "tensor", [(0, 1), (1, 0)])

    def collect(arrived):
        return pl.pallas_call(
            functools.partial(collect_kernel, capacity, len(arrived)),
            out_shape=jax.ShapeDtypeStruct((2 * len(arrived) * capacity, width), BF16),
            in_specs=[IN_VMEM] * len(arrived),
            out_specs=IN_VMEM,
            compiler_params=params(SMALL),
            cost_estimate=cost(COLLECT, len(arrived) * capacity, units, features),
            name="collect",
        )(*arrived)

    def front(own):
        other = exchange(own)
        rows = own.shape[0] // 2
        hidden, d_gate, d_up, sent = pl.pallas_call(
            functools.partial(front_kernel, tile),
            out_shape=[jax.ShapeDtypeStruct((units, rows), BF16)] * 3
            + [jax.ShapeDtypeStruct((rows, width), BF16)],
            in_specs=[IN_VMEM] * 5,
            out_specs=[IN_VMEM] * 4,
            compiler_params=params(SMALL),
            cost_estimate=cost(4, rows, units, features),
            name="front",
        )(own, other, gate_rows, up_rows, down_rows)
        for_sum = (d_gate, d_up, gate_rows, up_rows, exchange(sent))
        return (own, other, d_gate, d_up, hidden), for_sum

    got = {k: swap(k) for k in turns}
    got[0] = slabs[0]
    for_grads_a, for_sum_a = front(collect([got[k] for k in first]))
    for_grads_b, for_sum_b = front(collect([got[k] for k in second]))
    sum_a = pl.pallas_call(
        sum_kernel,
        out_shape=jax.ShapeDtypeStruct((len(first) * capacity, width), BF16),
        in_specs=[IN_VMEM] * 5,
        out_specs=IN_VMEM,
        compiler_params=params(SMALL),
        cost_estimate=cost(1, len(first) * capacity, units, features),
        name="sum",
    )(*for_sum_a)
    totals, done = pl.pallas_call(
        functools.partial(last_sum_kernel, capacity, (first, second)),
        out_shape=[
            jax.ShapeDtypeStruct((experts * capacity, width), BF16),
            jax.ShapeDtypeStruct((8, 128), F32),
        ],
        in_specs=[IN_VMEM] * 6,
        out_specs=[IN_VMEM] * 2,
        scratch_shapes=[pltpu.VMEM((len(second) * capacity, width), BF16)],
        compiler_params=params(SMALL),
        cost_estimate=cost(1, len(second) * capacity, units, features),
        name="last_sum",
    )(sum_a, *for_sum_b)
    returned = to_experts(totals, experts)

    def grads_specs(rows):
        return [pl.BlockSpec((2 * rows, width), lambda i: (0, 0))] * 2 + [
            pl.BlockSpec((tile, rows), lambda i: (i, 0))
        ] * 3

    sizes = [len(group) * capacity for group in (first, second)]
    grads = pl.pallas_call(
        functools.partial(grads_kernel, sizes),
        grid=(units // tile,),
        out_shape=[jax.ShapeDtypeStruct((units, features), BF16)] * 3,
        in_specs=grads_specs(sizes[0])
        + grads_specs(sizes[1])
        + [pl.BlockSpec((8, 128), lambda i: (0, 0))],
        out_specs=[pl.BlockSpec((tile, features), lambda i: (i, 0))] * 3,
        compiler_params=params(2 * SMALL),
        cost_estimate=cost(3, sum(sizes), units, features),
        name="grads",
    )(*for_grads_a, *for_grads_b, done)
    return combine(capacity, ids_row, returned, tok_rows), grads


def rows_by_weights(rows, weights):
    return lax.dot_general(rows, weights, (((1,), (1,)), ((), ())), preferred_element_type=F32)


def weight_grad(left, right):
    return lax.dot_general(
        left, right, (((0,), (0,)), ((), ())), preferred_element_type=F32
    ).astype(BF16)


def general(tokens, upstream, expert_ids, gate_rows, up_rows, down_rows):
    experts = lax.axis_size("expert")
    tok_rows, width = tokens.shape
    capacity = max(2, 2 * tok_rows // experts)
    route = expert_ids[:, 0]
    onehot = (route[:, None] == jnp.arange(experts, dtype=jnp.int32)[None, :]).astype(jnp.int32)
    before = jnp.cumsum(onehot, axis=0) - onehot
    target = route * capacity + jnp.sum(before * onehot, axis=1)
    slot = jnp.arange(experts * capacity, dtype=jnp.int32)
    placing = (target[None, :] == slot[:, None]).astype(BF16)
    both = jnp.concatenate([tokens, upstream], axis=1)
    own = to_experts(jnp.dot(placing, both, preferred_element_type=F32).astype(BF16), experts)
    x_all = lax.all_gather(own[:, :width], "tensor", axis=1, tiled=True)
    dy_all = lax.all_gather(own[:, width:], "tensor", axis=1, tiled=True)
    gate_pre = rows_by_weights(x_all, gate_rows)
    up_pre = rows_by_weights(x_all, up_rows)
    d_hidden = rows_by_weights(dy_all, down_rows)
    sig = jax.nn.sigmoid(gate_pre)
    silu = gate_pre * sig
    hidden = (silu * up_pre).astype(BF16)
    d_up = (d_hidden * silu).astype(BF16)
    d_gate = (d_hidden * up_pre * sig * (1.0 + gate_pre * (1.0 - sig))).astype(BF16)
    partial = jnp.dot(d_gate, gate_rows, preferred_element_type=F32) + jnp.dot(
        d_up, up_rows, preferred_element_type=F32
    )
    totals = lax.psum_scatter(partial.astype(BF16), "tensor", scatter_dimension=1, tiled=True)
    returned = to_experts(totals, experts)
    grads = [weight_grad(d_gate, x_all), weight_grad(d_up, x_all), weight_grad(hidden, dy_all)]
    return weight_grad(placing, returned), grads


def on_device(tokens, upstream, expert_ids, w_gate, w_up, w_down):
    experts = lax.axis_size("expert")
    capacity = 2 * tokens.shape[0] // experts
    pairs = lax.axis_size("tensor") == 2 and experts & (experts - 1) == 0 and experts > 4
    run = grouped if pairs and capacity % 16 == 0 else general
    grad_tokens, grads = run(tokens, upstream, expert_ids, w_gate[0], w_up[0], w_down[0])
    return (grad_tokens, *(grad[None] for grad in grads))


def solution(mesh):
    rows = P("expert", "tensor")
    weights = P("expert", "tensor", None)
    return jax.shard_map(
        on_device,
        mesh=mesh,
        in_specs=(rows, rows, P("expert", None), weights, weights, weights),
        out_specs=(rows, weights, weights, weights),
        check_vma=False,
    )
```

```python
import functools

import jax
import jax.numpy as jnp
from jax import lax
from jax.experimental import pallas as pl
from jax.experimental.pallas import tpu as pltpu
from jax.sharding import PartitionSpec as P

F32 = jnp.float32
BF16 = jnp.bfloat16
SMALL = 16 * 2**20
LARGE = 56 * 2**20
PIECES = 4
COLLECT = 16
IN_VMEM = pl.BlockSpec(memory_space=pltpu.VMEM)
IN_HBM = pl.BlockSpec(memory_space=pltpu.HBM)


def rank_among_same(row, axis):
    rows = row.shape[1]
    down = lax.broadcasted_iota(jnp.int32, (rows, rows), 0)
    right = lax.broadcasted_iota(jnp.int32, (rows, rows), 1)
    col = jnp.sum(jnp.where(down == right, row, 0), axis=1, keepdims=True)
    earlier = down > right if axis else down < right
    same = jnp.where((col == row) & earlier, 1, 0)
    return (col if axis else row), jnp.sum(same, axis=axis, keepdims=True)


def place_kernel(capacity, row_hbm, x_hbm, dy_hbm, *refs):
    *slabs, row_ref, x_ref, dy_ref, placed_ref, row_sem, in_sems, out_sems = refs
    row_copy = pltpu.make_async_copy(row_hbm, row_ref, row_sem)
    row_copy.start()
    step = x_ref.shape[0] // PIECES
    copies = [
        [
            pltpu.make_async_copy(
                from_ref.at[i * step : (i + 1) * step],
                to_ref.at[i * step : (i + 1) * step],
                in_sems.at[which, i],
            )
            for i in range(PIECES)
        ]
        for which, (from_ref, to_ref) in enumerate(((x_hbm, x_ref), (dy_hbm, dy_ref)))
    ]
    for copy in copies[0] + copies[1]:
        copy.start()
    me = lax.axis_index("expert")
    row_copy.wait()
    route, within = rank_among_same(row_ref[...], 0)
    slots = len(slabs) * capacity
    slot = lax.broadcasted_iota(jnp.int32, (slots, x_ref.shape[0]), 0)
    placing = jnp.where(slot == (route ^ me) * capacity + within, 1.0, 0.0).astype(BF16)
    out_copies = []
    for i, ref in enumerate((x_ref, dy_ref)):
        for copy in copies[i]:
            copy.wait()
        placed_ref[i] = jnp.dot(placing, ref[...], preferred_element_type=F32).astype(BF16)
        for k, slab in enumerate(slabs):
            out_copies.append(
                pltpu.make_async_copy(
                    placed_ref.at[i, k * capacity : (k + 1) * capacity],
                    slab.at[i * capacity : (i + 1) * capacity],
                    out_sems.at[i, k],
                )
            )
            out_copies[-1].start()
    for copy in out_copies:
        copy.wait()


def collect_kernel(capacity, count, *refs):
    slabs, out_ref = refs[:count], refs[-1]
    half = len(slabs) * capacity
    for i, slab in enumerate(slabs):
        out_ref[i * capacity : (i + 1) * capacity, :] = slab[:capacity, :]
        out_ref[half + i * capacity : half + (i + 1) * capacity, :] = slab[capacity:, :]


def side(which, width):
    return pl.ds(pl.multiple_of(which * width, width), width)


def input_rows(d_gate_ref, d_up_ref, gate_ref, up_ref, columns):
    over_hidden = (((0,), (0,)), ((), ()))
    return lax.dot_general(
        d_gate_ref[...], gate_ref[:, columns], over_hidden, preferred_element_type=F32
    ) + lax.dot_general(
        d_up_ref[...], up_ref[:, columns], over_hidden, preferred_element_type=F32
    )


def front_kernel(
    tile, own_ref, other_ref, gate_ref, up_ref, down_ref, hidden_ref, d_gate_ref, d_up_ref, sent_ref
):
    rows, width = sent_ref.shape
    mine = lax.axis_index("tensor")
    over_features = (((1,), (1,)), ((), ()))

    @pl.loop(0, hidden_ref.shape[0] // tile)
    def _(step):
        units = pl.ds(pl.multiple_of(step * tile, tile), tile)

        def product(weight_ref, start):
            return sum(
                lax.dot_general(
                    weight_ref[units, side(which, width)],
                    half_ref[start : start + rows, :],
                    over_features,
                    preferred_element_type=F32,
                )
                for which, half_ref in ((mine, own_ref), (1 - mine, other_ref))
            )

        gate_pre = product(gate_ref, 0)
        up_pre = product(up_ref, 0)
        d_hidden = product(down_ref, rows)
        sig = jax.nn.sigmoid(gate_pre)
        silu = gate_pre * sig
        hidden_ref[units, :] = (silu * up_pre).astype(BF16)
        d_up_ref[units, :] = (d_hidden * silu).astype(BF16)
        d_gate_ref[units, :] = (
            d_hidden * up_pre * sig * (1.0 + gate_pre * (1.0 - sig))
        ).astype(BF16)

    sent_ref[...] = input_rows(
        d_gate_ref, d_up_ref, gate_ref, up_ref, side(1 - mine, width)
    ).astype(BF16)


def kept_kernel(d_gate_ref, d_up_ref, gate_ref, up_ref, out_ref):
    columns = side(lax.axis_index("tensor"), out_ref.shape[1])
    out_ref[...] = input_rows(d_gate_ref, d_up_ref, gate_ref, up_ref, columns)


def sum_kernel(kept_ref, got_ref, out_ref):
    out_ref[...] = (kept_ref[...] + got_ref[...].astype(F32)).astype(BF16)


def last_sum_kernel(capacity, groups, sum_ref, kept_ref, got_ref, out_ref, done_ref):
    done_ref[...] = jnp.zeros_like(done_ref)
    me = lax.axis_index("expert")
    for last, group in enumerate(groups):
        for i, k in enumerate(group):
            here = slice(i * capacity, (i + 1) * capacity)
            there = pl.ds(pl.multiple_of((me ^ k) * capacity, capacity), capacity)
            if last:
                both = kept_ref[here, :] + got_ref[here, :].astype(F32)
                out_ref[there, :] = both.astype(BF16)
            else:
                out_ref[there, :] = sum_ref[here, :]


def grads_kernel(sizes, *refs):
    *ins, _, grad_gate_ref, grad_up_ref, grad_down_ref = refs
    mine = lax.axis_index("tensor")
    groups = [(*ins[5 * i : 5 * i + 5], rows) for i, rows in enumerate(sizes)]
    width = groups[0][0].shape[1]

    def total(left, half, second):
        return sum(
            jnp.dot(
                one[left][...],
                one[half][one[5] * second : one[5] * (second + 1), :],
                preferred_element_type=F32,
            )
            for one in groups
        ).astype(BF16)

    for half, which in enumerate((mine, 1 - mine)):
        grad_gate_ref[:, side(which, width)] = total(2, half, 0)
        grad_up_ref[:, side(which, width)] = total(3, half, 0)
        grad_down_ref[:, side(which, width)] = total(4, half, 1)


def combine_kernel(capacity, row_ref, back_hbm, out_ref, back_ref, sems):
    slots = back_ref.shape[0]
    step = slots // PIECES
    copies = [
        pltpu.make_async_copy(
            back_hbm.at[i * step : (i + 1) * step],
            back_ref.at[i * step : (i + 1) * step],
            sems.at[i],
        )
        for i in range(PIECES)
    ]
    for copy in copies:
        copy.start()
    route, within = rank_among_same(row_ref[...], 1)
    slot = lax.broadcasted_iota(jnp.int32, (out_ref.shape[0], slots), 1)
    placing = jnp.where(slot == route * capacity + within, 1.0, 0.0).astype(BF16)
    total = jnp.zeros(out_ref.shape, F32)
    for i, copy in enumerate(copies):
        copy.wait()
        total += jnp.dot(
            placing[:, i * step : (i + 1) * step],
            back_ref[i * step : (i + 1) * step],
            preferred_element_type=F32,
        )
    out_ref[...] = total.astype(BF16)


def params(limit):
    return pltpu.CompilerParams(vmem_limit_bytes=limit)


def cost(products, rows, hidden, features):
    return pl.CostEstimate(
        flops=2 * products * rows * hidden * features,
        bytes_accessed=2 * products * (hidden + rows) * features,
        transcendentals=0,
    )


def combine(capacity, ids_row, returned, tok_rows):
    slots, width = returned.shape
    return pl.pallas_call(
        functools.partial(combine_kernel, capacity),
        out_shape=jax.ShapeDtypeStruct((tok_rows, width), BF16),
        in_specs=[IN_VMEM, IN_HBM],
        out_specs=IN_VMEM,
        scratch_shapes=[pltpu.VMEM((slots, width), BF16), pltpu.SemaphoreType.DMA((PIECES,))],
        compiler_params=params(SMALL),
        name="combine",
    )(ids_row, returned)


def to_experts(rows, experts):
    return lax.all_to_all(
        rows.reshape(experts, rows.shape[0] // experts, rows.shape[1]),
        "expert",
        split_axis=0,
        concat_axis=0,
        tiled=True,
    ).reshape(rows.shape)


def grouped(tokens, upstream, expert_ids, gate_rows, up_rows, down_rows):
    experts = lax.axis_size("expert")
    tok_rows, width = tokens.shape
    units, features = gate_rows.shape
    capacity = max(2, 2 * tok_rows // experts)
    ids_row = expert_ids.reshape(1, tok_rows)
    tile = units // 2 if units % 32 == 0 else units

    far = [k for k in reversed(range(1, experts)) if k >= experts // 2]
    near = [k for k in reversed(range(1, experts)) if k < experts // 2]
    turns = [k for pair in zip(far, near) for k in pair] + far[len(near) :]
    cut = 3 * experts // 4
    first, second = turns[:cut], turns[cut:] + [0]

    slabs = list(
        pl.pallas_call(
            functools.partial(place_kernel, capacity),
            out_shape=[jax.ShapeDtypeStruct((2 * capacity, width), BF16)] * experts,
            in_specs=[IN_HBM] * 3,
            out_specs=[IN_HBM] * experts,
            scratch_shapes=[
                pltpu.VMEM((1, tok_rows), jnp.int32),
                pltpu.VMEM((tok_rows, width), BF16),
                pltpu.VMEM((tok_rows, width), BF16),
                pltpu.VMEM((2, experts * capacity, width), BF16),
                pltpu.SemaphoreType.DMA,
                pltpu.SemaphoreType.DMA((2, PIECES)),
                pltpu.SemaphoreType.DMA((2, experts)),
            ],
            compiler_params=params(LARGE),
            name="place",
        )(ids_row, tokens, upstream)
    )

    def swap(k):
        return lax.ppermute(slabs[k], "expert", [(e, e ^ k) for e in range(experts)])

    def exchange(values):
        return lax.ppermute(values, "tensor", [(0, 1), (1, 0)])

    def collect(arrived, after):
        return pl.pallas_call(
            functools.partial(collect_kernel, capacity, len(arrived)),
            out_shape=jax.ShapeDtypeStruct((2 * len(arrived) * capacity, width), BF16),
            in_specs=[IN_VMEM] * (len(arrived) + len(after)),
            out_specs=IN_VMEM,
            compiler_params=params(SMALL),
            cost_estimate=cost(COLLECT, len(arrived) * capacity, units, features),
            name="collect",
        )(*arrived, *after)

    def front(own):
        other = exchange(own)
        rows = own.shape[0] // 2
        hidden, d_gate, d_up, sent = pl.pallas_call(
            functools.partial(front_kernel, tile),
            out_shape=[jax.ShapeDtypeStruct((units, rows), BF16)] * 3
            + [jax.ShapeDtypeStruct((rows, width), BF16)],
            in_specs=[IN_VMEM] * 5,
            out_specs=[IN_VMEM] * 4,
            compiler_params=params(SMALL),
            cost_estimate=cost(4, rows, units, features),
            name="front",
        )(own, other, gate_rows, up_rows, down_rows)
        kept = pl.pallas_call(
            kept_kernel,
            out_shape=jax.ShapeDtypeStruct((rows, width), F32),
            in_specs=[IN_VMEM] * 4,
            out_specs=IN_VMEM,
            compiler_params=params(SMALL),
            cost_estimate=cost(1, rows, units, features),
            name="kept",
        )(d_gate, d_up, gate_rows, up_rows)
        return (own, other, d_gate, d_up, hidden), (kept, exchange(sent))

    got = {k: swap(k) for k in turns}
    got[0] = slabs[0]
    for_grads_a, for_sum_a = front(collect([got[k] for k in first], []))
    for_grads_b, for_sum_b = front(collect([got[k] for k in second], for_sum_a[:1]))
    sum_a = pl.pallas_call(
        sum_kernel,
        out_shape=jax.ShapeDtypeStruct((len(first) * capacity, width), BF16),
        in_specs=[IN_VMEM] * 2,
        out_specs=IN_VMEM,
        compiler_params=params(SMALL),
        name="sum",
    )(*for_sum_a)
    totals, done = pl.pallas_call(
        functools.partial(last_sum_kernel, capacity, (first, second)),
        out_shape=[
            jax.ShapeDtypeStruct((experts * capacity, width), BF16),
            jax.ShapeDtypeStruct((8, 128), F32),
        ],
        in_specs=[IN_VMEM] * 3,
        out_specs=[IN_VMEM] * 2,
        compiler_params=params(SMALL),
        name="last_sum",
    )(sum_a, *for_sum_b)
    returned = to_experts(totals, experts)

    def grads_specs(rows):
        return [pl.BlockSpec((2 * rows, width), lambda i: (0, 0))] * 2 + [
            pl.BlockSpec((tile, rows), lambda i: (i, 0))
        ] * 3

    sizes = [len(group) * capacity for group in (first, second)]
    grads = pl.pallas_call(
        functools.partial(grads_kernel, sizes),
        grid=(units // tile,),
        out_shape=[jax.ShapeDtypeStruct((units, features), BF16)] * 3,
        in_specs=grads_specs(sizes[0])
        + grads_specs(sizes[1])
        + [pl.BlockSpec((8, 128), lambda i: (0, 0))],
        out_specs=[pl.BlockSpec((tile, features), lambda i: (i, 0))] * 3,
        compiler_params=params(2 * SMALL),
        cost_estimate=cost(3, sum(sizes), units, features),
        name="grads",
    )(*for_grads_a, *for_grads_b, done)
    return combine(capacity, ids_row, returned, tok_rows), grads


def rows_by_weights(rows, weights):
    return lax.dot_general(rows, weights, (((1,), (1,)), ((), ())), preferred_element_type=F32)


def weight_grad(left, right):
    return lax.dot_general(
        left, right, (((0,), (0,)), ((), ())), preferred_element_type=F32
    ).astype(BF16)


def general(tokens, upstream, expert_ids, gate_rows, up_rows, down_rows):
    experts = lax.axis_size("expert")
    tok_rows, width = tokens.shape
    capacity = max(2, 2 * tok_rows // experts)
    route = expert_ids[:, 0]
    onehot = (route[:, None] == jnp.arange(experts, dtype=jnp.int32)[None, :]).astype(jnp.int32)
    before = jnp.cumsum(onehot, axis=0) - onehot
    target = route * capacity + jnp.sum(before * onehot, axis=1)
    slot = jnp.arange(experts * capacity, dtype=jnp.int32)
    placing = (target[None, :] == slot[:, None]).astype(BF16)
    both = jnp.concatenate([tokens, upstream], axis=1)
    own = to_experts(jnp.dot(placing, both, preferred_element_type=F32).astype(BF16), experts)
    x_all = lax.all_gather(own[:, :width], "tensor", axis=1, tiled=True)
    dy_all = lax.all_gather(own[:, width:], "tensor", axis=1, tiled=True)
    gate_pre = rows_by_weights(x_all, gate_rows)
    up_pre = rows_by_weights(x_all, up_rows)
    d_hidden = rows_by_weights(dy_all, down_rows)
    sig = jax.nn.sigmoid(gate_pre)
    silu = gate_pre * sig
    hidden = (silu * up_pre).astype(BF16)
    d_up = (d_hidden * silu).astype(BF16)
    d_gate = (d_hidden * up_pre * sig * (1.0 + gate_pre * (1.0 - sig))).astype(BF16)
    partial = jnp.dot(d_gate, gate_rows, preferred_element_type=F32) + jnp.dot(
        d_up, up_rows, preferred_element_type=F32
    )
    totals = lax.psum_scatter(partial.astype(BF16), "tensor", scatter_dimension=1, tiled=True)
    returned = to_experts(totals, experts)
    grads = [weight_grad(d_gate, x_all), weight_grad(d_up, x_all), weight_grad(hidden, dy_all)]
    return weight_grad(placing, returned), grads


def on_device(tokens, upstream, expert_ids, w_gate, w_up, w_down):
    experts = lax.axis_size("expert")
    capacity = 2 * tokens.shape[0] // experts
    pairs = lax.axis_size("tensor") == 2 and experts & (experts - 1) == 0 and experts > 4
    run = grouped if pairs and capacity % 16 == 0 else general
    grad_tokens, grads = run(tokens, upstream, expert_ids, w_gate[0], w_up[0], w_down[0])
    return (grad_tokens, *(grad[None] for grad in grads))


def solution(mesh):
    rows = P("expert", "tensor")
    weights = P("expert", "tensor", None)
    return jax.shard_map(
        on_device,
        mesh=mesh,
        in_specs=(rows, rows, P("expert", None), weights, weights, weights),
        out_specs=(rows, weights, weights, weights),
        check_vma=False,
    )
```

```python
import functools

import jax
import jax.numpy as jnp
from jax import lax
from jax.experimental import pallas as pl
from jax.experimental.pallas import tpu as pltpu
from jax.sharding import PartitionSpec as P

F32 = jnp.float32
BF16 = jnp.bfloat16
SMALL = 16 * 2**20
LARGE = 56 * 2**20
PIECES = 4
COLLECT = 16
IN_VMEM = pl.BlockSpec(memory_space=pltpu.VMEM)
IN_HBM = pl.BlockSpec(memory_space=pltpu.HBM)


def rank_among_same(row, axis):
    rows = row.shape[1]
    down = lax.broadcasted_iota(jnp.int32, (rows, rows), 0)
    right = lax.broadcasted_iota(jnp.int32, (rows, rows), 1)
    col = jnp.sum(jnp.where(down == right, row, 0), axis=1, keepdims=True)
    earlier = down > right if axis else down < right
    same = jnp.where((col == row) & earlier, 1, 0)
    return (col if axis else row), jnp.sum(same, axis=axis, keepdims=True)


def place_kernel(capacity, row_hbm, x_hbm, dy_hbm, *refs):
    *slabs, row_ref, x_ref, dy_ref, placed_ref, row_sem, in_sems, out_sems = refs
    row_copy = pltpu.make_async_copy(row_hbm, row_ref, row_sem)
    row_copy.start()
    step = x_ref.shape[0] // PIECES
    copies = [
        [
            pltpu.make_async_copy(
                from_ref.at[i * step : (i + 1) * step],
                to_ref.at[i * step : (i + 1) * step],
                in_sems.at[which, i],
            )
            for i in range(PIECES)
        ]
        for which, (from_ref, to_ref) in enumerate(((x_hbm, x_ref), (dy_hbm, dy_ref)))
    ]
    for copy in copies[0] + copies[1]:
        copy.start()
    me = lax.axis_index("expert")
    row_copy.wait()
    route, within = rank_among_same(row_ref[...], 0)
    slots = len(slabs) * capacity
    slot = lax.broadcasted_iota(jnp.int32, (slots, x_ref.shape[0]), 0)
    placing = jnp.where(slot == (route ^ me) * capacity + within, 1.0, 0.0).astype(BF16)
    out_copies = []
    for i, ref in enumerate((x_ref, dy_ref)):
        for copy in copies[i]:
            copy.wait()
        placed_ref[i] = jnp.dot(placing, ref[...], preferred_element_type=F32).astype(BF16)
        for k, slab in enumerate(slabs):
            out_copies.append(
                pltpu.make_async_copy(
                    placed_ref.at[i, k * capacity : (k + 1) * capacity],
                    slab.at[i * capacity : (i + 1) * capacity],
                    out_sems.at[i, k],
                )
            )
            out_copies[-1].start()
    for copy in out_copies:
        copy.wait()


def collect_kernel(capacity, count, *refs):
    slabs, out_ref = refs[:count], refs[-1]
    half = len(slabs) * capacity
    for i, slab in enumerate(slabs):
        out_ref[i * capacity : (i + 1) * capacity, :] = slab[:capacity, :]
        out_ref[half + i * capacity : half + (i + 1) * capacity, :] = slab[capacity:, :]


def side(which, width):
    return pl.ds(pl.multiple_of(which * width, width), width)


def input_rows(d_gate_ref, d_up_ref, gate_ref, up_ref, columns):
    over_hidden = (((0,), (0,)), ((), ()))
    return lax.dot_general(
        d_gate_ref[...], gate_ref[:, columns], over_hidden, preferred_element_type=F32
    ) + lax.dot_general(
        d_up_ref[...], up_ref[:, columns], over_hidden, preferred_element_type=F32
    )


OVER_FEATURES = (((1,), (1,)), ((), ()))


def begin_kernel(tile, own_ref, gate_ref, up_ref, down_ref, *out_refs):
    rows, width = out_refs[0].shape[1], own_ref.shape[1]
    columns = side(lax.axis_index("tensor"), width)

    @pl.loop(0, gate_ref.shape[0] // tile)
    def _(step):
        units = pl.ds(pl.multiple_of(step * tile, tile), tile)
        for weight_ref, out_ref, start in zip(
            (gate_ref, up_ref, down_ref), out_refs, (0, 0, rows)
        ):
            out_ref[units, :] = lax.dot_general(
                weight_ref[units, columns],
                own_ref[start : start + rows, :],
                OVER_FEATURES,
                preferred_element_type=F32,
            )


def front_kernel(tile, own_ref, other_ref, gate_ref, up_ref, down_ref, *refs):
    *begun_refs, hidden_ref, d_gate_ref, d_up_ref, sent_ref = refs
    rows, width = sent_ref.shape
    mine = lax.axis_index("tensor")

    @pl.loop(0, hidden_ref.shape[0] // tile)
    def _(step):
        units = pl.ds(pl.multiple_of(step * tile, tile), tile)

        def product(which, weight_ref, start):
            def share(half_ref, half):
                return lax.dot_general(
                    weight_ref[units, side(half, width)],
                    half_ref[start : start + rows, :],
                    OVER_FEATURES,
                    preferred_element_type=F32,
                )

            own = begun_refs[which][units, :] if begun_refs else share(own_ref, mine)
            return own + share(other_ref, 1 - mine)

        gate_pre = product(0, gate_ref, 0)
        up_pre = product(1, up_ref, 0)
        d_hidden = product(2, down_ref, rows)
        sig = jax.nn.sigmoid(gate_pre)
        silu = gate_pre * sig
        hidden_ref[units, :] = (silu * up_pre).astype(BF16)
        d_up_ref[units, :] = (d_hidden * silu).astype(BF16)
        d_gate_ref[units, :] = (
            d_hidden * up_pre * sig * (1.0 + gate_pre * (1.0 - sig))
        ).astype(BF16)

    sent_ref[...] = input_rows(
        d_gate_ref, d_up_ref, gate_ref, up_ref, side(1 - mine, width)
    ).astype(BF16)


def kept_kernel(d_gate_ref, d_up_ref, gate_ref, up_ref, out_ref):
    columns = side(lax.axis_index("tensor"), out_ref.shape[1])
    out_ref[...] = input_rows(d_gate_ref, d_up_ref, gate_ref, up_ref, columns)


def sum_kernel(kept_ref, got_ref, out_ref):
    out_ref[...] = (kept_ref[...] + got_ref[...].astype(F32)).astype(BF16)


def last_sum_kernel(capacity, groups, sum_ref, kept_ref, got_ref, out_ref, done_ref):
    done_ref[...] = jnp.zeros_like(done_ref)
    me = lax.axis_index("expert")
    for last, group in enumerate(groups):
        for i, k in enumerate(group):
            here = slice(i * capacity, (i + 1) * capacity)
            there = pl.ds(pl.multiple_of((me ^ k) * capacity, capacity), capacity)
            if last:
                both = kept_ref[here, :] + got_ref[here, :].astype(F32)
                out_ref[there, :] = both.astype(BF16)
            else:
                out_ref[there, :] = sum_ref[here, :]


def grads_kernel(sizes, *refs):
    *ins, _, grad_gate_ref, grad_up_ref, grad_down_ref = refs
    mine = lax.axis_index("tensor")
    groups = [(*ins[5 * i : 5 * i + 5], rows) for i, rows in enumerate(sizes)]
    width = groups[0][0].shape[1]

    def total(left, half, second):
        return sum(
            jnp.dot(
                one[left][...],
                one[half][one[5] * second : one[5] * (second + 1), :],
                preferred_element_type=F32,
            )
            for one in groups
        ).astype(BF16)

    for half, which in enumerate((mine, 1 - mine)):
        grad_gate_ref[:, side(which, width)] = total(2, half, 0)
        grad_up_ref[:, side(which, width)] = total(3, half, 0)
        grad_down_ref[:, side(which, width)] = total(4, half, 1)


def placing_kernel(capacity, row_ref, _, placing_ref):
    route, within = rank_among_same(row_ref[...], 1)
    slot = lax.broadcasted_iota(jnp.int32, placing_ref.shape, 1)
    placing_ref[...] = jnp.where(slot == route * capacity + within, 1.0, 0.0).astype(BF16)


def combine_kernel(placing_ref, back_hbm, out_ref, back_ref, sems):
    step = back_ref.shape[0] // PIECES
    copies = [
        pltpu.make_async_copy(
            back_hbm.at[i * step : (i + 1) * step],
            back_ref.at[i * step : (i + 1) * step],
            sems.at[i],
        )
        for i in range(PIECES)
    ]
    for copy in copies:
        copy.start()
    total = jnp.zeros(out_ref.shape, F32)
    for i, copy in enumerate(copies):
        copy.wait()
        total += jnp.dot(
            placing_ref[:, i * step : (i + 1) * step],
            back_ref[i * step : (i + 1) * step],
            preferred_element_type=F32,
        )
    out_ref[...] = total.astype(BF16)


def params(limit):
    return pltpu.CompilerParams(vmem_limit_bytes=limit)


def cost(products, rows, hidden, features):
    return pl.CostEstimate(
        flops=2 * products * rows * hidden * features,
        bytes_accessed=2 * products * (hidden + rows) * features,
        transcendentals=0,
    )


def placing_of(capacity, ids_row, slots, after):
    return pl.pallas_call(
        functools.partial(placing_kernel, capacity),
        out_shape=jax.ShapeDtypeStruct((ids_row.shape[1], slots), BF16),
        in_specs=[IN_VMEM] * 2,
        out_specs=IN_VMEM,
        compiler_params=params(SMALL),
        name="placing",
    )(ids_row, after)


def combine(placing, returned):
    slots, width = returned.shape
    return pl.pallas_call(
        combine_kernel,
        out_shape=jax.ShapeDtypeStruct((placing.shape[0], width), BF16),
        in_specs=[IN_VMEM, IN_HBM],
        out_specs=IN_VMEM,
        scratch_shapes=[pltpu.VMEM((slots, width), BF16), pltpu.SemaphoreType.DMA((PIECES,))],
        compiler_params=params(SMALL),
        name="combine",
    )(placing, returned)


def to_experts(rows, experts):
    return lax.all_to_all(
        rows.reshape(experts, rows.shape[0] // experts, rows.shape[1]),
        "expert",
        split_axis=0,
        concat_axis=0,
        tiled=True,
    ).reshape(rows.shape)


def grouped(tokens, upstream, expert_ids, gate_rows, up_rows, down_rows):
    experts = lax.axis_size("expert")
    tok_rows, width = tokens.shape
    units, features = gate_rows.shape
    capacity = max(2, 2 * tok_rows // experts)
    ids_row = expert_ids.reshape(1, tok_rows)
    tile = units // 2 if units % 32 == 0 else units

    far = [k for k in reversed(range(1, experts)) if k >= experts // 2]
    near = [k for k in reversed(range(1, experts)) if k < experts // 2]
    turns = [k for pair in zip(far, near) for k in pair] + far[len(near) :]
    cut = 3 * experts // 4
    first, second = turns[:cut], turns[cut:] + [0]

    slabs = list(
        pl.pallas_call(
            functools.partial(place_kernel, capacity),
            out_shape=[jax.ShapeDtypeStruct((2 * capacity, width), BF16)] * experts,
            in_specs=[IN_HBM] * 3,
            out_specs=[IN_HBM] * experts,
            scratch_shapes=[
                pltpu.VMEM((1, tok_rows), jnp.int32),
                pltpu.VMEM((tok_rows, width), BF16),
                pltpu.VMEM((tok_rows, width), BF16),
                pltpu.VMEM((2, experts * capacity, width), BF16),
                pltpu.SemaphoreType.DMA,
                pltpu.SemaphoreType.DMA((2, PIECES)),
                pltpu.SemaphoreType.DMA((2, experts)),
            ],
            compiler_params=params(LARGE),
            name="place",
        )(ids_row, tokens, upstream)
    )

    def swap(k):
        return lax.ppermute(slabs[k], "expert", [(e, e ^ k) for e in range(experts)])

    def exchange(values):
        return lax.ppermute(values, "tensor", [(0, 1), (1, 0)])

    def collect(arrived, after):
        return pl.pallas_call(
            functools.partial(collect_kernel, capacity, len(arrived)),
            out_shape=jax.ShapeDtypeStruct((2 * len(arrived) * capacity, width), BF16),
            in_specs=[IN_VMEM] * (len(arrived) + len(after)),
            out_specs=IN_VMEM,
            compiler_params=params(SMALL),
            cost_estimate=cost(COLLECT, len(arrived) * capacity, units, features),
            name="collect",
        )(*arrived, *after)

    def begin(own):
        rows = own.shape[0] // 2
        return pl.pallas_call(
            functools.partial(begin_kernel, tile),
            out_shape=[jax.ShapeDtypeStruct((units, rows), F32)] * 3,
            in_specs=[IN_VMEM] * 4,
            out_specs=[IN_VMEM] * 3,
            compiler_params=params(SMALL),
            cost_estimate=cost(2, rows, units, features),
            name="begin",
        )(own, gate_rows, up_rows, down_rows)

    def front(own, begun):
        other = exchange(own)
        rows = own.shape[0] // 2
        hidden, d_gate, d_up, sent = pl.pallas_call(
            functools.partial(front_kernel, tile),
            out_shape=[jax.ShapeDtypeStruct((units, rows), BF16)] * 3
            + [jax.ShapeDtypeStruct((rows, width), BF16)],
            in_specs=[IN_VMEM] * (5 + len(begun)),
            out_specs=[IN_VMEM] * 4,
            compiler_params=params(SMALL),
            cost_estimate=cost(4, rows, units, features),
            name="front",
        )(own, other, gate_rows, up_rows, down_rows, *begun)
        kept = pl.pallas_call(
            kept_kernel,
            out_shape=jax.ShapeDtypeStruct((rows, width), F32),
            in_specs=[IN_VMEM] * 4,
            out_specs=IN_VMEM,
            compiler_params=params(SMALL),
            cost_estimate=cost(1, rows, units, features),
            name="kept",
        )(d_gate, d_up, gate_rows, up_rows)
        return (own, other, d_gate, d_up, hidden), (kept, exchange(sent))

    got = {k: swap(k) for k in turns}
    got[0] = slabs[0]
    for_grads_a, for_sum_a = front(collect([got[k] for k in first], []), [])
    own_b = collect([got[k] for k in second], for_sum_a[:1])
    for_grads_b, for_sum_b = front(own_b, begin(own_b))
    sum_a = pl.pallas_call(
        sum_kernel,
        out_shape=jax.ShapeDtypeStruct((len(first) * capacity, width), BF16),
        in_specs=[IN_VMEM] * 2,
        out_specs=IN_VMEM,
        compiler_params=params(SMALL),
        name="sum",
    )(*for_sum_a)
    totals, done = pl.pallas_call(
        functools.partial(last_sum_kernel, capacity, (first, second)),
        out_shape=[
            jax.ShapeDtypeStruct((experts * capacity, width), BF16),
            jax.ShapeDtypeStruct((8, 128), F32),
        ],
        in_specs=[IN_VMEM] * 3,
        out_specs=[IN_VMEM] * 2,
        compiler_params=params(SMALL),
        name="last_sum",
    )(sum_a, *for_sum_b)
    returned = to_experts(totals, experts)
    placing = placing_of(capacity, ids_row, experts * capacity, done)

    def grads_specs(rows):
        return [pl.BlockSpec((2 * rows, width), lambda i: (0, 0))] * 2 + [
            pl.BlockSpec((tile, rows), lambda i: (i, 0))
        ] * 3

    sizes = [len(group) * capacity for group in (first, second)]
    grads = pl.pallas_call(
        functools.partial(grads_kernel, sizes),
        grid=(units // tile,),
        out_shape=[jax.ShapeDtypeStruct((units, features), BF16)] * 3,
        in_specs=grads_specs(sizes[0])
        + grads_specs(sizes[1])
        + [pl.BlockSpec(placing.shape, lambda i: (0, 0))],
        out_specs=[pl.BlockSpec((tile, features), lambda i: (i, 0))] * 3,
        compiler_params=params(2 * SMALL),
        cost_estimate=cost(3, sum(sizes), units, features),
        name="grads",
    )(*for_grads_a, *for_grads_b, placing)
    return combine(placing, returned), grads


def rows_by_weights(rows, weights):
    return lax.dot_general(rows, weights, (((1,), (1,)), ((), ())), preferred_element_type=F32)


def weight_grad(left, right):
    return lax.dot_general(
        left, right, (((0,), (0,)), ((), ())), preferred_element_type=F32
    ).astype(BF16)


def general(tokens, upstream, expert_ids, gate_rows, up_rows, down_rows):
    experts = lax.axis_size("expert")
    tok_rows, width = tokens.shape
    capacity = max(2, 2 * tok_rows // experts)
    route = expert_ids[:, 0]
    onehot = (route[:, None] == jnp.arange(experts, dtype=jnp.int32)[None, :]).astype(jnp.int32)
    before = jnp.cumsum(onehot, axis=0) - onehot
    target = route * capacity + jnp.sum(before * onehot, axis=1)
    slot = jnp.arange(experts * capacity, dtype=jnp.int32)
    placing = (target[None, :] == slot[:, None]).astype(BF16)
    both = jnp.concatenate([tokens, upstream], axis=1)
    own = to_experts(jnp.dot(placing, both, preferred_element_type=F32).astype(BF16), experts)
    x_all = lax.all_gather(own[:, :width], "tensor", axis=1, tiled=True)
    dy_all = lax.all_gather(own[:, width:], "tensor", axis=1, tiled=True)
    gate_pre = rows_by_weights(x_all, gate_rows)
    up_pre = rows_by_weights(x_all, up_rows)
    d_hidden = rows_by_weights(dy_all, down_rows)
    sig = jax.nn.sigmoid(gate_pre)
    silu = gate_pre * sig
    hidden = (silu * up_pre).astype(BF16)
    d_up = (d_hidden * silu).astype(BF16)
    d_gate = (d_hidden * up_pre * sig * (1.0 + gate_pre * (1.0 - sig))).astype(BF16)
    partial = jnp.dot(d_gate, gate_rows, preferred_element_type=F32) + jnp.dot(
        d_up, up_rows, preferred_element_type=F32
    )
    totals = lax.psum_scatter(partial.astype(BF16), "tensor", scatter_dimension=1, tiled=True)
    returned = to_experts(totals, experts)
    grads = [weight_grad(d_gate, x_all), weight_grad(d_up, x_all), weight_grad(hidden, dy_all)]
    return weight_grad(placing, returned), grads


def on_device(tokens, upstream, expert_ids, w_gate, w_up, w_down):
    experts = lax.axis_size("expert")
    capacity = 2 * tokens.shape[0] // experts
    pairs = lax.axis_size("tensor") == 2 and experts & (experts - 1) == 0 and experts > 4
    run = grouped if pairs and capacity % 16 == 0 else general
    grad_tokens, grads = run(tokens, upstream, expert_ids, w_gate[0], w_up[0], w_down[0])
    return (grad_tokens, *(grad[None] for grad in grads))


def solution(mesh):
    rows = P("expert", "tensor")
    weights = P("expert", "tensor", None)
    return jax.shard_map(
        on_device,
        mesh=mesh,
        in_specs=(rows, rows, P("expert", None), weights, weights, weights),
        out_specs=(rows, weights, weights, weights),
        check_vma=False,
    )
```

```python
import functools

import jax
import jax.numpy as jnp
from jax import lax
from jax.experimental import pallas as pl
from jax.experimental.pallas import tpu as pltpu
from jax.sharding import PartitionSpec as P

F32 = jnp.float32
BF16 = jnp.bfloat16
SMALL = 16 * 2**20
LARGE = 56 * 2**20
PIECES = 4
COLLECT = 16
IN_VMEM = pl.BlockSpec(memory_space=pltpu.VMEM)
IN_HBM = pl.BlockSpec(memory_space=pltpu.HBM)


def rank_among_same(row, axis):
    rows = row.shape[1]
    down = lax.broadcasted_iota(jnp.int32, (rows, rows), 0)
    right = lax.broadcasted_iota(jnp.int32, (rows, rows), 1)
    col = jnp.sum(jnp.where(down == right, row, 0), axis=1, keepdims=True)
    earlier = down > right if axis else down < right
    same = jnp.where((col == row) & earlier, 1, 0)
    return (col if axis else row), jnp.sum(same, axis=axis, keepdims=True)


def place_kernel(capacity, row_hbm, x_hbm, dy_hbm, *refs):
    *slabs, row_ref, x_ref, dy_ref, placed_ref, row_sem, in_sems, out_sems = refs
    row_copy = pltpu.make_async_copy(row_hbm, row_ref, row_sem)
    row_copy.start()
    step = x_ref.shape[0] // PIECES
    copies = [
        [
            pltpu.make_async_copy(
                from_ref.at[i * step : (i + 1) * step],
                to_ref.at[i * step : (i + 1) * step],
                in_sems.at[which, i],
            )
            for i in range(PIECES)
        ]
        for which, (from_ref, to_ref) in enumerate(((x_hbm, x_ref), (dy_hbm, dy_ref)))
    ]
    for copy in copies[0] + copies[1]:
        copy.start()
    me = lax.axis_index("expert")
    row_copy.wait()
    route, within = rank_among_same(row_ref[...], 0)
    slots = len(slabs) * capacity
    slot = lax.broadcasted_iota(jnp.int32, (slots, x_ref.shape[0]), 0)
    placing = jnp.where(slot == (route ^ me) * capacity + within, 1.0, 0.0).astype(BF16)
    out_copies = []
    for i, ref in enumerate((x_ref, dy_ref)):
        for copy in copies[i]:
            copy.wait()
        placed_ref[i] = jnp.dot(placing, ref[...], preferred_element_type=F32).astype(BF16)
        for k, slab in enumerate(slabs):
            out_copies.append(
                pltpu.make_async_copy(
                    placed_ref.at[i, k * capacity : (k + 1) * capacity],
                    slab.at[i * capacity : (i + 1) * capacity],
                    out_sems.at[i, k],
                )
            )
            out_copies[-1].start()
    for copy in out_copies:
        copy.wait()


def collect_kernel(capacity, count, *refs):
    slabs, out_ref = refs[:count], refs[-1]
    half = len(slabs) * capacity
    for i, slab in enumerate(slabs):
        out_ref[i * capacity : (i + 1) * capacity, :] = slab[:capacity, :]
        out_ref[half + i * capacity : half + (i + 1) * capacity, :] = slab[capacity:, :]


def side(which, width):
    return pl.ds(pl.multiple_of(which * width, width), width)


def input_rows(d_gate_ref, d_up_ref, gate_ref, up_ref, columns):
    over_hidden = (((0,), (0,)), ((), ()))
    return lax.dot_general(
        d_gate_ref[...], gate_ref[:, columns], over_hidden, preferred_element_type=F32
    ) + lax.dot_general(
        d_up_ref[...], up_ref[:, columns], over_hidden, preferred_element_type=F32
    )


OVER_FEATURES = (((1,), (1,)), ((), ()))


def begin_kernel(tile, own_ref, gate_ref, up_ref, down_ref, *out_refs):
    rows, width = out_refs[0].shape[1], own_ref.shape[1]
    columns = side(lax.axis_index("tensor"), width)

    @pl.loop(0, gate_ref.shape[0] // tile)
    def _(step):
        units = pl.ds(pl.multiple_of(step * tile, tile), tile)
        for weight_ref, out_ref, start in zip(
            (gate_ref, up_ref, down_ref), out_refs, (0, 0, rows)
        ):
            out_ref[units, :] = lax.dot_general(
                weight_ref[units, columns],
                own_ref[start : start + rows, :],
                OVER_FEATURES,
                preferred_element_type=F32,
            )


def front_kernel(tile, own_ref, other_ref, gate_ref, up_ref, down_ref, *refs):
    *begun_refs, hidden_hbm, d_gate_ref, d_up_ref, sent_ref, hidden_ref, sem = refs
    rows, width = sent_ref.shape
    mine = lax.axis_index("tensor")

    @pl.loop(0, hidden_ref.shape[0] // tile)
    def _(step):
        units = pl.ds(pl.multiple_of(step * tile, tile), tile)

        def product(which, weight_ref, start):
            def share(half_ref, half):
                return lax.dot_general(
                    weight_ref[units, side(half, width)],
                    half_ref[start : start + rows, :],
                    OVER_FEATURES,
                    preferred_element_type=F32,
                )

            own = begun_refs[which][units, :] if begun_refs else share(own_ref, mine)
            return own + share(other_ref, 1 - mine)

        gate_pre = product(0, gate_ref, 0)
        up_pre = product(1, up_ref, 0)
        d_hidden = product(2, down_ref, rows)
        sig = jax.nn.sigmoid(gate_pre)
        silu = gate_pre * sig
        hidden_ref[units, :] = (silu * up_pre).astype(BF16)
        d_up_ref[units, :] = (d_hidden * silu).astype(BF16)
        d_gate_ref[units, :] = (
            d_hidden * up_pre * sig * (1.0 + gate_pre * (1.0 - sig))
        ).astype(BF16)

    copy = pltpu.make_async_copy(hidden_ref, hidden_hbm, sem)
    copy.start()
    sent_ref[...] = input_rows(
        d_gate_ref, d_up_ref, gate_ref, up_ref, side(1 - mine, width)
    ).astype(BF16)
    copy.wait()


def kept_kernel(d_gate_ref, d_up_ref, gate_ref, up_ref, out_ref):
    columns = side(lax.axis_index("tensor"), out_ref.shape[1])
    out_ref[...] = input_rows(d_gate_ref, d_up_ref, gate_ref, up_ref, columns)


def sum_kernel(capacity, group, kept_ref, got_ref, *refs):
    out_hbm, done_ref, sum_ref, sems = refs[-4:]
    done_ref[...] = jnp.zeros_like(done_ref)
    me = lax.axis_index("expert")
    copies = []
    for i, k in enumerate(group):
        here = slice(i * capacity, (i + 1) * capacity)
        there = pl.ds(pl.multiple_of((me ^ k) * capacity, capacity), capacity)
        sum_ref[here, :] = (kept_ref[here, :] + got_ref[here, :].astype(F32)).astype(BF16)
        copies.append(
            pltpu.make_async_copy(sum_ref.at[here], out_hbm.at[there], sems.at[i])
        )
        copies[-1].start()
    for copy in copies:
        copy.wait()


def grads_kernel(sizes, *refs):
    *ins, _, grad_gate_ref, grad_up_ref, grad_down_ref = refs
    mine = lax.axis_index("tensor")
    groups = [(*ins[5 * i : 5 * i + 5], rows) for i, rows in enumerate(sizes)]
    width = groups[0][0].shape[1]

    def total(left, half, second):
        return sum(
            jnp.dot(
                one[left][...],
                one[half][one[5] * second : one[5] * (second + 1), :],
                preferred_element_type=F32,
            )
            for one in groups
        ).astype(BF16)

    for half, which in enumerate((mine, 1 - mine)):
        grad_gate_ref[:, side(which, width)] = total(2, half, 0)
        grad_up_ref[:, side(which, width)] = total(3, half, 0)
        grad_down_ref[:, side(which, width)] = total(4, half, 1)


def placing_kernel(capacity, row_ref, _, placing_ref):
    route, within = rank_among_same(row_ref[...], 1)
    slot = lax.broadcasted_iota(jnp.int32, placing_ref.shape, 1)
    placing_ref[...] = jnp.where(slot == route * capacity + within, 1.0, 0.0).astype(BF16)


def combine_kernel(placing_ref, back_hbm, out_ref, back_ref, sems):
    step = back_ref.shape[0] // PIECES
    copies = [
        pltpu.make_async_copy(
            back_hbm.at[i * step : (i + 1) * step],
            back_ref.at[i * step : (i + 1) * step],
            sems.at[i],
        )
        for i in range(PIECES)
    ]
    for copy in copies:
        copy.start()
    total = jnp.zeros(out_ref.shape, F32)
    for i, copy in enumerate(copies):
        copy.wait()
        total += jnp.dot(
            placing_ref[:, i * step : (i + 1) * step],
            back_ref[i * step : (i + 1) * step],
            preferred_element_type=F32,
        )
    out_ref[...] = total.astype(BF16)


def params(limit):
    return pltpu.CompilerParams(vmem_limit_bytes=limit)


def cost(products, rows, hidden, features):
    return pl.CostEstimate(
        flops=2 * products * rows * hidden * features,
        bytes_accessed=2 * products * (hidden + rows) * features,
        transcendentals=0,
    )


def placing_of(capacity, ids_row, slots, after):
    return pl.pallas_call(
        functools.partial(placing_kernel, capacity),
        out_shape=jax.ShapeDtypeStruct((ids_row.shape[1], slots), BF16),
        in_specs=[IN_VMEM] * 2,
        out_specs=IN_VMEM,
        compiler_params=params(SMALL),
        name="placing",
    )(ids_row, after)


def combine(placing, returned):
    slots, width = returned.shape
    return pl.pallas_call(
        combine_kernel,
        out_shape=jax.ShapeDtypeStruct((placing.shape[0], width), BF16),
        in_specs=[IN_VMEM, IN_HBM],
        out_specs=IN_VMEM,
        scratch_shapes=[pltpu.VMEM((slots, width), BF16), pltpu.SemaphoreType.DMA((PIECES,))],
        compiler_params=params(SMALL),
        name="combine",
    )(placing, returned)


def to_experts(rows, experts):
    return lax.all_to_all(
        rows.reshape(experts, rows.shape[0] // experts, rows.shape[1]),
        "expert",
        split_axis=0,
        concat_axis=0,
        tiled=True,
    ).reshape(rows.shape)


def grouped(tokens, upstream, expert_ids, gate_rows, up_rows, down_rows):
    experts = lax.axis_size("expert")
    tok_rows, width = tokens.shape
    units, features = gate_rows.shape
    capacity = max(2, 2 * tok_rows // experts)
    ids_row = expert_ids.reshape(1, tok_rows)
    tile = units // 2 if units % 32 == 0 else units

    far = [k for k in reversed(range(1, experts)) if k >= experts // 2]
    near = [k for k in reversed(range(1, experts)) if k < experts // 2]
    turns = [k for pair in zip(far, near) for k in pair] + far[len(near) :]
    cut = 3 * experts // 4
    first, second = turns[:cut], turns[cut:] + [0]

    slabs = list(
        pl.pallas_call(
            functools.partial(place_kernel, capacity),
            out_shape=[jax.ShapeDtypeStruct((2 * capacity, width), BF16)] * experts,
            in_specs=[IN_HBM] * 3,
            out_specs=[IN_HBM] * experts,
            scratch_shapes=[
                pltpu.VMEM((1, tok_rows), jnp.int32),
                pltpu.VMEM((tok_rows, width), BF16),
                pltpu.VMEM((tok_rows, width), BF16),
                pltpu.VMEM((2, experts * capacity, width), BF16),
                pltpu.SemaphoreType.DMA,
                pltpu.SemaphoreType.DMA((2, PIECES)),
                pltpu.SemaphoreType.DMA((2, experts)),
            ],
            compiler_params=params(LARGE),
            name="place",
        )(ids_row, tokens, upstream)
    )

    def swap(k):
        return lax.ppermute(slabs[k], "expert", [(e, e ^ k) for e in range(experts)])

    def exchange(values):
        return lax.ppermute(values, "tensor", [(0, 1), (1, 0)])

    def collect(arrived, after):
        return pl.pallas_call(
            functools.partial(collect_kernel, capacity, len(arrived)),
            out_shape=jax.ShapeDtypeStruct((2 * len(arrived) * capacity, width), BF16),
            in_specs=[IN_VMEM] * (len(arrived) + len(after)),
            out_specs=IN_VMEM,
            compiler_params=params(SMALL),
            cost_estimate=cost(COLLECT, len(arrived) * capacity, units, features),
            name="collect",
        )(*arrived, *after)

    def begin(own):
        rows = own.shape[0] // 2
        return pl.pallas_call(
            functools.partial(begin_kernel, tile),
            out_shape=[jax.ShapeDtypeStruct((units, rows), F32)] * 3,
            in_specs=[IN_VMEM] * 4,
            out_specs=[IN_VMEM] * 3,
            compiler_params=params(SMALL),
            cost_estimate=cost(2, rows, units, features),
            name="begin",
        )(own, gate_rows, up_rows, down_rows)

    def front(own, begun):
        other = exchange(own)
        rows = own.shape[0] // 2
        hidden, d_gate, d_up, sent = pl.pallas_call(
            functools.partial(front_kernel, tile),
            out_shape=[jax.ShapeDtypeStruct((units, rows), BF16)] * 3
            + [jax.ShapeDtypeStruct((rows, width), BF16)],
            in_specs=[IN_VMEM] * (5 + len(begun)),
            out_specs=[IN_HBM] + [IN_VMEM] * 3,
            scratch_shapes=[pltpu.VMEM((units, rows), BF16), pltpu.SemaphoreType.DMA],
            compiler_params=params(SMALL),
            cost_estimate=cost(4, rows, units, features),
            name="front",
        )(own, other, gate_rows, up_rows, down_rows, *begun)
        kept = pl.pallas_call(
            kept_kernel,
            out_shape=jax.ShapeDtypeStruct((rows, width), F32),
            in_specs=[IN_VMEM] * 4,
            out_specs=IN_VMEM,
            compiler_params=params(SMALL),
            cost_estimate=cost(1, rows, units, features),
            name="kept",
        )(d_gate, d_up, gate_rows, up_rows)
        return (own, other, d_gate, d_up, hidden), (kept, exchange(sent))

    got = {k: swap(k) for k in turns}
    got[0] = slabs[0]
    for_grads_a, for_sum_a = front(collect([got[k] for k in first], []), [])
    own_b = collect([got[k] for k in second], for_sum_a[:1])
    for_grads_b, for_sum_b = front(own_b, begin(own_b))

    def add_rows(group, kept, got_rows, earlier):
        return pl.pallas_call(
            functools.partial(sum_kernel, capacity, group),
            out_shape=[
                jax.ShapeDtypeStruct((experts * capacity, width), BF16),
                jax.ShapeDtypeStruct((8, 128), F32),
            ],
            in_specs=[IN_VMEM] * 2 + [IN_HBM] * len(earlier),
            out_specs=[IN_HBM, IN_VMEM],
            input_output_aliases={2: 0} if earlier else {},
            scratch_shapes=[
                pltpu.VMEM((len(group) * capacity, width), BF16),
                pltpu.SemaphoreType.DMA((len(group),)),
            ],
            compiler_params=params(SMALL),
            name="sum",
        )(kept, got_rows, *earlier)

    totals, _ = add_rows(first, *for_sum_a, [])
    totals, done = add_rows(second, *for_sum_b, [totals])
    returned = to_experts(totals, experts)
    placing = placing_of(capacity, ids_row, experts * capacity, done)

    def grads_specs(rows):
        return [pl.BlockSpec((2 * rows, width), lambda i: (0, 0))] * 2 + [
            pl.BlockSpec((tile, rows), lambda i: (i, 0))
        ] * 3

    sizes = [len(group) * capacity for group in (first, second)]
    grads = pl.pallas_call(
        functools.partial(grads_kernel, sizes),
        grid=(units // tile,),
        out_shape=[jax.ShapeDtypeStruct((units, features), BF16)] * 3,
        in_specs=grads_specs(sizes[0])
        + grads_specs(sizes[1])
        + [pl.BlockSpec(placing.shape, lambda i: (0, 0))],
        out_specs=[pl.BlockSpec((tile, features), lambda i: (i, 0))] * 3,
        compiler_params=params(2 * SMALL),
        cost_estimate=cost(3, sum(sizes), units, features),
        name="grads",
    )(*for_grads_a, *for_grads_b, placing)
    return combine(placing, returned), grads


def rows_by_weights(rows, weights):
    return lax.dot_general(rows, weights, (((1,), (1,)), ((), ())), preferred_element_type=F32)


def weight_grad(left, right):
    return lax.dot_general(
        left, right, (((0,), (0,)), ((), ())), preferred_element_type=F32
    ).astype(BF16)


def general(tokens, upstream, expert_ids, gate_rows, up_rows, down_rows):
    experts = lax.axis_size("expert")
    tok_rows, width = tokens.shape
    capacity = max(2, 2 * tok_rows // experts)
    route = expert_ids[:, 0]
    onehot = (route[:, None] == jnp.arange(experts, dtype=jnp.int32)[None, :]).astype(jnp.int32)
    before = jnp.cumsum(onehot, axis=0) - onehot
    target = route * capacity + jnp.sum(before * onehot, axis=1)
    slot = jnp.arange(experts * capacity, dtype=jnp.int32)
    placing = (target[None, :] == slot[:, None]).astype(BF16)
    both = jnp.concatenate([tokens, upstream], axis=1)
    own = to_experts(jnp.dot(placing, both, preferred_element_type=F32).astype(BF16), experts)
    x_all = lax.all_gather(own[:, :width], "tensor", axis=1, tiled=True)
    dy_all = lax.all_gather(own[:, width:], "tensor", axis=1, tiled=True)
    gate_pre = rows_by_weights(x_all, gate_rows)
    up_pre = rows_by_weights(x_all, up_rows)
    d_hidden = rows_by_weights(dy_all, down_rows)
    sig = jax.nn.sigmoid(gate_pre)
    silu = gate_pre * sig
    hidden = (silu * up_pre).astype(BF16)
    d_up = (d_hidden * silu).astype(BF16)
    d_gate = (d_hidden * up_pre * sig * (1.0 + gate_pre * (1.0 - sig))).astype(BF16)
    partial = jnp.dot(d_gate, gate_rows, preferred_element_type=F32) + jnp.dot(
        d_up, up_rows, preferred_element_type=F32
    )
    totals = lax.psum_scatter(partial.astype(BF16), "tensor", scatter_dimension=1, tiled=True)
    returned = to_experts(totals, experts)
    grads = [weight_grad(d_gate, x_all), weight_grad(d_up, x_all), weight_grad(hidden, dy_all)]
    return weight_grad(placing, returned), grads


def on_device(tokens, upstream, expert_ids, w_gate, w_up, w_down):
    experts = lax.axis_size("expert")
    capacity = 2 * tokens.shape[0] // experts
    pairs = lax.axis_size("tensor") == 2 and experts & (experts - 1) == 0 and experts > 4
    run = grouped if pairs and capacity % 16 == 0 else general
    grad_tokens, grads = run(tokens, upstream, expert_ids, w_gate[0], w_up[0], w_down[0])
    return (grad_tokens, *(grad[None] for grad in grads))


def solution(mesh):
    rows = P("expert", "tensor")
    weights = P("expert", "tensor", None)
    return jax.shard_map(
        on_device,
        mesh=mesh,
        in_specs=(rows, rows, P("expert", None), weights, weights, weights),
        out_specs=(rows, weights, weights, weights),
        check_vma=False,
    )
```

```python
import functools

import jax
import jax.numpy as jnp
from jax import lax
from jax.experimental import pallas as pl
from jax.experimental.pallas import tpu as pltpu
from jax.sharding import PartitionSpec as P

F32 = jnp.float32
BF16 = jnp.bfloat16
SMALL = 16 * 2**20
LARGE = 56 * 2**20
PIECES = 4
COLLECT = 16
IN_VMEM = pl.BlockSpec(memory_space=pltpu.VMEM)
IN_HBM = pl.BlockSpec(memory_space=pltpu.HBM)


def rank_among_same(row, axis):
    rows = row.shape[1]
    down = lax.broadcasted_iota(jnp.int32, (rows, rows), 0)
    right = lax.broadcasted_iota(jnp.int32, (rows, rows), 1)
    col = jnp.sum(jnp.where(down == right, row, 0), axis=1, keepdims=True)
    earlier = down > right if axis else down < right
    same = jnp.where((col == row) & earlier, 1, 0)
    return (col if axis else row), jnp.sum(same, axis=axis, keepdims=True)


def place_kernel(capacity, partners, row_hbm, x_hbm, dy_hbm, *refs):
    *slabs, row_ref, x_ref, dy_ref, placed_ref, row_sem, in_sems, out_sems = refs
    row_copy = pltpu.make_async_copy(row_hbm, row_ref, row_sem)
    row_copy.start()
    step = x_ref.shape[0] // PIECES
    copies = [
        [
            pltpu.make_async_copy(
                from_ref.at[i * step : (i + 1) * step],
                to_ref.at[i * step : (i + 1) * step],
                in_sems.at[which, i],
            )
            for i in range(PIECES)
        ]
        for which, (from_ref, to_ref) in enumerate(((x_hbm, x_ref), (dy_hbm, dy_ref)))
    ]
    for copy in copies[0] + copies[1]:
        copy.start()
    me = lax.axis_index("expert")
    row_copy.wait()
    route, within = rank_among_same(row_ref[...], 0)
    within_slab = lax.broadcasted_iota(jnp.int32, (capacity, x_ref.shape[0]), 0)
    slot = jnp.concatenate([within_slab + k * capacity for k in partners], axis=0)
    placing = jnp.where(slot == (route ^ me) * capacity + within, 1.0, 0.0).astype(BF16)
    out_copies = []
    for i, ref in enumerate((x_ref, dy_ref)):
        for copy in copies[i]:
            copy.wait()
        placed_ref[i] = jnp.dot(placing, ref[...], preferred_element_type=F32).astype(BF16)
        for j, slab in enumerate(slabs):
            out_copies.append(
                pltpu.make_async_copy(
                    placed_ref.at[i, j * capacity : (j + 1) * capacity],
                    slab.at[i * capacity : (i + 1) * capacity],
                    out_sems.at[i, j],
                )
            )
            out_copies[-1].start()
    for copy in out_copies:
        copy.wait()


def collect_kernel(capacity, count, *refs):
    slabs, out_ref = refs[:count], refs[-1]
    half = len(slabs) * capacity
    for i, slab in enumerate(slabs):
        out_ref[i * capacity : (i + 1) * capacity, :] = slab[:capacity, :]
        out_ref[half + i * capacity : half + (i + 1) * capacity, :] = slab[capacity:, :]


def side(which, width):
    return pl.ds(pl.multiple_of(which * width, width), width)


def input_rows(d_gate_ref, d_up_ref, gate_ref, up_ref, columns):
    over_hidden = (((0,), (0,)), ((), ()))
    return lax.dot_general(
        d_gate_ref[...], gate_ref[:, columns], over_hidden, preferred_element_type=F32
    ) + lax.dot_general(
        d_up_ref[...], up_ref[:, columns], over_hidden, preferred_element_type=F32
    )


OVER_FEATURES = (((1,), (1,)), ((), ()))


def begin_kernel(tile, own_ref, gate_ref, up_ref, down_ref, *out_refs):
    rows, width = out_refs[0].shape[1], own_ref.shape[1]
    columns = side(lax.axis_index("tensor"), width)

    @pl.loop(0, gate_ref.shape[0] // tile)
    def _(step):
        units = pl.ds(pl.multiple_of(step * tile, tile), tile)
        for weight_ref, out_ref, start in zip(
            (gate_ref, up_ref, down_ref), out_refs, (0, 0, rows)
        ):
            out_ref[units, :] = lax.dot_general(
                weight_ref[units, columns],
                own_ref[start : start + rows, :],
                OVER_FEATURES,
                preferred_element_type=F32,
            )


def front_kernel(tile, own_ref, other_ref, gate_ref, up_ref, down_ref, *refs):
    *begun_refs, hidden_ref, d_gate_ref, d_up_ref, sent_ref = refs
    rows, width = sent_ref.shape
    mine = lax.axis_index("tensor")

    @pl.loop(0, hidden_ref.shape[0] // tile)
    def _(step):
        units = pl.ds(pl.multiple_of(step * tile, tile), tile)

        def product(which, weight_ref, start):
            def share(half_ref, half):
                return lax.dot_general(
                    weight_ref[units, side(half, width)],
                    half_ref[start : start + rows, :],
                    OVER_FEATURES,
                    preferred_element_type=F32,
                )

            own = begun_refs[which][units, :] if begun_refs else share(own_ref, mine)
            return own + share(other_ref, 1 - mine)

        gate_pre = product(0, gate_ref, 0)
        up_pre = product(1, up_ref, 0)
        d_hidden = product(2, down_ref, rows)
        sig = jax.nn.sigmoid(gate_pre)
        silu = gate_pre * sig
        hidden_ref[units, :] = (silu * up_pre).astype(BF16)
        d_up_ref[units, :] = (d_hidden * silu).astype(BF16)
        d_gate_ref[units, :] = (
            d_hidden * up_pre * sig * (1.0 + gate_pre * (1.0 - sig))
        ).astype(BF16)

    sent_ref[...] = input_rows(
        d_gate_ref, d_up_ref, gate_ref, up_ref, side(1 - mine, width)
    ).astype(BF16)


def kept_kernel(d_gate_ref, d_up_ref, gate_ref, up_ref, out_ref):
    columns = side(lax.axis_index("tensor"), out_ref.shape[1])
    out_ref[...] = input_rows(d_gate_ref, d_up_ref, gate_ref, up_ref, columns)


def sum_kernel(kept_ref, got_ref, out_ref):
    out_ref[...] = (kept_ref[...] + got_ref[...].astype(F32)).astype(BF16)


def last_sum_kernel(capacity, groups, sum_ref, kept_ref, got_ref, out_ref, done_ref):
    done_ref[...] = jnp.zeros_like(done_ref)
    me = lax.axis_index("expert")
    for last, group in enumerate(groups):
        for i, k in enumerate(group):
            here = slice(i * capacity, (i + 1) * capacity)
            there = pl.ds(pl.multiple_of((me ^ k) * capacity, capacity), capacity)
            if last:
                both = kept_ref[here, :] + got_ref[here, :].astype(F32)
                out_ref[there, :] = both.astype(BF16)
            else:
                out_ref[there, :] = sum_ref[here, :]


def grads_kernel(sizes, *refs):
    *ins, _, grad_gate_ref, grad_up_ref, grad_down_ref = refs
    mine = lax.axis_index("tensor")
    groups = [(*ins[5 * i : 5 * i + 5], rows) for i, rows in enumerate(sizes)]
    width = groups[0][0].shape[1]

    def total(left, half, second):
        return sum(
            jnp.dot(
                one[left][...],
                one[half][one[5] * second : one[5] * (second + 1), :],
                preferred_element_type=F32,
            )
            for one in groups
        ).astype(BF16)

    for half, which in enumerate((mine, 1 - mine)):
        grad_gate_ref[:, side(which, width)] = total(2, half, 0)
        grad_up_ref[:, side(which, width)] = total(3, half, 0)
        grad_down_ref[:, side(which, width)] = total(4, half, 1)


def placing_kernel(capacity, row_ref, _, placing_ref):
    route, within = rank_among_same(row_ref[...], 1)
    slot = lax.broadcasted_iota(jnp.int32, placing_ref.shape, 1)
    placing_ref[...] = jnp.where(slot == route * capacity + within, 1.0, 0.0).astype(BF16)


def combine_kernel(placing_ref, back_hbm, out_ref, back_ref, sems):
    step = back_ref.shape[0] // PIECES
    copies = [
        pltpu.make_async_copy(
            back_hbm.at[i * step : (i + 1) * step],
            back_ref.at[i * step : (i + 1) * step],
            sems.at[i],
        )
        for i in range(PIECES)
    ]
    for copy in copies:
        copy.start()
    total = jnp.zeros(out_ref.shape, F32)
    for i, copy in enumerate(copies):
        copy.wait()
        total += jnp.dot(
            placing_ref[:, i * step : (i + 1) * step],
            back_ref[i * step : (i + 1) * step],
            preferred_element_type=F32,
        )
    out_ref[...] = total.astype(BF16)


def params(limit):
    return pltpu.CompilerParams(vmem_limit_bytes=limit)


def cost(products, rows, hidden, features):
    return pl.CostEstimate(
        flops=2 * products * rows * hidden * features,
        bytes_accessed=2 * products * (hidden + rows) * features,
        transcendentals=0,
    )


def placing_of(capacity, ids_row, slots, after):
    return pl.pallas_call(
        functools.partial(placing_kernel, capacity),
        out_shape=jax.ShapeDtypeStruct((ids_row.shape[1], slots), BF16),
        in_specs=[IN_VMEM] * 2,
        out_specs=IN_VMEM,
        compiler_params=params(SMALL),
        name="placing",
    )(ids_row, after)


def combine(placing, returned):
    slots, width = returned.shape
    return pl.pallas_call(
        combine_kernel,
        out_shape=jax.ShapeDtypeStruct((placing.shape[0], width), BF16),
        in_specs=[IN_VMEM, IN_HBM],
        out_specs=IN_VMEM,
        scratch_shapes=[pltpu.VMEM((slots, width), BF16), pltpu.SemaphoreType.DMA((PIECES,))],
        compiler_params=params(SMALL),
        name="combine",
    )(placing, returned)


def to_experts(rows, experts):
    return lax.all_to_all(
        rows.reshape(experts, rows.shape[0] // experts, rows.shape[1]),
        "expert",
        split_axis=0,
        concat_axis=0,
        tiled=True,
    ).reshape(rows.shape)


def grouped(tokens, upstream, expert_ids, gate_rows, up_rows, down_rows):
    experts = lax.axis_size("expert")
    tok_rows, width = tokens.shape
    units, features = gate_rows.shape
    capacity = max(2, 2 * tok_rows // experts)
    ids_row = expert_ids.reshape(1, tok_rows)
    tile = units // 2 if units % 32 == 0 else units

    far = [k for k in reversed(range(1, experts)) if k >= experts // 2]
    near = [k for k in reversed(range(1, experts)) if k < experts // 2]
    turns = [k for pair in zip(far, near) for k in pair] + far[len(near) :]
    cut = 3 * experts // 4
    first, second = turns[:cut], turns[cut:] + [0]

    def place(partners):
        return pl.pallas_call(
            functools.partial(place_kernel, capacity, partners),
            out_shape=[jax.ShapeDtypeStruct((2 * capacity, width), BF16)] * len(partners),
            in_specs=[IN_HBM] * 3,
            out_specs=[IN_HBM] * len(partners),
            scratch_shapes=[
                pltpu.VMEM((1, tok_rows), jnp.int32),
                pltpu.VMEM((tok_rows, width), BF16),
                pltpu.VMEM((tok_rows, width), BF16),
                pltpu.VMEM((2, len(partners) * capacity, width), BF16),
                pltpu.SemaphoreType.DMA,
                pltpu.SemaphoreType.DMA((2, PIECES)),
                pltpu.SemaphoreType.DMA((2, len(partners))),
            ],
            compiler_params=params(LARGE),
            name="place",
        )(ids_row, tokens, upstream)

    early = experts // 2 - 1
    slabs = {}
    for partners in (turns[:early], turns[early:] + [0]):
        slabs.update(zip(partners, place(partners)))

    def swap(k):
        return lax.ppermute(slabs[k], "expert", [(e, e ^ k) for e in range(experts)])

    def exchange(values):
        return lax.ppermute(values, "tensor", [(0, 1), (1, 0)])

    def collect(arrived, after):
        return pl.pallas_call(
            functools.partial(collect_kernel, capacity, len(arrived)),
            out_shape=jax.ShapeDtypeStruct((2 * len(arrived) * capacity, width), BF16),
            in_specs=[IN_VMEM] * (len(arrived) + len(after)),
            out_specs=IN_VMEM,
            compiler_params=params(SMALL),
            cost_estimate=cost(COLLECT, len(arrived) * capacity, units, features),
            name="collect",
        )(*arrived, *after)

    def begin(own):
        rows = own.shape[0] // 2
        return pl.pallas_call(
            functools.partial(begin_kernel, tile),
            out_shape=[jax.ShapeDtypeStruct((units, rows), F32)] * 3,
            in_specs=[IN_VMEM] * 4,
            out_specs=[IN_VMEM] * 3,
            compiler_params=params(SMALL),
            cost_estimate=cost(2, rows, units, features),
            name="begin",
        )(own, gate_rows, up_rows, down_rows)

    def front(own, begun):
        other = exchange(own)
        rows = own.shape[0] // 2
        hidden, d_gate, d_up, sent = pl.pallas_call(
            functools.partial(front_kernel, tile),
            out_shape=[jax.ShapeDtypeStruct((units, rows), BF16)] * 3
            + [jax.ShapeDtypeStruct((rows, width), BF16)],
            in_specs=[IN_VMEM] * (5 + len(begun)),
            out_specs=[IN_VMEM] * 4,
            compiler_params=params(SMALL),
            cost_estimate=cost(4, rows, units, features),
            name="front",
        )(own, other, gate_rows, up_rows, down_rows, *begun)
        kept = pl.pallas_call(
            kept_kernel,
            out_shape=jax.ShapeDtypeStruct((rows, width), F32),
            in_specs=[IN_VMEM] * 4,
            out_specs=IN_VMEM,
            compiler_params=params(SMALL),
            cost_estimate=cost(1, rows, units, features),
            name="kept",
        )(d_gate, d_up, gate_rows, up_rows)
        return (own, other, d_gate, d_up, hidden), (kept, exchange(sent))

    got = {k: swap(k) for k in turns}
    got[0] = slabs[0]
    for_grads_a, for_sum_a = front(collect([got[k] for k in first], []), [])
    own_b = collect([got[k] for k in second], for_sum_a[:1])
    for_grads_b, for_sum_b = front(own_b, begin(own_b))
    sum_a = pl.pallas_call(
        sum_kernel,
        out_shape=jax.ShapeDtypeStruct((len(first) * capacity, width), BF16),
        in_specs=[IN_VMEM] * 2,
        out_specs=IN_VMEM,
        compiler_params=params(SMALL),
        name="sum",
    )(*for_sum_a)
    totals, done = pl.pallas_call(
        functools.partial(last_sum_kernel, capacity, (first, second)),
        out_shape=[
            jax.ShapeDtypeStruct((experts * capacity, width), BF16),
            jax.ShapeDtypeStruct((8, 128), F32),
        ],
        in_specs=[IN_VMEM] * 3,
        out_specs=[IN_VMEM] * 2,
        compiler_params=params(SMALL),
        name="last_sum",
    )(sum_a, *for_sum_b)
    returned = to_experts(totals, experts)
    placing = placing_of(capacity, ids_row, experts * capacity, done)

    def grads_specs(rows):
        return [pl.BlockSpec((2 * rows, width), lambda i: (0, 0))] * 2 + [
            pl.BlockSpec((tile, rows), lambda i: (i, 0))
        ] * 3

    sizes = [len(group) * capacity for group in (first, second)]
    grads = pl.pallas_call(
        functools.partial(grads_kernel, sizes),
        grid=(units // tile,),
        out_shape=[jax.ShapeDtypeStruct((units, features), BF16)] * 3,
        in_specs=grads_specs(sizes[0])
        + grads_specs(sizes[1])
        + [pl.BlockSpec(placing.shape, lambda i: (0, 0))],
        out_specs=[pl.BlockSpec((tile, features), lambda i: (i, 0))] * 3,
        compiler_params=params(2 * SMALL),
        cost_estimate=cost(3, sum(sizes), units, features),
        name="grads",
    )(*for_grads_a, *for_grads_b, placing)
    return combine(placing, returned), grads


def rows_by_weights(rows, weights):
    return lax.dot_general(rows, weights, (((1,), (1,)), ((), ())), preferred_element_type=F32)


def weight_grad(left, right):
    return lax.dot_general(
        left, right, (((0,), (0,)), ((), ())), preferred_element_type=F32
    ).astype(BF16)


def general(tokens, upstream, expert_ids, gate_rows, up_rows, down_rows):
    experts = lax.axis_size("expert")
    tok_rows, width = tokens.shape
    capacity = max(2, 2 * tok_rows // experts)
    route = expert_ids[:, 0]
    onehot = (route[:, None] == jnp.arange(experts, dtype=jnp.int32)[None, :]).astype(jnp.int32)
    before = jnp.cumsum(onehot, axis=0) - onehot
    target = route * capacity + jnp.sum(before * onehot, axis=1)
    slot = jnp.arange(experts * capacity, dtype=jnp.int32)
    placing = (target[None, :] == slot[:, None]).astype(BF16)
    both = jnp.concatenate([tokens, upstream], axis=1)
    own = to_experts(jnp.dot(placing, both, preferred_element_type=F32).astype(BF16), experts)
    x_all = lax.all_gather(own[:, :width], "tensor", axis=1, tiled=True)
    dy_all = lax.all_gather(own[:, width:], "tensor", axis=1, tiled=True)
    gate_pre = rows_by_weights(x_all, gate_rows)
    up_pre = rows_by_weights(x_all, up_rows)
    d_hidden = rows_by_weights(dy_all, down_rows)
    sig = jax.nn.sigmoid(gate_pre)
    silu = gate_pre * sig
    hidden = (silu * up_pre).astype(BF16)
    d_up = (d_hidden * silu).astype(BF16)
    d_gate = (d_hidden * up_pre * sig * (1.0 + gate_pre * (1.0 - sig))).astype(BF16)
    partial = jnp.dot(d_gate, gate_rows, preferred_element_type=F32) + jnp.dot(
        d_up, up_rows, preferred_element_type=F32
    )
    totals = lax.psum_scatter(partial.astype(BF16), "tensor", scatter_dimension=1, tiled=True)
    returned = to_experts(totals, experts)
    grads = [weight_grad(d_gate, x_all), weight_grad(d_up, x_all), weight_grad(hidden, dy_all)]
    return weight_grad(placing, returned), grads


def on_device(tokens, upstream, expert_ids, w_gate, w_up, w_down):
    experts = lax.axis_size("expert")
    capacity = 2 * tokens.shape[0] // experts
    pairs = lax.axis_size("tensor") == 2 and experts & (experts - 1) == 0 and experts > 4
    run = grouped if pairs and capacity % 16 == 0 else general
    grad_tokens, grads = run(tokens, upstream, expert_ids, w_gate[0], w_up[0], w_down[0])
    return (grad_tokens, *(grad[None] for grad in grads))


def solution(mesh):
    rows = P("expert", "tensor")
    weights = P("expert", "tensor", None)
    return jax.shard_map(
        on_device,
        mesh=mesh,
        in_specs=(rows, rows, P("expert", None), weights, weights, weights),
        out_specs=(rows, weights, weights, weights),
        check_vma=False,
    )
```

```python
import functools

import jax
import jax.numpy as jnp
from jax import lax
from jax.experimental import pallas as pl
from jax.experimental.pallas import tpu as pltpu
from jax.sharding import PartitionSpec as P

F32 = jnp.float32
BF16 = jnp.bfloat16
SMALL = 16 * 2**20
LARGE = 56 * 2**20
PIECES = 4
COLLECT = 16
IN_VMEM = pl.BlockSpec(memory_space=pltpu.VMEM)
IN_HBM = pl.BlockSpec(memory_space=pltpu.HBM)


def rank_among_same(row, axis):
    rows = row.shape[1]
    down = lax.broadcasted_iota(jnp.int32, (rows, rows), 0)
    right = lax.broadcasted_iota(jnp.int32, (rows, rows), 1)
    col = jnp.sum(jnp.where(down == right, row, 0), axis=1, keepdims=True)
    earlier = down > right if axis else down < right
    same = jnp.where((col == row) & earlier, 1, 0)
    return (col if axis else row), jnp.sum(same, axis=axis, keepdims=True)


def place_kernel(capacity, partners, row_hbm, x_hbm, dy_hbm, *refs):
    *slabs, row_ref, x_ref, dy_ref, placed_ref, row_sem, in_sems, out_sems = refs
    row_copy = pltpu.make_async_copy(row_hbm, row_ref, row_sem)
    row_copy.start()
    step = x_ref.shape[0] // PIECES
    copies = [
        [
            pltpu.make_async_copy(
                from_ref.at[i * step : (i + 1) * step],
                to_ref.at[i * step : (i + 1) * step],
                in_sems.at[which, i],
            )
            for i in range(PIECES)
        ]
        for which, (from_ref, to_ref) in enumerate(((x_hbm, x_ref), (dy_hbm, dy_ref)))
    ]
    for copy in copies[0] + copies[1]:
        copy.start()
    me = lax.axis_index("expert")
    row_copy.wait()
    route, within = rank_among_same(row_ref[...], 0)
    within_slab = lax.broadcasted_iota(jnp.int32, (capacity, x_ref.shape[0]), 0)
    slot = jnp.concatenate([within_slab + k * capacity for k in partners], axis=0)
    placing = jnp.where(slot == (route ^ me) * capacity + within, 1.0, 0.0).astype(BF16)
    out_copies = []
    for i, ref in enumerate((x_ref, dy_ref)):
        for copy in copies[i]:
            copy.wait()
        placed_ref[i] = jnp.dot(placing, ref[...], preferred_element_type=F32).astype(BF16)
        for j, slab in enumerate(slabs):
            out_copies.append(
                pltpu.make_async_copy(
                    placed_ref.at[i, j * capacity : (j + 1) * capacity],
                    slab.at[i * capacity : (i + 1) * capacity],
                    out_sems.at[i, j],
                )
            )
            out_copies[-1].start()
    for copy in out_copies:
        copy.wait()


def collect_kernel(capacity, count, *refs):
    slabs, out_ref = refs[:count], refs[-1]
    half = len(slabs) * capacity
    for i, slab in enumerate(slabs):
        out_ref[i * capacity : (i + 1) * capacity, :] = slab[:capacity, :]
        out_ref[half + i * capacity : half + (i + 1) * capacity, :] = slab[capacity:, :]


def side(which, width):
    return pl.ds(pl.multiple_of(which * width, width), width)


def input_rows(d_gate_ref, d_up_ref, gate_ref, up_ref, columns):
    over_hidden = (((0,), (0,)), ((), ()))
    return lax.dot_general(
        d_gate_ref[...], gate_ref[:, columns], over_hidden, preferred_element_type=F32
    ) + lax.dot_general(
        d_up_ref[...], up_ref[:, columns], over_hidden, preferred_element_type=F32
    )


OVER_FEATURES = (((1,), (1,)), ((), ()))


def begin_kernel(tile, own_ref, gate_ref, up_ref, down_ref, *out_refs):
    rows, width = out_refs[0].shape[1], own_ref.shape[1]
    columns = side(lax.axis_index("tensor"), width)

    @pl.loop(0, gate_ref.shape[0] // tile)
    def _(step):
        units = pl.ds(pl.multiple_of(step * tile, tile), tile)
        for weight_ref, out_ref, start in zip(
            (gate_ref, up_ref, down_ref), out_refs, (0, 0, rows)
        ):
            out_ref[units, :] = lax.dot_general(
                weight_ref[units, columns],
                own_ref[start : start + rows, :],
                OVER_FEATURES,
                preferred_element_type=F32,
            )


def front_kernel(tile, own_ref, other_ref, gate_ref, up_ref, down_ref, *refs):
    *begun_refs, hidden_ref, d_gate_ref, d_up_ref, sent_ref = refs
    rows, width = sent_ref.shape
    mine = lax.axis_index("tensor")

    @pl.loop(0, hidden_ref.shape[0] // tile)
    def _(step):
        units = pl.ds(pl.multiple_of(step * tile, tile), tile)

        def product(which, weight_ref, start):
            def share(half_ref, half):
                return lax.dot_general(
                    weight_ref[units, side(half, width)],
                    half_ref[start : start + rows, :],
                    OVER_FEATURES,
                    preferred_element_type=F32,
                )

            own = begun_refs[which][units, :] if begun_refs else share(own_ref, mine)
            return own + share(other_ref, 1 - mine)

        gate_pre = product(0, gate_ref, 0)
        up_pre = product(1, up_ref, 0)
        d_hidden = product(2, down_ref, rows)
        sig = jax.nn.sigmoid(gate_pre)
        silu = gate_pre * sig
        hidden_ref[units, :] = (silu * up_pre).astype(BF16)
        d_up_ref[units, :] = (d_hidden * silu).astype(BF16)
        d_gate_ref[units, :] = (
            d_hidden * up_pre * sig * (1.0 + gate_pre * (1.0 - sig))
        ).astype(BF16)

    sent_ref[...] = input_rows(
        d_gate_ref, d_up_ref, gate_ref, up_ref, side(1 - mine, width)
    ).astype(BF16)


def kept_kernel(d_gate_ref, d_up_ref, gate_ref, up_ref, out_ref):
    columns = side(lax.axis_index("tensor"), out_ref.shape[1])
    out_ref[...] = input_rows(d_gate_ref, d_up_ref, gate_ref, up_ref, columns)


def sum_kernel(kept_ref, got_ref, out_ref):
    out_ref[...] = (kept_ref[...] + got_ref[...].astype(F32)).astype(BF16)


def last_sum_kernel(capacity, groups, sum_ref, kept_ref, got_ref, out_ref, done_ref):
    done_ref[...] = jnp.zeros_like(done_ref)
    me = lax.axis_index("expert")
    for last, group in enumerate(groups):
        for i, k in enumerate(group):
            here = slice(i * capacity, (i + 1) * capacity)
            there = pl.ds(pl.multiple_of((me ^ k) * capacity, capacity), capacity)
            if last:
                both = kept_ref[here, :] + got_ref[here, :].astype(F32)
                out_ref[there, :] = both.astype(BF16)
            else:
                out_ref[there, :] = sum_ref[here, :]


def grads_kernel(sizes, *refs):
    *ins, _, grad_gate_ref, grad_up_ref, grad_down_ref = refs
    mine = lax.axis_index("tensor")
    groups = [(*ins[5 * i : 5 * i + 5], rows) for i, rows in enumerate(sizes)]
    width = groups[0][0].shape[1]

    def total(left, half, second):
        return sum(
            jnp.dot(
                one[left][...],
                one[half][one[5] * second : one[5] * (second + 1), :],
                preferred_element_type=F32,
            )
            for one in groups
        ).astype(BF16)

    for half, which in enumerate((mine, 1 - mine)):
        grad_gate_ref[:, side(which, width)] = total(2, half, 0)
        grad_up_ref[:, side(which, width)] = total(3, half, 0)
        grad_down_ref[:, side(which, width)] = total(4, half, 1)


def placing_kernel(capacity, row_ref, _, placing_ref):
    route, within = rank_among_same(row_ref[...], 1)
    slot = lax.broadcasted_iota(jnp.int32, placing_ref.shape, 1)
    placing_ref[...] = jnp.where(slot == route * capacity + within, 1.0, 0.0).astype(BF16)


def combine_kernel(placing_ref, back_hbm, out_ref, back_ref, sems):
    step = back_ref.shape[0] // PIECES
    copies = [
        pltpu.make_async_copy(
            back_hbm.at[i * step : (i + 1) * step],
            back_ref.at[i * step : (i + 1) * step],
            sems.at[i],
        )
        for i in range(PIECES)
    ]
    for copy in copies:
        copy.start()
    total = jnp.zeros(out_ref.shape, F32)
    for i, copy in enumerate(copies):
        copy.wait()
        total += jnp.dot(
            placing_ref[:, i * step : (i + 1) * step],
            back_ref[i * step : (i + 1) * step],
            preferred_element_type=F32,
        )
    out_ref[...] = total.astype(BF16)


def params(limit):
    return pltpu.CompilerParams(vmem_limit_bytes=limit)


def cost(products, rows, hidden, features):
    return pl.CostEstimate(
        flops=2 * products * rows * hidden * features,
        bytes_accessed=2 * products * (hidden + rows) * features,
        transcendentals=0,
    )


def placing_of(capacity, ids_row, slots, after):
    return pl.pallas_call(
        functools.partial(placing_kernel, capacity),
        out_shape=jax.ShapeDtypeStruct((ids_row.shape[1], slots), BF16),
        in_specs=[IN_VMEM] * 2,
        out_specs=IN_VMEM,
        compiler_params=params(SMALL),
        name="placing",
    )(ids_row, after)


def combine(placing, returned):
    slots, width = returned.shape
    return pl.pallas_call(
        combine_kernel,
        out_shape=jax.ShapeDtypeStruct((placing.shape[0], width), BF16),
        in_specs=[IN_VMEM, IN_HBM],
        out_specs=IN_VMEM,
        scratch_shapes=[pltpu.VMEM((slots, width), BF16), pltpu.SemaphoreType.DMA((PIECES,))],
        compiler_params=params(SMALL),
        name="combine",
    )(placing, returned)


def to_experts(rows, experts):
    return lax.all_to_all(
        rows.reshape(experts, rows.shape[0] // experts, rows.shape[1]),
        "expert",
        split_axis=0,
        concat_axis=0,
        tiled=True,
    ).reshape(rows.shape)


def grouped(tokens, upstream, expert_ids, gate_rows, up_rows, down_rows):
    experts = lax.axis_size("expert")
    tok_rows, width = tokens.shape
    units, features = gate_rows.shape
    capacity = max(2, 2 * tok_rows // experts)
    ids_row = expert_ids.reshape(1, tok_rows)
    tile = units // 2 if units % 32 == 0 else units

    far = [k for k in reversed(range(1, experts)) if k >= experts // 2]
    near = [k for k in reversed(range(1, experts)) if k < experts // 2]
    turns = [k for pair in zip(far, near) for k in pair] + far[len(near) :]
    cut = 3 * experts // 4
    turns = turns[:cut] + sorted(turns[cut:], key=lambda k: k < experts // 2)
    first, second = turns[:cut], turns[cut:] + [0]

    def place(partners):
        return pl.pallas_call(
            functools.partial(place_kernel, capacity, partners),
            out_shape=[jax.ShapeDtypeStruct((2 * capacity, width), BF16)] * len(partners),
            in_specs=[IN_HBM] * 3,
            out_specs=[IN_HBM] * len(partners),
            scratch_shapes=[
                pltpu.VMEM((1, tok_rows), jnp.int32),
                pltpu.VMEM((tok_rows, width), BF16),
                pltpu.VMEM((tok_rows, width), BF16),
                pltpu.VMEM((2, len(partners) * capacity, width), BF16),
                pltpu.SemaphoreType.DMA,
                pltpu.SemaphoreType.DMA((2, PIECES)),
                pltpu.SemaphoreType.DMA((2, len(partners))),
            ],
            compiler_params=params(LARGE),
            name="place",
        )(ids_row, tokens, upstream)

    early = experts // 4 + 1
    slabs = {}
    for partners in (turns[:early], turns[early:] + [0]):
        slabs.update(zip(partners, place(partners)))

    def swap(k):
        return lax.ppermute(slabs[k], "expert", [(e, e ^ k) for e in range(experts)])

    def exchange(values):
        return lax.ppermute(values, "tensor", [(0, 1), (1, 0)])

    def collect(arrived, after):
        return pl.pallas_call(
            functools.partial(collect_kernel, capacity, len(arrived)),
            out_shape=jax.ShapeDtypeStruct((2 * len(arrived) * capacity, width), BF16),
            in_specs=[IN_VMEM] * (len(arrived) + len(after)),
            out_specs=IN_VMEM,
            compiler_params=params(SMALL),
            cost_estimate=cost(COLLECT, len(arrived) * capacity, units, features),
            name="collect",
        )(*arrived, *after)

    def begin(own):
        rows = own.shape[0] // 2
        return pl.pallas_call(
            functools.partial(begin_kernel, tile),
            out_shape=[jax.ShapeDtypeStruct((units, rows), F32)] * 3,
            in_specs=[IN_VMEM] * 4,
            out_specs=[IN_VMEM] * 3,
            compiler_params=params(SMALL),
            cost_estimate=cost(2, rows, units, features),
            name="begin",
        )(own, gate_rows, up_rows, down_rows)

    def front(own, begun):
        other = exchange(own)
        rows = own.shape[0] // 2
        hidden, d_gate, d_up, sent = pl.pallas_call(
            functools.partial(front_kernel, tile),
            out_shape=[jax.ShapeDtypeStruct((units, rows), BF16)] * 3
            + [jax.ShapeDtypeStruct((rows, width), BF16)],
            in_specs=[IN_VMEM] * (5 + len(begun)),
            out_specs=[IN_VMEM] * 4,
            compiler_params=params(SMALL),
            cost_estimate=cost(4, rows, units, features),
            name="front",
        )(own, other, gate_rows, up_rows, down_rows, *begun)
        kept = pl.pallas_call(
            kept_kernel,
            out_shape=jax.ShapeDtypeStruct((rows, width), F32),
            in_specs=[IN_VMEM] * 4,
            out_specs=IN_VMEM,
            compiler_params=params(SMALL),
            cost_estimate=cost(1, rows, units, features),
            name="kept",
        )(d_gate, d_up, gate_rows, up_rows)
        return (own, other, d_gate, d_up, hidden), (kept, exchange(sent))

    got = {k: swap(k) for k in turns}
    got[0] = slabs[0]
    for_grads_a, for_sum_a = front(collect([got[k] for k in first], []), [])
    own_b = collect([got[k] for k in second], for_sum_a[:1])
    for_grads_b, for_sum_b = front(own_b, begin(own_b))
    sum_a = pl.pallas_call(
        sum_kernel,
        out_shape=jax.ShapeDtypeStruct((len(first) * capacity, width), BF16),
        in_specs=[IN_VMEM] * 2,
        out_specs=IN_VMEM,
        compiler_params=params(SMALL),
        name="sum",
    )(*for_sum_a)
    totals, done = pl.pallas_call(
        functools.partial(last_sum_kernel, capacity, (first, second)),
        out_shape=[
            jax.ShapeDtypeStruct((experts * capacity, width), BF16),
            jax.ShapeDtypeStruct((8, 128), F32),
        ],
        in_specs=[IN_VMEM] * 3,
        out_specs=[IN_VMEM] * 2,
        compiler_params=params(SMALL),
        name="last_sum",
    )(sum_a, *for_sum_b)
    returned = to_experts(totals, experts)
    placing = placing_of(capacity, ids_row, experts * capacity, done)

    def grads_specs(rows):
        return [pl.BlockSpec((2 * rows, width), lambda i: (0, 0))] * 2 + [
            pl.BlockSpec((tile, rows), lambda i: (i, 0))
        ] * 3

    sizes = [len(group) * capacity for group in (first, second)]
    grads = pl.pallas_call(
        functools.partial(grads_kernel, sizes),
        grid=(units // tile,),
        out_shape=[jax.ShapeDtypeStruct((units, features), BF16)] * 3,
        in_specs=grads_specs(sizes[0])
        + grads_specs(sizes[1])
        + [pl.BlockSpec(placing.shape, lambda i: (0, 0))],
        out_specs=[pl.BlockSpec((tile, features), lambda i: (i, 0))] * 3,
        compiler_params=params(2 * SMALL),
        cost_estimate=cost(3, sum(sizes), units, features),
        name="grads",
    )(*for_grads_a, *for_grads_b, placing)
    return combine(placing, returned), grads


def rows_by_weights(rows, weights):
    return lax.dot_general(rows, weights, (((1,), (1,)), ((), ())), preferred_element_type=F32)


def weight_grad(left, right):
    return lax.dot_general(
        left, right, (((0,), (0,)), ((), ())), preferred_element_type=F32
    ).astype(BF16)


def general(tokens, upstream, expert_ids, gate_rows, up_rows, down_rows):
    experts = lax.axis_size("expert")
    tok_rows, width = tokens.shape
    capacity = max(2, 2 * tok_rows // experts)
    route = expert_ids[:, 0]
    onehot = (route[:, None] == jnp.arange(experts, dtype=jnp.int32)[None, :]).astype(jnp.int32)
    before = jnp.cumsum(onehot, axis=0) - onehot
    target = route * capacity + jnp.sum(before * onehot, axis=1)
    slot = jnp.arange(experts * capacity, dtype=jnp.int32)
    placing = (target[None, :] == slot[:, None]).astype(BF16)
    both = jnp.concatenate([tokens, upstream], axis=1)
    own = to_experts(jnp.dot(placing, both, preferred_element_type=F32).astype(BF16), experts)
    x_all = lax.all_gather(own[:, :width], "tensor", axis=1, tiled=True)
    dy_all = lax.all_gather(own[:, width:], "tensor", axis=1, tiled=True)
    gate_pre = rows_by_weights(x_all, gate_rows)
    up_pre = rows_by_weights(x_all, up_rows)
    d_hidden = rows_by_weights(dy_all, down_rows)
    sig = jax.nn.sigmoid(gate_pre)
    silu = gate_pre * sig
    hidden = (silu * up_pre).astype(BF16)
    d_up = (d_hidden * silu).astype(BF16)
    d_gate = (d_hidden * up_pre * sig * (1.0 + gate_pre * (1.0 - sig))).astype(BF16)
    partial = jnp.dot(d_gate, gate_rows, preferred_element_type=F32) + jnp.dot(
        d_up, up_rows, preferred_element_type=F32
    )
    totals = lax.psum_scatter(partial.astype(BF16), "tensor", scatter_dimension=1, tiled=True)
    returned = to_experts(totals, experts)
    grads = [weight_grad(d_gate, x_all), weight_grad(d_up, x_all), weight_grad(hidden, dy_all)]
    return weight_grad(placing, returned), grads


def on_device(tokens, upstream, expert_ids, w_gate, w_up, w_down):
    experts = lax.axis_size("expert")
    capacity = 2 * tokens.shape[0] // experts
    pairs = lax.axis_size("tensor") == 2 and experts & (experts - 1) == 0 and experts > 4
    run = grouped if pairs and capacity % 16 == 0 else general
    grad_tokens, grads = run(tokens, upstream, expert_ids, w_gate[0], w_up[0], w_down[0])
    return (grad_tokens, *(grad[None] for grad in grads))


def solution(mesh):
    rows = P("expert", "tensor")
    weights = P("expert", "tensor", None)
    return jax.shard_map(
        on_device,
        mesh=mesh,
        in_specs=(rows, rows, P("expert", None), weights, weights, weights),
        out_specs=(rows, weights, weights, weights),
        check_vma=False,
    )
```

```python
import functools

import jax
import jax.numpy as jnp
from jax import lax
from jax.experimental import pallas as pl
from jax.experimental.pallas import tpu as pltpu
from jax.sharding import PartitionSpec as P

F32 = jnp.float32
BF16 = jnp.bfloat16
SMALL = 16 * 2**20
LARGE = 56 * 2**20
PIECES = 4
COLLECT = 16
IN_VMEM = pl.BlockSpec(memory_space=pltpu.VMEM)
IN_HBM = pl.BlockSpec(memory_space=pltpu.HBM)


def rank_among_same(row, axis):
    rows = row.shape[1]
    down = lax.broadcasted_iota(jnp.int32, (rows, rows), 0)
    right = lax.broadcasted_iota(jnp.int32, (rows, rows), 1)
    col = jnp.sum(jnp.where(down == right, row, 0), axis=1, keepdims=True)
    earlier = down > right if axis else down < right
    same = jnp.where((col == row) & earlier, 1, 0)
    return (col if axis else row), jnp.sum(same, axis=axis, keepdims=True)


def place_kernel(capacity, partners, row_hbm, x_hbm, dy_hbm, *refs):
    *slabs, row_ref, x_ref, dy_ref, placed_ref, row_sem, in_sems, out_sems = refs
    row_copy = pltpu.make_async_copy(row_hbm, row_ref, row_sem)
    row_copy.start()
    step = x_ref.shape[0] // PIECES
    copies = [
        [
            pltpu.make_async_copy(
                from_ref.at[i * step : (i + 1) * step],
                to_ref.at[i * step : (i + 1) * step],
                in_sems.at[which, i],
            )
            for i in range(PIECES)
        ]
        for which, (from_ref, to_ref) in enumerate(((x_hbm, x_ref), (dy_hbm, dy_ref)))
    ]
    for copy in copies[0] + copies[1]:
        copy.start()
    me = lax.axis_index("expert")
    row_copy.wait()
    route, within = rank_among_same(row_ref[...], 0)
    within_slab = lax.broadcasted_iota(jnp.int32, (capacity, x_ref.shape[0]), 0)
    slot = jnp.concatenate([within_slab + k * capacity for k in partners], axis=0)
    placing = jnp.where(slot == (route ^ me) * capacity + within, 1.0, 0.0).astype(BF16)
    out_copies = []
    for i, ref in enumerate((x_ref, dy_ref)):
        for copy in copies[i]:
            copy.wait()
        placed_ref[i] = jnp.dot(placing, ref[...], preferred_element_type=F32).astype(BF16)
        for j, slab in enumerate(slabs):
            out_copies.append(
                pltpu.make_async_copy(
                    placed_ref.at[i, j * capacity : (j + 1) * capacity],
                    slab.at[i * capacity : (i + 1) * capacity],
                    out_sems.at[i, j],
                )
            )
            out_copies[-1].start()
    for copy in out_copies:
        copy.wait()


def collect_kernel(capacity, count, *refs):
    slabs, out_ref = refs[:count], refs[-1]
    half = len(slabs) * capacity
    for i, slab in enumerate(slabs):
        out_ref[i * capacity : (i + 1) * capacity, :] = slab[:capacity, :]
        out_ref[half + i * capacity : half + (i + 1) * capacity, :] = slab[capacity:, :]


def side(which, width):
    return pl.ds(pl.multiple_of(which * width, width), width)


def input_rows(d_gate_ref, d_up_ref, gate_ref, up_ref, columns):
    over_hidden = (((0,), (0,)), ((), ()))
    return lax.dot_general(
        d_gate_ref[...], gate_ref[:, columns], over_hidden, preferred_element_type=F32
    ) + lax.dot_general(
        d_up_ref[...], up_ref[:, columns], over_hidden, preferred_element_type=F32
    )


OVER_FEATURES = (((1,), (1,)), ((), ()))


def begin_kernel(tile, own_ref, gate_ref, up_ref, down_ref, *out_refs):
    rows, width = out_refs[0].shape[1], own_ref.shape[1]
    columns = side(lax.axis_index("tensor"), width)

    @pl.loop(0, gate_ref.shape[0] // tile)
    def _(step):
        units = pl.ds(pl.multiple_of(step * tile, tile), tile)
        for weight_ref, out_ref, start in zip(
            (gate_ref, up_ref, down_ref), out_refs, (0, 0, rows)
        ):
            out_ref[units, :] = lax.dot_general(
                weight_ref[units, columns],
                own_ref[start : start + rows, :],
                OVER_FEATURES,
                preferred_element_type=F32,
            )


def front_kernel(tile, own_ref, other_ref, gate_ref, up_ref, down_ref, *refs):
    *begun_refs, hidden_ref, d_gate_ref, d_up_ref, sent_ref = refs
    rows, width = sent_ref.shape
    mine = lax.axis_index("tensor")

    @pl.loop(0, hidden_ref.shape[0] // tile)
    def _(step):
        units = pl.ds(pl.multiple_of(step * tile, tile), tile)

        def product(which, weight_ref, start):
            def share(half_ref, half):
                return lax.dot_general(
                    weight_ref[units, side(half, width)],
                    half_ref[start : start + rows, :],
                    OVER_FEATURES,
                    preferred_element_type=F32,
                )

            own = begun_refs[which][units, :] if begun_refs else share(own_ref, mine)
            return own + share(other_ref, 1 - mine)

        gate_pre = product(0, gate_ref, 0)
        up_pre = product(1, up_ref, 0)
        d_hidden = product(2, down_ref, rows)
        sig = jax.nn.sigmoid(gate_pre)
        silu = gate_pre * sig
        hidden_ref[units, :] = (silu * up_pre).astype(BF16)
        d_up_ref[units, :] = (d_hidden * silu).astype(BF16)
        d_gate_ref[units, :] = (
            d_hidden * up_pre * sig * (1.0 + gate_pre * (1.0 - sig))
        ).astype(BF16)

    sent_ref[...] = input_rows(
        d_gate_ref, d_up_ref, gate_ref, up_ref, side(1 - mine, width)
    ).astype(BF16)


def kept_kernel(d_gate_ref, d_up_ref, gate_ref, up_ref, out_ref):
    columns = side(lax.axis_index("tensor"), out_ref.shape[1])
    out_ref[...] = input_rows(d_gate_ref, d_up_ref, gate_ref, up_ref, columns)


def sum_kernel(kept_ref, got_ref, out_ref):
    out_ref[...] = (kept_ref[...] + got_ref[...].astype(F32)).astype(BF16)


def last_sum_kernel(capacity, groups, sum_ref, kept_ref, got_ref, out_ref, done_ref):
    done_ref[...] = jnp.zeros_like(done_ref)
    me = lax.axis_index("expert")
    for last, group in enumerate(groups):
        for i, k in enumerate(group):
            here = slice(i * capacity, (i + 1) * capacity)
            there = pl.ds(pl.multiple_of((me ^ k) * capacity, capacity), capacity)
            if last:
                both = kept_ref[here, :] + got_ref[here, :].astype(F32)
                out_ref[there, :] = both.astype(BF16)
            else:
                out_ref[there, :] = sum_ref[here, :]


def grads_kernel(sizes, *refs):
    *ins, _, grad_gate_ref, grad_up_ref, grad_down_ref = refs
    mine = lax.axis_index("tensor")
    groups = [(*ins[5 * i : 5 * i + 5], rows) for i, rows in enumerate(sizes)]
    width = groups[0][0].shape[1]

    def total(left, half, second):
        return sum(
            jnp.dot(
                one[left][...],
                one[half][one[5] * second : one[5] * (second + 1), :],
                preferred_element_type=F32,
            )
            for one in groups
        ).astype(BF16)

    for half, which in enumerate((mine, 1 - mine)):
        grad_gate_ref[:, side(which, width)] = total(2, half, 0)
        grad_up_ref[:, side(which, width)] = total(3, half, 0)
        grad_down_ref[:, side(which, width)] = total(4, half, 1)


def placing_kernel(capacity, row_ref, _, placing_ref):
    route, within = rank_among_same(row_ref[...], 1)
    slot = lax.broadcasted_iota(jnp.int32, placing_ref.shape, 1)
    placing_ref[...] = jnp.where(slot == route * capacity + within, 1.0, 0.0).astype(BF16)


def combine_kernel(placing_ref, back_hbm, out_ref, back_ref, sems):
    step = back_ref.shape[0] // PIECES
    copies = [
        pltpu.make_async_copy(
            back_hbm.at[i * step : (i + 1) * step],
            back_ref.at[i * step : (i + 1) * step],
            sems.at[i],
        )
        for i in range(PIECES)
    ]
    for copy in copies:
        copy.start()
    total = jnp.zeros(out_ref.shape, F32)
    for i, copy in enumerate(copies):
        copy.wait()
        total += jnp.dot(
            placing_ref[:, i * step : (i + 1) * step],
            back_ref[i * step : (i + 1) * step],
            preferred_element_type=F32,
        )
    out_ref[...] = total.astype(BF16)


def params(limit):
    return pltpu.CompilerParams(vmem_limit_bytes=limit)


def cost(products, rows, hidden, features):
    return pl.CostEstimate(
        flops=2 * products * rows * hidden * features,
        bytes_accessed=2 * products * (hidden + rows) * features,
        transcendentals=0,
    )


def placing_of(capacity, ids_row, slots, after):
    return pl.pallas_call(
        functools.partial(placing_kernel, capacity),
        out_shape=jax.ShapeDtypeStruct((ids_row.shape[1], slots), BF16),
        in_specs=[IN_VMEM] * 2,
        out_specs=IN_VMEM,
        compiler_params=params(SMALL),
        name="placing",
    )(ids_row, after)


def combine(placing, returned):
    slots, width = returned.shape
    return pl.pallas_call(
        combine_kernel,
        out_shape=jax.ShapeDtypeStruct((placing.shape[0], width), BF16),
        in_specs=[IN_VMEM, IN_HBM],
        out_specs=IN_VMEM,
        scratch_shapes=[pltpu.VMEM((slots, width), BF16), pltpu.SemaphoreType.DMA((PIECES,))],
        compiler_params=params(SMALL),
        name="combine",
    )(placing, returned)


def to_experts(rows, experts):
    return lax.all_to_all(
        rows.reshape(experts, rows.shape[0] // experts, rows.shape[1]),
        "expert",
        split_axis=0,
        concat_axis=0,
        tiled=True,
    ).reshape(rows.shape)


def grouped(tokens, upstream, expert_ids, gate_rows, up_rows, down_rows):
    experts = lax.axis_size("expert")
    tok_rows, width = tokens.shape
    units, features = gate_rows.shape
    capacity = max(2, 2 * tok_rows // experts)
    ids_row = expert_ids.reshape(1, tok_rows)
    tile = units // 2 if units % 32 == 0 else units

    far = [k for k in reversed(range(1, experts)) if k >= experts // 2]
    near = [k for k in reversed(range(1, experts)) if k < experts // 2]
    turns = [k for pair in zip(far, near) for k in pair] + far[len(near) :]
    cut = 3 * experts // 4
    turns = turns[:cut] + sorted(turns[cut:], key=lambda k: k < experts // 2)
    first, second = turns[:cut], turns[cut:] + [0]

    def place(partners):
        return pl.pallas_call(
            functools.partial(place_kernel, capacity, partners),
            out_shape=[jax.ShapeDtypeStruct((2 * capacity, width), BF16)] * len(partners),
            in_specs=[IN_HBM] * 3,
            out_specs=[IN_HBM] * len(partners),
            scratch_shapes=[
                pltpu.VMEM((1, tok_rows), jnp.int32),
                pltpu.VMEM((tok_rows, width), BF16),
                pltpu.VMEM((tok_rows, width), BF16),
                pltpu.VMEM((2, len(partners) * capacity, width), BF16),
                pltpu.SemaphoreType.DMA,
                pltpu.SemaphoreType.DMA((2, PIECES)),
                pltpu.SemaphoreType.DMA((2, len(partners))),
            ],
            compiler_params=params(LARGE),
            name="place",
        )(ids_row, tokens, upstream)

    early = experts // 4 + 1
    slabs = {}
    for partners in (turns[:early], turns[early:] + [0]):
        slabs.update(zip(partners, place(partners)))

    def swap(k):
        return lax.ppermute(slabs[k], "expert", [(e, e ^ k) for e in range(experts)])

    def exchange(values):
        return lax.ppermute(values, "tensor", [(0, 1), (1, 0)])

    def collect(arrived, after):
        return pl.pallas_call(
            functools.partial(collect_kernel, capacity, len(arrived)),
            out_shape=jax.ShapeDtypeStruct((2 * len(arrived) * capacity, width), BF16),
            in_specs=[IN_VMEM] * (len(arrived) + len(after)),
            out_specs=IN_VMEM,
            compiler_params=params(SMALL),
            cost_estimate=cost(COLLECT, len(arrived) * capacity, units, features),
            name="collect",
        )(*arrived, *after)

    def begin(own):
        rows = own.shape[0] // 2
        return pl.pallas_call(
            functools.partial(begin_kernel, units),
            out_shape=[jax.ShapeDtypeStruct((units, rows), F32)] * 3,
            in_specs=[IN_VMEM] * 4,
            out_specs=[IN_VMEM] * 3,
            compiler_params=params(SMALL),
            cost_estimate=cost(2, rows, units, features),
            name="begin",
        )(own, gate_rows, up_rows, down_rows)

    def front(own, begun):
        other = exchange(own)
        rows = own.shape[0] // 2
        hidden, d_gate, d_up, sent = pl.pallas_call(
            functools.partial(front_kernel, units),
            out_shape=[jax.ShapeDtypeStruct((units, rows), BF16)] * 3
            + [jax.ShapeDtypeStruct((rows, width), BF16)],
            in_specs=[IN_VMEM] * (5 + len(begun)),
            out_specs=[IN_VMEM] * 4,
            compiler_params=params(SMALL),
            cost_estimate=cost(4, rows, units, features),
            name="front",
        )(own, other, gate_rows, up_rows, down_rows, *begun)
        kept = pl.pallas_call(
            kept_kernel,
            out_shape=jax.ShapeDtypeStruct((rows, width), F32),
            in_specs=[IN_VMEM] * 4,
            out_specs=IN_VMEM,
            compiler_params=params(SMALL),
            cost_estimate=cost(1, rows, units, features),
            name="kept",
        )(d_gate, d_up, gate_rows, up_rows)
        return (own, other, d_gate, d_up, hidden), (kept, exchange(sent))

    got = {k: swap(k) for k in turns}
    got[0] = slabs[0]
    for_grads_a, for_sum_a = front(collect([got[k] for k in first], []), [])
    own_b = collect([got[k] for k in second], for_sum_a[:1])
    for_grads_b, for_sum_b = front(own_b, begin(own_b))
    sum_a = pl.pallas_call(
        sum_kernel,
        out_shape=jax.ShapeDtypeStruct((len(first) * capacity, width), BF16),
        in_specs=[IN_VMEM] * 2,
        out_specs=IN_VMEM,
        compiler_params=params(SMALL),
        name="sum",
    )(*for_sum_a)
    totals, done = pl.pallas_call(
        functools.partial(last_sum_kernel, capacity, (first, second)),
        out_shape=[
            jax.ShapeDtypeStruct((experts * capacity, width), BF16),
            jax.ShapeDtypeStruct((8, 128), F32),
        ],
        in_specs=[IN_VMEM] * 3,
        out_specs=[IN_VMEM] * 2,
        compiler_params=params(SMALL),
        name="last_sum",
    )(sum_a, *for_sum_b)
    returned = to_experts(totals, experts)
    placing = placing_of(capacity, ids_row, experts * capacity, done)

    def grads_specs(rows):
        return [pl.BlockSpec((2 * rows, width), lambda i: (0, 0))] * 2 + [
            pl.BlockSpec((tile, rows), lambda i: (i, 0))
        ] * 3

    sizes = [len(group) * capacity for group in (first, second)]
    grads = pl.pallas_call(
        functools.partial(grads_kernel, sizes),
        grid=(units // tile,),
        out_shape=[jax.ShapeDtypeStruct((units, features), BF16)] * 3,
        in_specs=grads_specs(sizes[0])
        + grads_specs(sizes[1])
        + [pl.BlockSpec(placing.shape, lambda i: (0, 0))],
        out_specs=[pl.BlockSpec((tile, features), lambda i: (i, 0))] * 3,
        compiler_params=params(2 * SMALL),
        cost_estimate=cost(3, sum(sizes), units, features),
        name="grads",
    )(*for_grads_a, *for_grads_b, placing)
    return combine(placing, returned), grads


def rows_by_weights(rows, weights):
    return lax.dot_general(rows, weights, (((1,), (1,)), ((), ())), preferred_element_type=F32)


def weight_grad(left, right):
    return lax.dot_general(
        left, right, (((0,), (0,)), ((), ())), preferred_element_type=F32
    ).astype(BF16)


def general(tokens, upstream, expert_ids, gate_rows, up_rows, down_rows):
    experts = lax.axis_size("expert")
    tok_rows, width = tokens.shape
    capacity = max(2, 2 * tok_rows // experts)
    route = expert_ids[:, 0]
    onehot = (route[:, None] == jnp.arange(experts, dtype=jnp.int32)[None, :]).astype(jnp.int32)
    before = jnp.cumsum(onehot, axis=0) - onehot
    target = route * capacity + jnp.sum(before * onehot, axis=1)
    slot = jnp.arange(experts * capacity, dtype=jnp.int32)
    placing = (target[None, :] == slot[:, None]).astype(BF16)
    both = jnp.concatenate([tokens, upstream], axis=1)
    own = to_experts(jnp.dot(placing, both, preferred_element_type=F32).astype(BF16), experts)
    x_all = lax.all_gather(own[:, :width], "tensor", axis=1, tiled=True)
    dy_all = lax.all_gather(own[:, width:], "tensor", axis=1, tiled=True)
    gate_pre = rows_by_weights(x_all, gate_rows)
    up_pre = rows_by_weights(x_all, up_rows)
    d_hidden = rows_by_weights(dy_all, down_rows)
    sig = jax.nn.sigmoid(gate_pre)
    silu = gate_pre * sig
    hidden = (silu * up_pre).astype(BF16)
    d_up = (d_hidden * silu).astype(BF16)
    d_gate = (d_hidden * up_pre * sig * (1.0 + gate_pre * (1.0 - sig))).astype(BF16)
    partial = jnp.dot(d_gate, gate_rows, preferred_element_type=F32) + jnp.dot(
        d_up, up_rows, preferred_element_type=F32
    )
    totals = lax.psum_scatter(partial.astype(BF16), "tensor", scatter_dimension=1, tiled=True)
    returned = to_experts(totals, experts)
    grads = [weight_grad(d_gate, x_all), weight_grad(d_up, x_all), weight_grad(hidden, dy_all)]
    return weight_grad(placing, returned), grads


def on_device(tokens, upstream, expert_ids, w_gate, w_up, w_down):
    experts = lax.axis_size("expert")
    capacity = 2 * tokens.shape[0] // experts
    pairs = lax.axis_size("tensor") == 2 and experts & (experts - 1) == 0 and experts > 4
    run = grouped if pairs and capacity % 16 == 0 else general
    grad_tokens, grads = run(tokens, upstream, expert_ids, w_gate[0], w_up[0], w_down[0])
    return (grad_tokens, *(grad[None] for grad in grads))


def solution(mesh):
    rows = P("expert", "tensor")
    weights = P("expert", "tensor", None)
    return jax.shard_map(
        on_device,
        mesh=mesh,
        in_specs=(rows, rows, P("expert", None), weights, weights, weights),
        out_specs=(rows, weights, weights, weights),
        check_vma=False,
    )
```
